32 devices in a mesh: dp: 8 (over z, y), sp: 4 (over x, core).
Axes of the slice: x: 2, y: 2, z: 4, core: 2. Of those that a mesh axis runs over, the one named last changes fastest.
Arguments:
- tokens: bfloat16 [16384, 1024], P(('dp', 'sp')), may hold values from -6 to 6
- seq_spans: int32 [8, 4], P('dp'), may hold values from 64 to 2048, as said below
- valid_mask: int32 [16384], P(('dp', 'sp')), may hold values from 0 to 1, as said below
- cotangent: bfloat16 [16384, 1024], P(('dp', 'sp')), may hold values from -12 to 12
- w_qkv: bfloat16 [1024, 3072], P('dp', 'sp'), may hold values from -0.1875 to 0.1875
- w_out: bfloat16 [1024, 1024], P('dp', 'sp'), may hold values from -1.5 to 1.5
- w_up: bfloat16 [1024, 4096], P('dp', 'sp'), may hold values from -0.1875 to 0.1875
- w_down: bfloat16 [1024, 4096], P('dp', 'sp'), may hold values from -0.09375 to 0.09375
- model_gains: float32 [3, 1024], replicated, may hold values from 0.5 to 1.5
- model_shifts: float32 [7, 1024], replicated, may hold values from -1.8 to 1.8
- mid_gain: float32 [4096], replicated, may hold values from 0.5 to 1.5
- hidden_shifts: float32 [2, 4096], replicated, may hold values from -3 to 3
- head_scale: float32 [16], replicated, may hold values from 0.5 to 2
Outputs:
- layer_out: bfloat16 [16384, 1024], P(('dp', 'sp'))
- grad_tokens: float32 [16384, 1024], P(('dp', 'sp'))
- grad_w_qkv: float32 [1024, 3072], P('dp', 'sp')
- grad_w_out: float32 [1024, 1024], P('dp', 'sp')
- grad_w_up: float32 [1024, 4096], P('dp', 'sp')
- grad_w_down: float32 [1024, 4096], P('dp', 'sp')
- grad_model_gains: float32 [3, 1024], replicated
- grad_model_shifts: float32 [7, 1024], replicated
- grad_mid_gain: float32 [4096], replicated
- grad_hidden_shifts: float32 [2, 4096], replicated
- grad_head_scale: float32 [16], replicated
The draws below stay inside these ranges and needn't reach their ends.
Inputs may be any that keep to these rules, and one draw needn't show every extreme that they name: `seq_spans`: each row holds the token counts of the 4 consecutive slots of one group and sums to 2048; in every row one slot starts within the first 512 tokens of the group and ends within the last 512. `valid_mask`: within each slot the ones form a leading run of one token or more, and the rest of the slot is 0.
All inputs are finite; a program needn't handle non-finite values.
Results may differ from the reference program's by a relative error of at most 0.018.
Values may be sent and summed in bfloat16 or wider, within the bound.
No kernel may reach another device: no remote copies, remote signals or barrier semaphores. Data moves between devices by JAX's collectives and lax.ppermute only.
A program may use at most 192 MiB of HBM per device.

```python
import math
import jax
import jax.numpy as jnp
from jax import lax

D = 1024
FF = 4096
HEADS = 16
SEQS = 4
GROUP = 2048
ROWS = 512
TOKENS = 16384
N_DP = 8


def pack_layout(key):
    long_key, short_key, tail_key, trim_key = jax.random.split(key, 4)
    long_slot = jax.random.randint(long_key, (N_DP, 1), 0, SEQS)
    slots = lax.broadcasted_iota(jnp.int32, (N_DP, SEQS), 1)
    is_long = slots == long_slot
    shorts = jax.random.randint(short_key, (N_DP, SEQS), ROWS // 8, ROWS // 4)
    short_total = jnp.sum(jnp.where(is_long, 0, shorts), axis=1, keepdims=True)
    spans = jnp.where(is_long, GROUP - short_total, shorts)
    long_tail = jax.random.randint(tail_key, (N_DP, SEQS), 0, ROWS // 8)
    short_tail = jax.random.randint(trim_key, (N_DP, SEQS), 0, shorts // 2 + 1)
    lengths = spans - jnp.where(is_long, long_tail, short_tail)
    return (spans.astype(jnp.int32), lengths.astype(jnp.int32))


def draw_seq_spans(key, part):
    spans, lengths = pack_layout(key)
    return spans


def draw_valid_mask(key, part):
    spans, lengths = pack_layout(key)
    span_ends = jnp.cumsum(spans, axis=1).astype(jnp.int32)
    starts = span_ends - spans
    places = lax.broadcasted_iota(jnp.int32, (N_DP, GROUP, SEQS), 1)
    inside = (places >= starts[:, None, :]) & (places < starts[:, None, :] + lengths[:, None, :])
    return jnp.any(inside, axis=2).astype(jnp.int32).reshape(N_DP * GROUP)


def strengthened(values, own_key, source, target, shards_of, factor):
    owner, partner = [(jnp.arange(values.shape[position]) // (values.shape[position] // shards_of)).reshape([-1 if axis == position else 1 for axis in range(values.ndim)]) for position in (source, target)]
    chosen = jax.random.permutation(own_key, shards_of)[partner]
    strong = (owner == chosen) | (owner == (partner + shards_of // 2) % shards_of)
    return jnp.where(strong, factor * values, values)


def levels(rng, dims, cuts, smallest, largest):
    level = 1.0
    for position, shards_of in cuts:
        steps = jax.random.uniform(jax.random.fold_in(jax.random.fold_in(rng, 6), position), (shards_of,), jnp.float32, smallest / len(cuts), largest / len(cuts))
        level = level * jnp.repeat(jnp.exp(steps), dims[position] // shards_of).reshape((-1,) + (1,) * (len(dims) - 1 - position))
    return level


def noise(own_key, dims, width, bound, pieces=(), held_as=jnp.bfloat16):
    gain = levels(own_key, dims, pieces, -0.22, 0.18) if pieces else 1.0
    drawn = jax.random.normal(own_key, dims, jnp.float32) * width * gain
    return jnp.minimum(jnp.maximum(drawn, -bound), bound).astype(held_as)


def heavy_noise(own_key, dims, width, bound, cuts, heavy, kind=jnp.bfloat16):
    array = width * jax.random.normal(own_key, dims, jnp.float32)
    if cuts:
        array = array * levels(own_key, dims, cuts, -0.22, 0.18)
    return jnp.clip(strengthened(array, jax.random.fold_in(own_key, 3), *heavy), -bound, bound).astype(kind)


def setup_inputs(seed: int = 0) -> dict:
    splits = jax.random.split(jax.random.key(seed), 14)
    tokens = noise(splits[0], (TOKENS, D), 1.0, 6.0, ((0, 32),))
    seq_spans = draw_seq_spans(jax.random.fold_in(splits[13], 71), 0)
    valid_mask = draw_valid_mask(jax.random.fold_in(splits[13], 71), 0)
    cotangent = heavy_noise(splits[3], (TOKENS, D), 1.0, 12.0, ((0, 32),), (0, 1, 32, 2.75))
    w_qkv = noise(splits[4], (D, 3 * D), D ** -0.5, 0.1875, ((0, 8), (1, 4)))
    w_out = noise(splits[5], (D, D), (D // 64) ** -0.5, 1.5, ((0, 8), (1, 4)))
    w_up = noise(splits[6], (D, FF), D ** -0.5, 0.1875, ((0, 8), (1, 4)))
    w_down = noise(splits[7], (D, FF), FF ** -0.5, 0.09375, ((0, 8), (1, 4)))
    model_gains = jnp.clip(1.0 + 0.1 * jax.random.normal(splits[8], (3, D), jnp.float32), 0.5, 1.5)
    model_shifts = noise(splits[9], (7, D), 0.3, 1.8, (), jnp.float32)
    mid_gain = jnp.clip(1.0 + 0.1 * jax.random.normal(splits[10], (FF,), jnp.float32), 0.5, 1.5)
    hidden_shifts = noise(splits[11], (2, FF), 0.5, 3.0, (), jnp.float32)
    head_scale = jnp.clip(jnp.exp(jax.random.uniform(splits[12], (HEADS,), jnp.float32, math.log(0.5), math.log(2.0))), 0.5, 2.0)
    return dict(tokens=tokens, seq_spans=seq_spans, valid_mask=valid_mask, cotangent=cotangent, w_qkv=w_qkv, w_out=w_out, w_up=w_up, w_down=w_down, model_gains=model_gains, model_shifts=model_shifts, mid_gain=mid_gain, hidden_shifts=hidden_shifts, head_scale=head_scale)


EPSILON = 1e-05
MASKED = -1e+30
HIGHEST = lax.Precision.HIGHEST

@jax.custom_vjp
def low(v):
    return lax.optimization_barrier(v.astype(jnp.bfloat16)).astype(jnp.float32)

@jax.custom_vjp
def low_back(v):
    return v

def low_keep(v):
    return (low(v), None)

def low_pass(kept, grad):
    return (grad,)

def back_keep(v):
    return (v, None)

def back_low(kept, grad):
    return (low(grad),)
low.defvjp(low_keep, low_pass)
low_back.defvjp(back_keep, back_low)

def layer_norm(inputs, gain_row, shift_row):
    row_mean = lax.optimization_barrier(jnp.mean(inputs, axis=-1, keepdims=True))
    centred = inputs - row_mean
    variance = lax.optimization_barrier(jnp.mean(centred * centred, axis=-1, keepdims=True))
    return centred * lax.rsqrt(variance + EPSILON) * gain_row + shift_row

def head_attention(queries, key_rows, value_rows, visible, factor):
    scores = low_back(jnp.dot(queries, key_rows.T, precision=HIGHEST) * factor)
    scores = jnp.where(visible, scores, MASKED)
    row_peak = lax.optimization_barrier(jnp.max(scores, axis=-1, keepdims=True))
    exponent = jnp.exp(scores - row_peak)
    weights = exponent / lax.optimization_barrier(jnp.sum(exponent, axis=-1, keepdims=True))
    return jnp.dot(low(weights), value_rows, precision=HIGHEST)

def group_forward(stream, params, span_row, valid_row):
    w_qkv, w_out, w_up, w_down, model_gains, model_shifts, mid_gain, hidden_shifts, head_scale = params
    group_rows, model_width = stream.shape
    head_count = head_scale.shape[0]
    head_width = model_width // head_count
    factor = head_width ** (-0.5)
    positions = jnp.arange(group_rows, dtype=jnp.int32)
    span_ends = jnp.cumsum(span_row).astype(jnp.int32)
    segment = lax.optimization_barrier(jnp.sum((positions[:, None] >= span_ends[None, :]).astype(jnp.int32), axis=1))
    visible = (segment[:, None] == segment[None, :]) & (positions[None, :] <= positions[:, None]) & (valid_row[None, :] > 0)
    first_norm = low(layer_norm(stream, model_gains[0], model_shifts[3]))
    qkv_shift = jnp.concatenate([model_shifts[0], jnp.zeros_like(model_shifts[0]), model_shifts[1]])
    projected = low(low_back(jnp.dot(first_norm, w_qkv, precision=HIGHEST) + qkv_shift))
    per_head = projected.reshape(group_rows, 3, head_count, head_width).transpose(1, 2, 0, 3)
    attend = jax.checkpoint(lambda queries, key_rows, value_rows: head_attention(queries, key_rows, value_rows, visible, factor))
    attended = lax.map(lambda triple: attend(triple[0], triple[1], triple[2]), (per_head[0], per_head[1], per_head[2]))
    attended = low_back(attended)
    scaled = low(low_back(attended * head_scale[:, None, None]))
    merged = scaled.transpose(1, 0, 2).reshape(group_rows, model_width)
    attn_pre = low_back(jnp.dot(merged, w_out, precision=HIGHEST) + model_shifts[2])
    middle = stream + layer_norm(attn_pre, model_gains[1], model_shifts[4])
    second_norm = low(layer_norm(middle, model_gains[2], model_shifts[5]))
    hidden_pre = low_back(jnp.dot(second_norm, w_up, precision=HIGHEST) + hidden_shifts[0])
    hidden = low(layer_norm(jax.nn.gelu(hidden_pre), mid_gain, hidden_shifts[1]))
    return middle + jnp.dot(hidden, w_down.T, precision=HIGHEST) + model_shifts[6]

def reference(tokens, seq_spans, valid_mask, cotangent, w_qkv, w_out, w_up, w_down, model_gains, model_shifts, mid_gain, hidden_shifts, head_scale):
    params = tuple((item.astype(jnp.float32) for item in (w_qkv, w_out, w_up, w_down, model_gains, model_shifts, mid_gain, hidden_shifts, head_scale)))
    group_count = seq_spans.shape[0]
    model_width = tokens.shape[1]
    stream_all = tokens.astype(jnp.float32).reshape(group_count, -1, model_width)
    upstream_all = (cotangent.astype(jnp.float32) * valid_mask.astype(jnp.float32)[:, None]).reshape(group_count, -1, model_width)
    valid_all = valid_mask.reshape(group_count, -1)

    def one_group(running, item):
        stream, upstream, span_row, valid_row = item
        result, pull = jax.vjp(lambda inputs, weights: group_forward(inputs, weights, span_row, valid_row), stream, params)
        input_grad, param_grads = pull(upstream)
        running = jax.tree.map(jnp.add, running, param_grads)
        return (running, (result.astype(jnp.bfloat16), input_grad))
    empty_sum = jax.tree.map(jnp.zeros_like, params)
    totals, (outputs, input_grads) = lax.scan(one_group, empty_sum, (stream_all, upstream_all, seq_spans, valid_all))
    return (outputs.reshape(-1, model_width), input_grads.reshape(-1, model_width), totals[0], totals[1], totals[2], totals[3], totals[4], totals[5], totals[6], totals[7], totals[8])
```

```python
import functools

import jax
import jax.numpy as jnp
import numpy as np
from jax import lax
from jax.experimental import pallas as pl
from jax.experimental.pallas import tpu as pltpu
from jax.sharding import PartitionSpec as P

EPSILON = 1e-05
MASKED = -1e30
HEAD = 64
BQ = 256
bf16 = jnp.bfloat16
f32 = jnp.float32


def mm(a, b):
    return lax.dot_general(a, b, (((1,), (0,)), ((), ())), preferred_element_type=f32)


def mm_rows(a, b):
    return lax.dot_general(a, b, (((0,), (0,)), ((), ())), preferred_element_type=f32)


def mm_cols(a, b):
    return lax.dot_general(a, b, (((1,), (1,)), ((), ())), preferred_element_type=f32)


def skipping(kernel, at, count):
    return lambda *refs: kernel(*refs[:at], *refs[at + count :])


def unread(deps):
    return [pl.BlockSpec(memory_space=pl.ANY)] * len(deps)


def lanes_of(x, h):
    lane = lax.broadcasted_iota(jnp.int32, x.shape, 1) // HEAD
    return jnp.where(lane == h, x, jnp.zeros_like(x))


def segment_of(spans, places):
    count, end = jnp.zeros_like(places), jnp.int32(0)
    for k in range(spans.shape[0]):
        end = end + spans[k]
        count = count + (places >= end).astype(jnp.int32)
    return count


class Heads:
    def __init__(self, nh, local, first, blocks, order_at, who_at, parts):
        self.nh, self.local, self.first, self.blocks = nh, local, first, blocks
        self.order_at, self.who_at, self.parts = order_at, who_at, parts


def keys_of(hd, tab, spans, keep_ref, kseg, bk):
    for j in range(hd.parts):
        at = pl.ds(pl.multiple_of(tab[hd.order_at + j] * bk, bk), bk)
        places = j * bk + lax.broadcasted_iota(jnp.int32, (bk, 1), 0)
        kseg[at, :] = jnp.where(keep_ref[at, :] > 0.5, segment_of(spans, places), -1)


def visible(i, j, bk, spans, kseg, at):
    kpos = j * bk + lax.broadcasted_iota(jnp.int32, (bk, BQ), 0)
    qpos = i * BQ + lax.broadcasted_iota(jnp.int32, (bk, BQ), 1)
    qseg = segment_of(spans, i * BQ + lax.broadcasted_iota(jnp.int32, (1, BQ), 1))
    return (kseg[at, :] == qseg) & (kpos <= qpos)


def each_block(hd, tab, spans, i, bk, body):
    first = segment_of(spans, i * BQ)

    def step(j, carry):
        at = pl.ds(pl.multiple_of(tab[hd.order_at + j] * bk, bk), bk)
        pl.when(first <= segment_of(spans, (j + 1) * bk - 1))(lambda: body(j, at))
        return carry

    lax.fori_loop(0, (i * BQ) // bk + 1, step, 0)


def fwd_kernel(hd, bk, tab, spans, q_ref, k_ref, v_ref, keep_ref, hs_ref, scaled_ref, o_ref, lse_ref,
               kseg, vms, sscr, mpart, lpart, acc):
    nh = hd.nh
    i = pl.program_id(0)

    @pl.when(i == 0)
    def _():
        for h in range(nh):
            vms[h] = lanes_of(v_ref[...], h)
        keys_of(hd, tab, spans, keep_ref, kseg, bk)

    qs = q_ref[...] * bf16(0.125)
    qm = [lanes_of(qs, h) for h in range(nh)]
    mpart[...] = jnp.full_like(mpart, MASKED)
    lpart[...] = jnp.zeros_like(lpart)
    acc[...] = jnp.zeros_like(acc)

    def one(j, at):
        kb = k_ref[at, :]
        mask = visible(i, j, bk, spans, kseg, at)
        for h in range(nh):
            s = jnp.where(mask, mm_cols(kb, qm[h]), MASKED)
            sscr[h, at, :] = s
            mpart[h] = jnp.maximum(mpart[h], jnp.max(s.reshape(bk // 8, 8, BQ), axis=0))

    each_block(hd, tab, spans, i, bk, one)
    ms = [jnp.max(mpart[h], axis=0, keepdims=True) for h in range(nh)]

    def two(j, at):
        pts = []
        for h in range(nh):
            p = jnp.exp(sscr[h, at, :] - ms[h])
            lpart[h] += jnp.sum(p.reshape(bk // 8, 8, BQ), axis=0)
            pts.append(p.astype(bf16).T)
        acc[...] += mm(
            jnp.concatenate(pts, axis=1),
            jnp.concatenate([vms[h, at, :] for h in range(nh)], axis=0),
        )

    each_block(hd, tab, spans, i, bk, two)
    out_t = acc[...].T
    parts = []
    for h in range(nh):
        rows = slice(h * HEAD, (h + 1) * HEAD)
        total = jnp.sum(lpart[h], axis=0, keepdims=True)
        result = out_t[rows, :] * (1.0 / total)
        o_ref[rows, :] = result
        parts.append(result * hs_ref[0, tab[hd.who_at] * hd.local + hd.first + h])
        lse_ref[h : h + 1, :] = ms[h] + jnp.log(total)
    scaled_ref[...] = jnp.concatenate(parts, axis=0).T.astype(bf16)


def head_specs(hd, n, w, bk):
    q, k, v = hd.blocks
    ratio = bk // BQ
    return [
        pl.BlockSpec((BQ, w), lambda i, t, s: (t[hd.order_at + (i * BQ) // bk] * ratio + i % ratio, q)),
        pl.BlockSpec((n, w), lambda i, t, s: (0, k)),
        pl.BlockSpec((n, w), lambda i, t, s: (0, v)),
    ]


def attend_forward(hd, tab, spans, qkv, keep, head_scale, deps=()):
    n, nh, w = qkv.shape[0], hd.nh, hd.nh * HEAD
    bk = n // hd.parts
    return pl.pallas_call(
        skipping(functools.partial(fwd_kernel, hd, bk), 7, len(deps)),
        grid_spec=pltpu.PrefetchScalarGridSpec(
            num_scalar_prefetch=2,
            grid=(n // BQ,),
            in_specs=head_specs(hd, n, w, bk)
            + [pl.BlockSpec((n, 1), lambda i, t, s: (0, 0)), pl.BlockSpec(memory_space=pltpu.SMEM)]
            + unread(deps),
            out_specs=[
                pl.BlockSpec((BQ, w), lambda i, t, s: (i, 0)),
                pl.BlockSpec((w, BQ), lambda i, t, s: (0, i)),
                pl.BlockSpec((8, BQ), lambda i, t, s: (0, i)),
            ],
            scratch_shapes=[
                pltpu.VMEM((n, 1), jnp.int32),
                pltpu.VMEM((nh, n, w), bf16),
                pltpu.VMEM((nh, n, BQ), f32),
                pltpu.VMEM((nh, 8, BQ), f32),
                pltpu.VMEM((nh, 8, BQ), f32),
                pltpu.VMEM((BQ, w), f32),
            ],
        ),
        out_shape=[
            jax.ShapeDtypeStruct((n, w), bf16),
            jax.ShapeDtypeStruct((w, n), f32),
            jax.ShapeDtypeStruct((8, n), f32),
        ],
        compiler_params=pltpu.CompilerParams(vmem_limit_bytes=48 << 20),
        cost_estimate=pl.CostEstimate(
            flops=nh * n * n * HEAD * 26, bytes_accessed=n * w * 12, transcendentals=nh * n * n // 2
        ),
        name="attend_forward",
    )(tab, spans, qkv, qkv, qkv, keep, head_scale[None], *deps)


def bwd_kernel(hd, bk, tab, spans, q_ref, k_ref, v_ref, keep_ref, hs_ref, sg_ref, o_ref, lse_ref,
               grad_ref, sums_ref, kseg, dk, dv, dq, gacc, kms):
    nh = hd.nh
    i = pl.program_id(0)
    n, w = k_ref.shape[0], nh * HEAD

    @pl.when(i == 0)
    def _():
        dk[...] = jnp.zeros_like(dk)
        dv[...] = jnp.zeros_like(dv)
        gacc[...] = jnp.zeros_like(gacc)
        for h in range(nh):
            kms[h] = lanes_of(k_ref[...], h)
        keys_of(hd, tab, spans, keep_ref, kseg, bk)

    qs = q_ref[...] * bf16(0.125)
    qm = [lanes_of(qs, h) for h in range(nh)]
    scales = [hs_ref[0, tab[hd.who_at] * hd.local + hd.first + h] for h in range(nh)]
    sg = sg_ref[...].astype(f32)
    lane = lax.broadcasted_iota(jnp.int32, (1, w), 1) // HEAD
    scale_row = jnp.zeros((1, w), f32)
    for h in range(nh):
        scale_row = jnp.where(lane == h, scales[h], scale_row)
    grads = (sg * scale_row).astype(bf16)
    dom = [lanes_of(grads, h) for h in range(nh)]
    o = o_ref[...]
    gacc[...] += sg.T * o
    weighed = grads.astype(f32).T * o
    delta = [jnp.sum(weighed[h * HEAD : (h + 1) * HEAD, :], axis=0, keepdims=True) for h in range(nh)]
    lse = [lse_ref[h : h + 1, :] for h in range(nh)]
    qcat = jnp.concatenate(qm, axis=0)
    docat = jnp.concatenate(dom, axis=0)
    dq[...] = jnp.zeros_like(dq)

    def block(j, at):
        kb = k_ref[at, :]
        vb = v_ref[at, :]
        mask = visible(i, j, bk, spans, kseg, at)
        ps, dss, dsts = [], [], []
        for h in range(nh):
            p = jnp.where(mask, jnp.exp(mm_cols(kb, qm[h]) - lse[h]), 0.0)
            ds = (p * (mm_cols(vb, dom[h]) - delta[h])).astype(bf16)
            ps.append(p.astype(bf16))
            dsts.append(ds.T)
            dss.append(ds)
        dv[at, :] += mm(jnp.concatenate(ps, axis=1), docat)
        dk[at, :] += mm(jnp.concatenate(dss, axis=1), qcat)
        dq[...] += mm(
            jnp.concatenate(dsts, axis=1),
            jnp.concatenate([kms[h, at, :] for h in range(nh)], axis=0),
        )

    each_block(hd, tab, spans, i, bk, block)
    mine = tab[hd.order_at + (i * BQ) // bk] * bk + (i * BQ) % bk
    grad_ref[pl.ds(pl.multiple_of(mine, BQ), BQ), 0:w] = (dq[...] * 0.125).astype(bf16)

    @pl.when(i == n // BQ - 1)
    def _():
        grad_ref[:, w : 2 * w] = dk[...].astype(bf16)
        grad_ref[:, 2 * w : 3 * w] = dv[...].astype(bf16)
        place = lax.broadcasted_iota(jnp.int32, (1, 3 * w), 1)
        gains = jnp.zeros((1, 3 * w), f32)
        for h in range(nh):
            gains = jnp.where(place == h, jnp.sum(gacc[h * HEAD : (h + 1) * HEAD, :]), gains)
        sums_ref[...] = jnp.zeros_like(sums_ref)
        sums_ref[0:1, :] = jnp.sum(grad_ref[...].astype(f32), axis=0, keepdims=True)
        sums_ref[1:2, :] = gains


def attend_backward(hd, tab, spans, qkv, keep, head_scale, scaled_grad, o_t, lse, deps=()):
    n, nh, w = qkv.shape[0], hd.nh, hd.nh * HEAD
    bk = n // hd.parts
    return pl.pallas_call(
        skipping(functools.partial(bwd_kernel, hd, bk), 10, len(deps)),
        grid_spec=pltpu.PrefetchScalarGridSpec(
            num_scalar_prefetch=2,
            grid=(n // BQ,),
            in_specs=head_specs(hd, n, w, bk)
            + [
                pl.BlockSpec((n, 1), lambda i, t, s: (0, 0)),
                pl.BlockSpec(memory_space=pltpu.SMEM),
                pl.BlockSpec((BQ, w), lambda i, t, s: (i, 0)),
                pl.BlockSpec((w, BQ), lambda i, t, s: (0, i)),
                pl.BlockSpec((8, BQ), lambda i, t, s: (0, i)),
            ]
            + unread(deps),
            out_specs=[
                pl.BlockSpec((n, 3 * w), lambda i, t, s: (0, 0)),
                pl.BlockSpec((8, 3 * w), lambda i, t, s: (0, 0)),
            ],
            scratch_shapes=[
                pltpu.VMEM((n, 1), jnp.int32),
                pltpu.VMEM((n, w), f32),
                pltpu.VMEM((n, w), f32),
                pltpu.VMEM((BQ, w), f32),
                pltpu.VMEM((w, BQ), f32),
                pltpu.VMEM((nh, n, w), bf16),
            ],
        ),
        out_shape=[
            jax.ShapeDtypeStruct((n, 3 * w), bf16),
            jax.ShapeDtypeStruct((8, 3 * w), f32),
        ],
        compiler_params=pltpu.CompilerParams(vmem_limit_bytes=52 << 20),
        cost_estimate=pl.CostEstimate(
            flops=nh * n * n * HEAD * 42, bytes_accessed=n * w * 20, transcendentals=nh * n * n // 2
        ),
        name="attend_backward",
    )(tab, spans, qkv, qkv, qkv, keep, head_scale[None], scaled_grad, o_t, lse, *deps)


def swap(x, axis, bits):
    return lax.ppermute(x, axis, [(i, i ^ bits) for i in range(lax.axis_size(axis))])


def reorder(x, idx, width):
    rows, cols = x.shape
    return jnp.take(x.reshape(rows, cols // width, width), idx, axis=1).reshape(rows, cols)


def reorder_rows(x, idx, height):
    rows, cols = x.shape
    return jnp.take(x.reshape(rows // height, height, cols), idx, axis=0).reshape(rows, cols)


class Grid:
    def __init__(self, dp, sp):
        self.dp, self.sp = dp, sp
        self.nx = max(sp // 2, 1)
        self.ny = self.nx if dp % self.nx == 0 else 1
        self.nz = dp // self.ny
        self.z_bits = [self.ny * k for k in range(1, self.nz)]
        self.y_bits = list(range(1, self.ny))
        self.x_bits = [2 * k for k in range(1, self.nx)]

    def gather_z(self, w):
        return jnp.concatenate([w] + [swap(w, "dp", b) for b in self.z_bits], axis=0)

    def gather_y(self, w):
        return jnp.concatenate([w] + [swap(w, "dp", b) for b in self.y_bits], axis=0)

    def gather(self, w):
        half = w.shape[1] // 2
        rows = self.gather_z(w)
        first, other = rows[:, :half], rows[:, half:]
        first = self.gather_y(first)
        firsts = [first] + [swap(first, "sp", b) for b in self.x_bits]
        other = jnp.concatenate([other] + [swap(other, "sp", b) for b in self.x_bits], axis=1)
        other = self.gather_y(other)
        parts = []
        for k in range(self.nx):
            parts += [firsts[k], other[:, k * half : (k + 1) * half]]
        return jnp.concatenate(parts, axis=1)

    def fold(self, parts, axis, bits):
        total = parts[0].astype(f32)
        for part, b in zip(parts[1:], bits, strict=True):
            total = total + swap(part.astype(bf16), axis, b).astype(f32)
        return total

    def scatter_y(self, g):
        rows = g.shape[0] // self.ny
        return self.fold([g[k * rows : (k + 1) * rows] for k in range(self.ny)], "dp", self.y_bits)

    def scatter_z(self, g):
        rows = g.shape[0] // self.nz
        return self.fold([g[k * rows : (k + 1) * rows] for k in range(self.nz)], "dp", self.z_bits)

    def scatter_x(self, g):
        cols = g.shape[1] // self.nx
        return self.fold([g[:, k * cols : (k + 1) * cols] for k in range(self.nx)], "sp", self.x_bits)

    def scatter(self, g):
        cols = g.shape[1] // self.nx
        half = cols // 2
        first = jnp.concatenate([g[:, k * cols : k * cols + half] for k in range(self.nx)], axis=1)
        other = jnp.concatenate([g[:, k * cols + half : (k + 1) * cols] for k in range(self.nx)], axis=1)
        first = self.scatter_y(self.scatter_x(first))
        other = self.scatter_x(self.scatter_y(other))
        return self.scatter_z(jnp.concatenate([first, other], axis=1))

    def all_sum(self, v):
        for axis in ("sp", "dp"):
            bit = 1
            while bit < lax.axis_size(axis):
                v = v + swap(v, axis, bit)
                bit *= 2
        return v


def norm_forward(halves, gains, shifts):
    width = sum(h.shape[1] for h in halves)
    mean = sum(jnp.sum(h, axis=1, keepdims=True) for h in halves) / width
    centred = [h - mean for h in halves]
    inv_std = lax.rsqrt(sum(jnp.sum(c * c, axis=1, keepdims=True) for c in centred) / width + EPSILON)
    normed = [c * inv_std for c in centred]
    return [n * a + b for n, a, b in zip(normed, gains, shifts)], normed, inv_std


def norm_backward(incoming, normed, inv_std, gains):
    width = sum(h.shape[1] for h in incoming)
    scaled = [e * a for e, a in zip(incoming, gains)]
    mean = sum(jnp.sum(s, axis=1, keepdims=True) for s in scaled) / width
    along = sum(jnp.sum(s * n, axis=1, keepdims=True) for s, n in zip(scaled, normed)) / width
    grads = [inv_std * (s - mean - n * along) for s, n in zip(scaled, normed)]
    gain_sums = [jnp.sum(e * n, axis=0) for e, n in zip(incoming, normed)]
    return grads, gain_sums, [jnp.sum(e, axis=0) for e in incoming]


def general_layer(
    tokens,
    seq_spans,
    valid_mask,
    cotangent,
    w_qkv,
    w_out,
    w_up,
    w_down,
    model_gains,
    model_shifts,
    mid_gain,
    hidden_shifts,
    head_scale,
):
    dp, sp = lax.axis_size("dp"), lax.axis_size("sp")
    grid = Grid(dp, sp)
    nx, ny, nz = grid.nx, grid.ny, grid.nz
    me_d, me_s = lax.axis_index("dp"), lax.axis_index("sp")
    rows, width = tokens.shape
    group = rows * sp
    heads = head_scale.shape[0]
    nh = heads // sp
    lw = nh * HEAD
    block = width // dp
    ff = mid_gain.shape[0]

    place = jnp.arange(dp, dtype=jnp.int32)
    to_rel = ((place % nz) * ny + place // nz) ^ me_d
    away = place ^ me_d
    to_abs = (away % ny) * nz + away // ny
    sp_place = jnp.arange(sp, dtype=jnp.int32)
    sp_rel = ((sp_place % nx) * 2 + sp_place // nx) ^ me_s
    sp_away = sp_place ^ me_s
    sp_abs = (sp_away % 2) * nx + sp_away // 2

    pad_rows = 16
    valid_rows = rows // lw
    blocks = w_qkv.reshape(block, 3, lw).transpose(1, 0, 2)
    blocks = jnp.concatenate([blocks, jnp.zeros((sp - 3, block, lw), bf16)], axis=0)
    turned = jnp.concatenate(
        [lax.dynamic_slice_in_dim(blocks, (t - 3 * me_s) % sp, 1, 0) for t in range(sp)], axis=0
    )
    flag_rows = jnp.concatenate(
        [valid_mask.astype(bf16).reshape(valid_rows, lw), jnp.zeros((pad_rows - valid_rows, lw), bf16)], axis=0
    )
    sent = jnp.concatenate([turned, jnp.broadcast_to(flag_rows[None], (sp, pad_rows, lw))], axis=1)
    got = lax.all_to_all(sent, "sp", 0, 0, tiled=True)
    keep = got[:, block : block + valid_rows].reshape(group) > 0.5
    wq_shard = jnp.concatenate(
        [lax.dynamic_slice_in_dim(got, (t * sp + me_s) // 3, 1, 0)[0, :block] for t in range(3)], axis=1
    )
    wq = grid.gather_y(grid.gather_z(wq_shard))

    gains = reorder(model_gains, to_rel, block)
    shifts = reorder(model_shifts, to_rel, block)
    stream = reorder(tokens, to_rel, block).astype(f32)
    upstream = reorder(cotangent, to_rel, block) * valid_mask.astype(bf16)[:, None]
    (first_out,), (first_normed,), first_std = norm_forward([stream], gains[0:1], shifts[3:4])
    first = first_out.astype(bf16)

    crossed = [first] + [swap(first, "sp", b) for b in grid.x_bits]
    firsts = []
    for piece in crossed:
        firsts += [piece, swap(piece, "sp", 1)]
    piece_bits = [b for k in [0] + grid.x_bits for b in (k, k + 1)]
    qkv_shift = jnp.concatenate(
        [
            lax.dynamic_slice_in_dim(model_shifts[0], me_s * lw, lw, 0),
            jnp.zeros((lw,), f32),
            lax.dynamic_slice_in_dim(model_shifts[1], me_s * lw, lw, 0),
        ]
    )
    firsts_cat = jnp.concatenate(firsts, axis=0)
    qkv_rel = (mm(firsts_cat, wq) + qkv_shift).astype(bf16)
    group_order = sp_place ^ me_s
    qkv = reorder_rows(qkv_rel, group_order, rows)

    low_down = jnp.concatenate([w_out, w_down], axis=1)
    od_own = grid.gather(low_down)
    up_own = grid.gather(w_up)
    oc, dc = w_out.shape[1], w_down.shape[1]
    out_own = jnp.concatenate([od_own[:, k * (oc + dc) : k * (oc + dc) + oc] for k in range(nx)], axis=1)
    down_own = jnp.concatenate([od_own[:, k * (oc + dc) + oc : (k + 1) * (oc + dc)] for k in range(nx)], axis=1)
    wos = jnp.concatenate([out_own, swap(out_own, "sp", 1)], axis=1)
    downs = [down_own, swap(down_own, "sp", 1)]
    ups = [up_own, swap(up_own, "sp", 1)]
    wo = reorder(reorder_rows(wos, to_abs, block), sp_abs, oc)

    tab = jnp.concatenate([sp_place, me_s[None].astype(jnp.int32)])
    hd = Heads(nh, nh, 0, (0, 1, 2), 0, sp, sp)
    keep_col = keep.astype(f32)[:, None]
    scaled, o_t, lse = attend_forward(hd, tab, seq_spans[0], qkv, keep_col, head_scale)
    returned = lax.all_to_all(scaled.reshape(sp, rows, lw), "sp", 0, 0, tiled=True)
    merged = jnp.concatenate([returned[t] for t in range(sp)], axis=1)

    attn_pre = reorder(mm(merged, wo) + model_shifts[2], to_rel, block)
    (attn_out,), (attn_normed,), attn_std = norm_forward([attn_pre], gains[1:2], shifts[4:5])
    middle = stream + attn_out
    (second_out,), (second_normed,), second_std = norm_forward([middle], gains[2:3], shifts[5:6])
    second = second_out.astype(bf16)

    ff_half = ff // 2
    hidden_vectors = reorder(
        jnp.concatenate([mid_gain[None], hidden_shifts], axis=0), sp_rel, ff // sp
    )
    split = lambda v: [v[:, :ff_half], v[:, ff_half:]]
    hg, hb, hs = split(hidden_vectors[0:1]), split(hidden_vectors[1:2]), split(hidden_vectors[2:3])
    pre = [mm(second, w) + b for w, b in zip(ups, hb)]
    activated, pulls = zip(*[jax.vjp(jax.nn.gelu, p) for p in pre])
    hidden_out, hidden_normed, hidden_std = norm_forward(activated, hg, hs)
    hidden = [h.astype(bf16) for h in hidden_out]
    out_rel = middle + mm_cols(hidden[0], downs[0]) + mm_cols(hidden[1], downs[1]) + shifts[6:7]
    layer_out = reorder(out_rel.astype(bf16), to_abs, block)

    pair = lambda x: jnp.concatenate([x, swap(x, "sp", 1)], axis=0)
    across = lambda halves: jnp.concatenate([halves[0], swap(halves[1], "sp", 1)], axis=0)
    upstream_pair = pair(upstream)
    g_down = mm_rows(upstream_pair, across(hidden)).astype(bf16)
    grad_w_down = grid.scatter(g_down)

    hidden_grad = [mm(upstream, w) for w in downs]
    act_grad, grad_mid, grad_mid_shift = norm_backward(hidden_grad, hidden_normed, hidden_std, hg)
    pre_grad = [pull(a)[0].astype(bf16) for pull, a in zip(pulls, act_grad)]
    second_grad = mm_cols(pre_grad[0], ups[0]) + mm_cols(pre_grad[1], ups[1])
    (middle_part,), (gain_ffn,), (shift_ffn,) = norm_backward([second_grad], [second_normed], second_std, gains[2:3])
    middle_grad = upstream.astype(f32) + middle_part
    (attn_grad_full,), (gain_attn,), (shift_attn,) = norm_backward([middle_grad], [attn_normed], attn_std, gains[1:2])
    attn_grad_rel = attn_grad_full.astype(bf16)
    attn_grad = reorder(attn_grad_rel, to_abs, block)
    merged_grad = mm_cols(attn_grad, wo).astype(bf16)
    scattered = jnp.stack([merged_grad[:, t * lw : (t + 1) * lw] for t in range(sp)], axis=0)
    scaled_grad = lax.all_to_all(scattered, "sp", 0, 0, tiled=True).reshape(group, lw)

    g_up = mm_rows(pair(second), across(pre_grad)).astype(bf16)
    grad_w_up = grid.scatter(g_up)
    merged_rel = reorder(merged, to_rel, block)
    attn_grad_cols = reorder(attn_grad, sp_rel, oc)
    g_out = mm_rows(pair(merged_rel), across([attn_grad_cols[:, : width // 2], attn_grad_cols[:, width // 2 :]]))
    grad_w_out = grid.scatter_z(grid.scatter_y(grid.scatter_x(g_out)))

    qkv_grad, head_sums = attend_backward(
        hd, tab, seq_spans[0], qkv, keep_col, head_scale, scaled_grad, o_t, lse
    )
    qkv_grad_rel = reorder_rows(qkv_grad, group_order, rows)
    first_part = mm_cols(qkv_grad_rel, wq)
    pieces = [first_part[t * rows : (t + 1) * rows] for t in range(sp)]
    folded = [
        pieces[t].astype(f32) + swap(pieces[t + 1].astype(bf16), "sp", 1).astype(f32) for t in range(0, sp, 2)
    ]
    first_grad = grid.fold(folded, "sp", grid.x_bits)
    (input_part,), (gain_in,), (shift_in,) = norm_backward([first_grad], [first_normed], first_std, gains[0:1])
    grad_tokens = reorder(middle_grad + input_part, to_abs, block)

    g_qkv = mm_rows(firsts_cat, qkv_grad_rel)
    g_mine = grid.scatter_z(grid.scatter_y(g_qkv)).astype(bf16)
    g_blocks = jnp.concatenate(
        [g_mine.reshape(block, 3, lw).transpose(1, 0, 2), jnp.zeros((1, block, lw), bf16)], axis=0
    )
    back = []
    for t in range(sp):
        which = jnp.int32(3)
        for u in range(3):
            which = jnp.where((u * sp + me_s) // 3 == t, u, which)
        back.append(lax.dynamic_slice_in_dim(g_blocks, which, 1, 0))
    home = lax.all_to_all(jnp.concatenate(back, axis=0), "sp", 0, 0, tiled=True)
    grad_w_qkv = jnp.concatenate(
        [lax.dynamic_slice_in_dim(home, (3 * me_s + u) % sp, 1, 0)[0] for u in range(3)], axis=1
    ).astype(f32)

    qkv_sums = jnp.sum(qkv_grad.astype(f32), axis=0)
    zeros = jnp.zeros((2, width), f32)
    bias_sums = lax.dynamic_update_slice(
        zeros, jnp.stack([qkv_sums[:lw], qkv_sums[2 * lw :]]), (0, me_s * lw)
    )
    sum_early = jnp.concatenate(
        [
            reorder(
                jnp.stack(
                    [
                        gain_attn,
                        gain_ffn,
                        jnp.sum(attn_grad_rel.astype(f32), axis=0),
                        shift_attn,
                        shift_ffn,
                        jnp.sum(upstream.astype(f32), axis=0),
                    ]
                ),
                to_abs,
                block,
            ),
            reorder(
                jnp.stack(
                    [
                        jnp.concatenate(grad_mid),
                        jnp.concatenate([jnp.sum(p.astype(f32), axis=0) for p in pre_grad]),
                        jnp.concatenate(grad_mid_shift),
                    ]
                ),
                sp_abs,
                ff // sp,
            ).reshape(3 * ff // width, width),
        ],
        axis=0,
    )
    early = grid.all_sum(sum_early)
    scale_row = lax.dynamic_update_slice(
        jnp.zeros((1, width), f32), head_sums[1:2, :nh], (0, me_s * nh)
    )
    late = grid.all_sum(
        jnp.concatenate(
            [reorder(jnp.stack([gain_in, shift_in]), to_abs, block), bias_sums, scale_row], axis=0
        )
    )
    grad_model_gains = jnp.stack([late[0], early[0], early[1]])
    grad_model_shifts = jnp.stack([late[2], late[3], early[2], late[1], early[3], early[4], early[5]])
    hidden_sums = early[6:].reshape(3, ff)
    return (
        layer_out,
        grad_tokens,
        grad_w_qkv,
        grad_w_out,
        grad_w_up,
        grad_w_down,
        grad_model_gains,
        grad_model_shifts,
        hidden_sums[0],
        hidden_sums[1:3],
        late[4, :heads],
    )


REL, HID, ORD, COLS, WHO, SEND, SLOT = 0, 8, 16, 24, 32, 33, 36
LANES = 128


def matchings(sp):
    left = {s: {3 * s + k: (3 * s + k) % sp for k in range(3)} for s in range(sp)}
    rounds = []
    for _ in range(3):
        taken = {}

        def seat(s, seen):
            for b, to in sorted(left[s].items(), key=lambda e: e[1] != s):
                if to not in seen:
                    seen.add(to)
                    if to not in taken or seat(taken[to][0], seen):
                        taken[to] = (s, b)
                        return True
            return False

        for s in range(sp):
            seat(s, set())
        one = [None] * sp
        for to, (s, b) in taken.items():
            one[s] = (b - 3 * s, b // sp, to)
            del left[s][b]
        rounds.append(one)
    return rounds


def tables(dp, sp, ny, nz, rounds):
    out = np.zeros((dp * sp, 128), np.int32)
    for d in range(dp):
        for s in range(sp):
            row = out[d * sp + s]
            where = {}
            for p in range(dp):
                row[REL + p] = ((p % nz) * ny + p // nz) ^ d
                where[row[REL + p]] = p
            for q in range(2 * sp):
                dc, half, dx = q // 4, q // 2 % 2, q % 2
                row[HID + q] = ((dx * 2 + dc) ^ s) * 2 + half
                row[COLS + q] = where[row[HID + q]]
            for t in range(sp):
                row[ORD + t] = s ^ t
            row[WHO] = s
            for m in range(3):
                row[SEND + m] = rounds[m][s][0]
                row[SLOT + m] = next(rounds[m][a][1] for a in range(sp) if rounds[m][a][2] == s)
    return out


def span(index, size):
    return pl.ds(pl.multiple_of(index * size, size), size)


def norm_of(x):
    mean = jnp.mean(x, axis=1, keepdims=True)
    centred = x - mean
    inv_std = lax.rsqrt(jnp.mean(centred * centred, axis=1, keepdims=True) + EPSILON)
    return centred * inv_std, inv_std


def norm_back(incoming, normed, inv_std, gain):
    scaled = incoming * gain
    mean = jnp.mean(scaled, axis=1, keepdims=True)
    along = jnp.mean(scaled * normed, axis=1, keepdims=True)
    return inv_std * (scaled - mean - normed * along)


def down_sum(x):
    return jnp.sum(x, axis=0, keepdims=True)


def whole(shape):
    return pl.BlockSpec(shape, lambda *_: (0,) * len(shape))


def by_rows(rows, cols):
    return pl.BlockSpec((rows, cols), lambda i, *_: (i, 0))


def call(name, body, tab, args, outs, steps=1, in_specs=None, out_specs=None, scratch=(), deps=(), vmem=40, flops=0, moved=0):
    in_specs = [whole(a.shape) for a in args] if in_specs is None else in_specs
    out_specs = [whole(s) for s, _ in outs] if out_specs is None else out_specs
    return pl.pallas_call(
        skipping(body, 1 + len(args), len(deps)),
        grid_spec=pltpu.PrefetchScalarGridSpec(
            num_scalar_prefetch=1,
            grid=(steps,),
            in_specs=list(in_specs) + unread(deps),
            out_specs=list(out_specs),
            scratch_shapes=list(scratch),
        ),
        out_shape=[jax.ShapeDtypeStruct(s, t) for s, t in outs],
        compiler_params=pltpu.CompilerParams(vmem_limit_bytes=vmem << 20),
        cost_estimate=pl.CostEstimate(flops=int(flops), bytes_accessed=int(moved) or (4 << 20), transcendentals=0),
        name=name,
    )(tab, *args, *deps)


def part_body(tab, w, *outs):
    width = outs[0].shape[1]
    for m, out in enumerate(outs):
        out[...] = w[:, span(tab[SEND + m], width)]


def join_body(tab, *refs):
    pieces, out = refs[:-1], refs[-1]
    for m, piece in enumerate(pieces):
        for e in range(2):
            out[:, span(tab[SLOT + m] + 3 * e, LANES)] = piece[:, e * LANES : (e + 1) * LANES]


def unjoin_body(tab, e0, e1, *outs):
    for m, out in enumerate(outs):
        for e, g in enumerate((e0, e1)):
            out[:, e * LANES : (e + 1) * LANES] = g[:, span(tab[SLOT + m], LANES)].astype(bf16)


def home_body(tab, *refs):
    pieces, out = refs[:-1], refs[-1]
    width = pieces[0].shape[1]
    for m, piece in enumerate(pieces):
        out[:, span(tab[SEND + m], width)] = piece[...].astype(f32)


def prologue_body(tab, tok, cot, vcol, vrow, gains, shifts, mid, hsh, first_ref, up_ref, tokr_ref, vec_ref, hid_ref):
    rows, width = tok.shape
    unit = mid.shape[1] // 8
    valid = vcol[...]
    vec_ref[...] = jnp.zeros_like(vec_ref)
    hid_ref[...] = jnp.zeros_like(hid_ref)
    for p in range(8):
        at, to = span(tab[REL + p], LANES), slice(p * LANES, (p + 1) * LANES)
        tokr_ref[:, to] = tok[:, at]
        vec_ref[0:3, to] = gains[:, at]
        vec_ref[3:10, to] = shifts[:, at]
        at, to = span(tab[HID + p], unit), slice(p * unit, (p + 1) * unit)
        hid_ref[0:1, to] = mid[:, at]
        hid_ref[1:3, to] = hsh[:, at]
    gain, shift = vec_ref[0:1, :], vec_ref[6:7, :]

    def chunk(i, carry):
        at = span(i, 64)
        normed, _ = norm_of(tokr_ref[at, :].astype(f32))
        first_ref[at, :] = (normed * gain + shift).astype(bf16)
        return carry

    lax.fori_loop(0, rows // 64, chunk, 0)
    first_ref[rows:, :] = jnp.broadcast_to(vrow[...], (16, width))
    for p in range(8):
        at, to = span(tab[REL + p], LANES), slice(p * LANES, (p + 1) * LANES)
        masked = cot[:, at].astype(f32) * valid
        up_ref[:, to] = masked.astype(bf16)
        vec_ref[10:11, to] = down_sum(masked)


def project_body(count, tab, *refs):
    pieces, (w0, w1, shifts, out_ref, keep_ref) = refs[:count], refs[count:]
    rows, depth = out_ref.shape[0], w0.shape[0]
    bias = []
    for e in range(2):
        at = pl.ds(pl.multiple_of(tab[WHO] * 2 * LANES + e * LANES, LANES), LANES)
        bias += [shifts[0:1, at], jnp.zeros((1, LANES), f32), shifts[1:2, at]]
    bias = jnp.concatenate(bias, axis=1)
    for k in range(count):

        @pl.when(pl.program_id(0) == k)
        def _():
            x = pieces[k]
            out_ref[...] = (mm(x[:rows, :depth], w0[...]) + mm(x[:rows, depth:], w1[...]) + bias).astype(bf16)
            keep_ref[...] = x[rows:, :rows].astype(f32).T[:, 0:1]


def middle_body(tab, r0, r1, tok, vec, *refs):
    pieces, (second_ref, mid_ref, norm_ref, std_ref, merged_ref, wo) = refs[:12], refs[12:]
    half = pieces[2].shape[0]

    @pl.when(pl.program_id(0) == 0)
    def _():
        for c in range(2):
            a0, a1, b00, b01, b10, b11 = pieces[6 * c : 6 * c + 6]
            for dx, a in enumerate((a0, a1)):
                wo[:, span(tab[COLS + 4 * c + dx], LANES)] = a[...]
            for dx, (top, bottom) in enumerate(((b00, b10), (b01, b11))):
                to = span(tab[COLS + 4 * c + 2 + dx], LANES)
                wo[:half, to] = top[...]
                wo[half:, to] = bottom[...]

    for p in range(8):
        a = tab[REL + p]
        source, odd = a // 2, lax.rem(a, 2)
        merged_ref[:, p * LANES : (p + 1) * LANES] = jnp.where(odd == 0, r0[source], r1[source])
    normed, inv_std = norm_of(mm(merged_ref[...], wo[...]) + vec[5:6, :])
    middle = tok[...].astype(f32) + (normed * vec[1:2, :] + vec[7:8, :])
    norm_ref[...] = normed
    std_ref[...] = inv_std
    mid_ref[...] = middle
    again, _ = norm_of(middle)
    second_ref[...] = (again * vec[2:3, :] + vec[8:9, :]).astype(bf16)


GELU = 0.7978845608028654
CUBE = 0.044715


def ffn_body(unit, tab, second, upstream, mid, hid, vec, *refs):
    ins, (hown, hsib, pown, psib, sg_ref, lo_ref, sums_ref, upv, dnv, act, slope, back, sems) = refs[:16], refs[16:]
    i = pl.program_id(0)
    depth = upv.shape[0] // 2
    ff = upv.shape[1]

    def copies(q, which):
        c, half, dx = q // 4, q // 2 % 2, q % 2
        held = (upv, dnv)[which]
        a0, a1, b0, b1 = ins[8 * which + 4 * c : 8 * which + 4 * c + 4]
        to, at = pl.ds(q * unit, unit), pl.ds(0, unit)
        if half == 0:
            pairs = [((a0, a1)[dx].at[:, at], held.at[:, to])]
        else:
            rows = pl.ds(dx * depth, depth)
            pairs = [(b0.at[rows, at], held.at[pl.ds(0, depth), to]), (b1.at[rows, at], held.at[pl.ds(depth, depth), to])]
        return [pltpu.make_async_copy(a, b, sems.at[which, q, k]) for k, (a, b) in enumerate(pairs)]

    @pl.when(i == 0)
    def _():
        sums_ref[...] = jnp.zeros_like(sums_ref)
        for q in range(8):
            for copy in copies(q, 0):
                copy.start()
        for q in range(8):
            for copy in copies(q, 1):
                copy.start()

    x = second[...]
    total = jnp.zeros((x.shape[0], 1), f32)
    for q in range(8):
        at = slice(q * unit, (q + 1) * unit)

        @pl.when(i == 0)
        def _():
            for copy in copies(q, 0):
                copy.wait()

        pre = mm(x, upv[:, at]) + hid[1:2, at]
        squared = pre * pre
        t = jnp.tanh(pre * (GELU + (GELU * CUBE) * squared))
        one = 0.5 + 0.5 * t
        value = pre * one
        act[:, at] = value
        slope[:, at] = one + 0.5 * pre * (1.0 - t * t) * (GELU + (3 * GELU * CUBE) * squared)
        total = total + jnp.sum(value, axis=1, keepdims=True)
    mean = total / ff
    total = jnp.zeros_like(mean)
    for q in range(8):
        at = slice(q * unit, (q + 1) * unit)
        centred = act[:, at] - mean
        total = total + jnp.sum(centred * centred, axis=1, keepdims=True)
    inv_std = lax.rsqrt(total / ff + EPSILON)
    u = upstream[...]
    m1, m2 = jnp.zeros_like(mean), jnp.zeros_like(mean)
    low = jnp.zeros(mid.shape, f32)
    for q in range(8):
        at = slice(q * unit, (q + 1) * unit)

        @pl.when(i == 0)
        def _():
            for copy in copies(q, 1):
                copy.wait()

        incoming = mm(u, dnv[:, at])
        normed = (act[:, at] - mean) * inv_std
        act[:, at] = normed
        gain = hid[0:1, at]
        held, to = ((hown, at) if q < 4 else (hsib, slice((q - 4) * unit, (q - 3) * unit)))
        hidden = (normed * gain + hid[2:3, at]).astype(bf16)
        held[:, to] = hidden
        low = low + mm_cols(hidden, dnv[:, at])
        along = incoming * normed
        sums_ref[0:1, at] += down_sum(along)
        sums_ref[2:3, at] += down_sum(incoming)
        m1 = m1 + jnp.sum(incoming * gain, axis=1, keepdims=True)
        m2 = m2 + jnp.sum(along * gain, axis=1, keepdims=True)
        back[:, at] = incoming
    m1, m2 = m1 / ff, m2 / ff
    second_grad = jnp.zeros(mid.shape, f32)
    for q in range(8):
        at = slice(q * unit, (q + 1) * unit)
        grad = inv_std * (back[:, at] * hid[0:1, at] - m1 - act[:, at] * m2)
        pre_grad = (grad * slope[:, at]).astype(bf16)
        held, to = ((pown, at) if q < 4 else (psib, slice((q - 4) * unit, (q - 3) * unit)))
        held[:, to] = pre_grad
        sums_ref[1:2, at] += down_sum(pre_grad.astype(f32))
        second_grad = second_grad + mm_cols(pre_grad, upv[:, at])
    sg_ref[...] = second_grad
    out = (mid[...] + low + vec[9:10, :]).astype(bf16)
    for p in range(8):
        lo_ref[:, span(tab[REL + p], LANES)] = out[:, p * LANES : (p + 1) * LANES]


def heads_body(tab, grad, mid, norm, std, up, vec, wo, mg_ref, own_ref, sib_ref, o0_ref, o1_ref, sums_ref, scr):
    @pl.when(pl.program_id(0) == 0)
    def _():
        sums_ref[...] = jnp.zeros_like(sums_ref)

    incoming = grad[...]
    again, inv_std = norm_of(mid[...])
    sums_ref[1:2, :] += down_sum(incoming * again)
    sums_ref[4:5, :] += down_sum(incoming)
    middle_grad = up[...].astype(f32) + norm_back(incoming, again, inv_std, vec[2:3, :])
    mg_ref[...] = middle_grad
    normed = norm[...]
    sums_ref[0:1, :] += down_sum(middle_grad * normed)
    sums_ref[3:4, :] += down_sum(middle_grad)
    low = norm_back(middle_grad, normed, std[...], vec[1:2, :]).astype(bf16)
    sums_ref[2:3, :] += down_sum(low.astype(f32))
    scr[...] = low
    for q in range(8):
        held = own_ref if q < 4 else sib_ref
        held[:, (q % 4) * LANES : (q % 4 + 1) * LANES] = scr[:, span(tab[COLS + q], LANES)]
    got = mm_cols(low, wo[...]).astype(bf16)
    for p in range(8):
        a = tab[REL + p]
        source, odd = a // 2, lax.rem(a, 2)
        for e, out in enumerate((o0_ref, o1_ref)):

            @pl.when(odd == e)
            def _():
                out[source] = got[:, p * LANES : (p + 1) * LANES]


def grads_body(sets, widths, tab, *refs):
    ins, (ak, asend, bk, bsend, xt) = refs[: 4 * sets], refs[4 * sets :]
    half = bk.shape[0]
    total = sum(widths)
    at = 0
    for n, wide in enumerate(widths):
        x0, x1, y0, y1 = ins[4 * n : 4 * n + 4]
        tokens = x0.shape[0]

        @pl.when(pl.program_id(0) == n)
        def _():
            xt[:, :tokens] = x0[...].T
            xt[:, tokens:] = x1[...].T
            for q in range(4):
                cols = slice(q * wide, (q + 1) * wide)
                g = mm(xt[...], jnp.concatenate([y0[:, cols], y1[:, cols]], axis=0)).astype(bf16)
                if q < 2:
                    (ak, asend)[q][:, at : at + wide] = g
                else:
                    to = slice((q - 2) * total + at, (q - 2) * total + at + wide)
                    bk[:, to] = g[:half]
                    bsend[:, to] = g[half:]

        at += wide


def fold_body(tab, ak, ra, bk, rb, a2k, a2s, b2k, b2s):
    rows, cols = b2k.shape
    a = ak[...].astype(f32) + ra[...].astype(f32)
    a2k[...] = a[:rows].astype(bf16)
    a2s[...] = a[rows:].astype(bf16)
    b = bk[...].astype(f32) + rb[...].astype(f32)
    b2k[...] = b[:, :cols].astype(bf16)
    b2s[...] = b[:, cols:].astype(bf16)


def spread_body(tab, ak, ra, bk, rb, keep, *sends):
    rows, cols = keep.shape[0], ak.shape[1]
    for side, (k, r) in enumerate(((ak, ra), (bk, rb))):
        total = k[...].astype(f32) + r[...].astype(f32)
        to = slice(side * cols, (side + 1) * cols)
        keep[:, to] = total[:rows]
        for n, send in enumerate(sends, 1):
            send[:, to] = total[n * rows : (n + 1) * rows].astype(bf16)


def gathered_body(widths, tab, keep, *refs):
    received, outs = refs[: len(refs) - len(widths)], refs[len(refs) - len(widths) :]
    total = keep[...]
    for r in received:
        total = total + r[...].astype(f32)
    half = keep.shape[1] // 2
    at = 0
    for out, wide in zip(outs, widths):
        out[:, :wide] = total[:, at : at + wide]
        out[:, wide:] = total[:, half + at : half + at + wide]
        at += wide


def scatter_weights(grid, tab, sets, widths, tag, deps=()):
    rows = sets[0][0].shape[1]
    total = sum(widths)
    args = [a for one in sets for a in one]
    outs = [((rows, total), bf16)] * 2 + [((rows // 2, 2 * total), bf16)] * 2
    tokens = sets[0][0].shape[0]
    ak, asend, bk, bsend = call(
        "grads_" + tag, functools.partial(grads_body, len(sets), widths), tab, args, outs, steps=len(sets),
        scratch=[pltpu.VMEM((rows, 2 * tokens), bf16)], vmem=56, flops=2 * rows * 4 * total * 2 * tokens, deps=deps,
    )
    ra, rb = swap(asend, "sp", 2), swap(bsend, "dp", 1)
    yield (ra, rb)
    quarter = [((rows // 2, total), bf16)] * 4
    a2k, a2s, b2k, b2s = call("fold_" + tag, fold_body, tab, [ak, ra, bk, rb], quarter, moved=8 << 20)
    ra, rb = swap(a2s, "dp", 1), swap(b2s, "sp", 2)
    yield (ra, rb)
    shard = (rows // 8, 2 * total)
    keep, *sends = call("spread_" + tag, spread_body, tab, [a2k, ra, b2k, rb], [(shard, f32)] + [(shard, bf16)] * 3)
    received = [swap(s, "dp", b) for s, b in zip(sends, grid.z_bits)]
    yield tuple(received)
    yield call(
        "sum_" + tag, functools.partial(gathered_body, widths), tab, [keep] + received,
        [((rows // 8, 2 * w), f32) for w in widths],
    )


def slabs_body(tab, *refs):
    pieces, (first, other) = refs[:-2], refs[-2:]
    rows, half = pieces[0].shape[0], first.shape[1]
    for k, piece in enumerate(pieces):
        to = slice(k * rows, (k + 1) * rows)
        first[to, :] = piece[:, :half]
        other[to, :] = piece[:, half:]


def stack_body(tab, a, b, out):
    rows = a.shape[0]
    out[:rows, :] = a[...]
    out[rows:, :] = b[...]


def stack(tab, a, b, tag):
    return call("stack_" + tag, stack_body, tab, [a, b], [((2 * a.shape[0], a.shape[1]), a.dtype)])[0]


def gather_weights(grid, tab, shard, tag, deps=()):
    if deps:
        shard = call("shard_" + tag, lambda tab, x, o: o.__setitem__(Ellipsis, x[...]), tab, [shard], [(shard.shape, bf16)], deps=deps)[0]
    pieces = [shard] + [swap(shard, "dp", b) for b in grid.z_bits]
    yield tuple(pieces[1:])
    rows, cols = shard.shape
    first, other = call("slabs_" + tag, slabs_body, tab, pieces, [((4 * rows, cols // 2), bf16)] * 2)
    ra, rb = swap(first, "dp", 1), swap(other, "sp", 2)
    yield (ra, rb)
    a0 = stack(tab, first, ra, tag)
    b0 = stack(tab, other, rb, tag)
    a1, b1 = swap(a0, "sp", 2), swap(b0, "dp", 1)
    own = [a0, a1, b0, b1]
    yield (a1, b1)
    sib = [swap(p, "sp", 1) for p in own]
    yield own + sib


def first_grad_body(tab, g0, g1, wy0, wy1, mine, cross, far):
    i = pl.program_id(0)
    half = 3 * LANES
    g = jnp.concatenate([g0[...], g1[...]], axis=1)
    got = jnp.concatenate([mm_cols(g, wy0[...]), mm_cols(g, wy1[...])], axis=1)
    rows = g0.shape[0]

    @pl.when(i == 0)
    def _():
        mine[...] = got

    @pl.when(i == 1)
    def _():
        cross[:rows] = got.astype(bf16)

    @pl.when(i == 2)
    def _():
        far[...] = got

    @pl.when(i == 3)
    def _():
        cross[rows:] = got.astype(bf16)


def relay_body(tab, far, theirs, out):
    out[...] = (far[...] + theirs[...].astype(f32)).astype(bf16)


def final_body(tab, mine, theirs, crossed, tok, mg, vec, s0, s1, out_ref, late_ref, acc):
    i = pl.program_id(0)
    width = tok.shape[1]

    @pl.when(i == 0)
    def _():
        acc[...] = jnp.zeros_like(acc)

    incoming = mine[...] + theirs[...].astype(f32) + crossed[...].astype(f32)
    normed, inv_std = norm_of(tok[...].astype(f32))
    acc[0:1, :] += down_sum(incoming * normed)
    acc[1:2, :] += down_sum(incoming)
    total = mg[...] + norm_back(incoming, normed, inv_std, vec[0:1, :])
    for p in range(8):
        out_ref[:, span(tab[REL + p], LANES)] = total[:, p * LANES : (p + 1) * LANES]

    @pl.when(i == pl.num_programs(0) - 1)
    def _():
        late_ref[...] = jnp.zeros_like(late_ref)
        for p in range(8):
            late_ref[0:2, span(tab[REL + p], LANES)] = acc[0:2, p * LANES : (p + 1) * LANES]
        lane = lax.broadcasted_iota(jnp.int32, (1, LANES), 1)
        for e, s in enumerate((s0, s1)):
            at = pl.ds(pl.multiple_of(tab[WHO] * 2 * LANES + e * LANES, LANES), LANES)
            late_ref[2:3, at] = s[0:1, :LANES]
            late_ref[3:4, at] = s[0:1, 2 * LANES :]
            for h in range(2):
                head = tab[WHO] * 4 + 2 * e + h
                late_ref[4:5, :LANES] += jnp.where(lane == head, jnp.sum(jnp.where(lane == h, s[1:2, :LANES], 0.0)), 0.0)


def pack_body(tab, sums, vec, hid, out_ref):
    width, unit = sums.shape[1], hid.shape[1] // 8
    out_ref[...] = jnp.zeros_like(out_ref)
    for p in range(8):
        to, at = span(tab[REL + p], LANES), slice(p * LANES, (p + 1) * LANES)
        out_ref[0:5, to] = sums[0:5, at]
        out_ref[5:6, to] = vec[10:11, at]
    for v in range(3):
        for q in range(8):
            unit_at = tab[HID + q]
            row, col = 6 + 4 * v + unit_at // 2, lax.rem(unit_at, 2)
            out_ref[pl.ds(row, 1), span(col, unit)] = hid[v : v + 1, q * unit : (q + 1) * unit]


def fast_layer(
    tokens,
    seq_spans,
    valid_mask,
    cotangent,
    w_qkv,
    w_out,
    w_up,
    w_down,
    model_gains,
    model_shifts,
    mid_gain,
    hidden_shifts,
    head_scale,
):
    dp, sp = lax.axis_size("dp"), lax.axis_size("sp")
    grid = Grid(dp, sp)
    rows, width = tokens.shape
    group = rows * sp
    heads = head_scale.shape[0]
    block = width // dp
    ff = mid_gain.shape[0]
    unit = ff // 8
    shard_lanes = 2 * LANES
    step = rows // 2

    rounds = matchings(sp)
    device = lax.axis_index("dp") * sp + lax.axis_index("sp")
    tab = lax.dynamic_slice_in_dim(jnp.asarray(tables(dp, sp, grid.ny, grid.nz, rounds)), device, 1, 0)[0]
    spans = seq_spans[0]
    forth = [[(s, rounds[m][s][2]) for s in range(sp)] for m in range(3)]
    back_to = [[(t, s) for s, t in pairs] for pairs in forth]
    carry = lambda x, pairs: x if all(a == b for a, b in pairs) else lax.ppermute(x, "sp", pairs)

    half_down, half_out = w_down.shape[1] // 2, w_out.shape[1] // 2
    shard = jnp.concatenate(
        [w_down[:, :half_down], w_out[:, :half_out], w_down[:, half_down:], w_out[:, half_out:]], axis=1
    )
    down_stages = gather_weights(grid, tab, shard, "down")
    arrived = next(down_stages)

    sent = call("part", part_body, tab, [w_qkv], [((block, shard_lanes), bf16)] * 3)
    moved = [carry(x, pairs) for x, pairs in zip(sent, forth)]
    wq_shard = call("join", join_body, tab, moved, [((block, 3 * shard_lanes), bf16)])[0]
    wq0 = grid.gather_z(wq_shard)
    wq1 = swap(wq0, "dp", 1)

    vcol = valid_mask.astype(f32)[:, None]
    vrow = jnp.pad(valid_mask.astype(bf16), (0, width - rows))[None]
    first, upstream, tokr, vec, hid = call(
        "prologue", prologue_body, tab,
        [tokens, cotangent, vcol, vrow, model_gains, model_shifts, mid_gain[None], hidden_shifts],
        [((rows + 16, width), bf16), ((rows, width), bf16), ((rows, width), bf16), ((16, width), f32), ((8, ff), f32)],
    )
    beyond = swap(first, "sp", 2)
    firsts = [first, swap(first, "sp", 1), beyond, swap(beyond, "sp", 1)]

    up_stages = gather_weights(grid, tab, w_up, "up", deps=arrived)
    next(up_stages)
    arrived = next(down_stages)

    pieces = firsts
    qkv, keep = call(
        "project", functools.partial(project_body, sp), tab, pieces + [wq0, wq1, model_shifts],
        [((group, 3 * shard_lanes), bf16), ((group, 1), f32)], steps=sp,
        out_specs=[by_rows(rows, 3 * shard_lanes), by_rows(rows, 1)], flops=2 * group * width * 3 * shard_lanes,
    )
    firsts_cat = jnp.concatenate([f[:rows] for f in firsts], axis=0)

    hds = [Heads(2, heads // sp, 2 * e, (3 * e, 3 * e + 1, 3 * e + 2), ORD, WHO, sp) for e in range(2)]
    attended = [attend_forward(hds[0], tab, spans, qkv, keep, head_scale, deps=arrived)]
    send_home = lambda x: lax.all_to_all(x.reshape(sp, rows, LANES), "sp", 0, 0, tiled=True)
    returned = [send_home(attended[0][0])]
    arrived_down = next(down_stages)
    arrived_up = next(up_stages)
    attended.append(attend_forward(hds[1], tab, spans, qkv, keep, head_scale, deps=arrived_up))
    returned.append(send_home(attended[1][0]))
    downs = next(down_stages)
    next(up_stages)
    ups = next(up_stages)

    out_at = half_down // LANES
    wo_args, wo_specs = [], []
    for c in range(2):
        a0, a1, b0, b1 = downs[4 * c : 4 * c + 4]
        wo_args += [a0, a1, b0, b0, b1, b1]
        wo_specs += [pl.BlockSpec((width, LANES), lambda *_: (0, out_at))] * 2
        for r in (0, 1, 0, 1):
            wo_specs.append(pl.BlockSpec((width // 2, LANES), lambda *_, r=r: (r, out_at)))
    ret_spec = pl.BlockSpec((sp, step, LANES), lambda i, *_: (0, i, 0))
    second, middle, attn_normed, attn_std, merged, wo = call(
        "to_middle", middle_body, tab, returned + [tokr, vec] + wo_args,
        [((rows, width), bf16), ((rows, width), f32), ((rows, width), f32), ((rows, 1), f32), ((rows, width), bf16), ((width, width), bf16)],
        steps=2,
        in_specs=[ret_spec, ret_spec, by_rows(step, width), whole(vec.shape)] + wo_specs,
        out_specs=[by_rows(step, width)] * 3 + [by_rows(step, 1), by_rows(step, width), whole((width, width))],
        flops=4 * rows * width * width,
    )

    anywhere = pl.BlockSpec(memory_space=pl.ANY)
    hid_own, hid_sib, pre_own, pre_sib, second_grad, layer_out, hidden_sums = call(
        "ffn", functools.partial(ffn_body, unit), tab, [second, upstream, middle, hid, vec] + ups + downs,
        [((rows, ff // 2), bf16)] * 4 + [((rows, width), f32), ((rows, width), bf16), ((8, ff), f32)],
        steps=2,
        in_specs=[by_rows(step, width)] * 3 + [whole(hid.shape), whole(vec.shape)] + [anywhere] * 16,
        out_specs=[by_rows(step, ff // 2)] * 4 + [by_rows(step, width)] * 2 + [whole((8, ff))],
        scratch=[pltpu.VMEM((width, ff), bf16)] * 2 + [pltpu.VMEM((step, ff), f32)] * 3 + [pltpu.SemaphoreType.DMA((2, 8, 2))],
        vmem=60, flops=20 * rows * width * ff, moved=40 << 20,
    )

    upstream_sib = swap(upstream, "sp", 1)
    down_sums = scatter_weights(grid, tab, [(upstream, upstream_sib, hid_own, swap(hid_sib, "sp", 1))], (unit,), "down")
    arrived = next(down_sums)

    middle_grad, attn_own, attn_sib, back0, back1, sums = call(
        "to_heads", heads_body, tab, [second_grad, middle, attn_normed, attn_std, upstream, vec, wo],
        [((rows, width), f32)] + [((rows, width // 2), bf16)] * 2 + [((sp, rows, LANES), bf16)] * 2 + [((8, width), f32)],
        steps=2,
        in_specs=[by_rows(step, width)] * 3 + [by_rows(step, 1), by_rows(step, width), whole(vec.shape), whole(wo.shape)],
        out_specs=[by_rows(step, width)] + [by_rows(step, width // 2)] * 2 + [ret_spec] * 2 + [whole((8, width))],
        scratch=[pltpu.VMEM((step, width), bf16)], flops=4 * rows * width * width,
    )
    fetch = lambda x: lax.all_to_all(x, "sp", 0, 0, tiled=True).reshape(group, LANES)
    grads_in = [fetch(back0), fetch(back1)]

    up_sums = scatter_weights(
        grid, tab,
        [(second, swap(second, "sp", 1), pre_own, swap(pre_sib, "sp", 1)), (merged, swap(merged, "sp", 1), attn_own, swap(attn_sib, "sp", 1))],
        (unit, LANES), "up",
    )
    early = grid.all_sum(call("pack", pack_body, tab, [sums, vec, hidden_sums], [((24, width), f32)])[0])

    first_up = next(up_sums)
    qkv_grads = [attend_backward(hds[0], tab, spans, qkv, keep, head_scale, grads_in[0], *attended[0][1:], deps=arrived)]
    arrived = next(down_sums)
    wide = 3 * LANES

    def qkv_scatter(e):
        g = mm_rows(firsts_cat, qkv_grads[e][0])
        sent = g[width // 2 :].astype(bf16)
        got = swap(sent, "dp", 1)
        yield (got,)
        total = g[: width // 2] + got.astype(f32)
        received = [swap(total[n * block : (n + 1) * block].astype(bf16), "dp", b) for n, b in enumerate(grid.z_bits, 1)]
        yield tuple(received)
        out = total[:block]
        for r in received:
            out = out + r.astype(f32)
        yield out

    qkv_sums = [qkv_scatter(0)]
    next(qkv_sums[0])
    qkv_grads.append(
        attend_backward(hds[1], tab, spans, qkv, keep, head_scale, grads_in[1], *attended[1][1:], deps=first_up + arrived)
    )
    (grad_w_down,) = (next(down_sums), next(down_sums))[1]
    next(up_sums)
    next(up_sums)
    grad_w_up, grad_w_out = next(up_sums)
    next(qkv_sums[0])

    by_token = lambda cols: pl.BlockSpec((rows, cols), lambda i, *_: (i, 0))
    mine, cross, far = call(
        "first_grad", first_grad_body, tab, [qkv_grads[0][0], qkv_grads[1][0], wq0, wq1],
        [((rows, width), f32), ((2 * rows, width), bf16), ((rows, width), f32)], steps=sp,
        in_specs=[by_token(wide), by_token(wide), whole(wq0.shape), whole(wq1.shape)], flops=2 * group * width * 2 * wide,
    )
    theirs = swap(cross, "sp", 1)
    relayed = call("relay", relay_body, tab, [far, theirs], [((rows, width), bf16)],
                   in_specs=[whole(far.shape), pl.BlockSpec((rows, width), lambda *_: (1, 0))])[0]
    crossed = swap(relayed, "sp", 2)

    qkv_sums.append(qkv_scatter(1))
    next(qkv_sums[1])
    next(qkv_sums[1])
    g_mine = [next(g) for g in qkv_sums]
    sent = call("unjoin", unjoin_body, tab, g_mine, [((block, shard_lanes), bf16)] * 3)
    got = [carry(x, pairs) for x, pairs in zip(sent, back_to)]
    grad_w_qkv = call("home", home_body, tab, got, [((block, 3 * shard_lanes), f32)])[0]

    grad_tokens, late = call(
        "to_tokens", final_body, tab, [mine, theirs, crossed, tokr, middle_grad, vec, qkv_grads[0][1], qkv_grads[1][1]],
        [((rows, width), f32), ((8, width), f32)], steps=2,
        in_specs=[by_rows(step, width)] * 5 + [whole(vec.shape), whole((8, wide)), whole((8, wide))],
        out_specs=[by_rows(step, width), whole((8, width))], scratch=[pltpu.VMEM((8, width), f32)],
    )
    late = grid.all_sum(late)
    grad_model_gains = jnp.stack([late[0], early[0], early[1]])
    grad_model_shifts = jnp.stack([late[2], late[3], early[2], late[1], early[3], early[4], early[5]])
    totals = early[6 : 6 + 3 * ff // width].reshape(3, ff)
    return (
        layer_out,
        grad_tokens,
        grad_w_qkv,
        grad_w_out,
        grad_w_up,
        grad_w_down,
        grad_model_gains,
        grad_model_shifts,
        totals[0],
        totals[1:3],
        late[4, :heads],
    )


def per_device(*arrays):
    dp, sp = lax.axis_size("dp"), lax.axis_size("sp")
    (rows, width), heads, ff = arrays[0].shape, arrays[12].shape[0], arrays[10].shape[0]
    if (dp, sp) == (8, 4) and width == 8 * LANES and heads * HEAD == width and ff == 4 * width and rows % BQ == 0:
        return fast_layer(*arrays)
    return general_layer(*arrays)


def solution(mesh):
    rows = P(("dp", "sp"), None)
    placed = (rows, P("dp", None), P(("dp", "sp")), rows) + (P("dp", "sp"),) * 4 + (P(),) * 5
    return jax.shard_map(
        per_device,
        mesh=mesh,
        in_specs=placed,
        out_specs=(rows, rows) + (P("dp", "sp"),) * 4 + (P(),) * 5,
        check_vma=False,
    )
```

```python
import functools

import jax
import jax.numpy as jnp
import numpy as np
from jax import lax
from jax.experimental import pallas as pl
from jax.experimental.pallas import tpu as pltpu
from jax.sharding import PartitionSpec as P

EPSILON = 1e-05
MASKED = -1e30
HEAD = 64
BQ = 256
bf16 = jnp.bfloat16
f32 = jnp.float32


def mm(a, b):
    return lax.dot_general(a, b, (((1,), (0,)), ((), ())), preferred_element_type=f32)


def mm_rows(a, b):
    return lax.dot_general(a, b, (((0,), (0,)), ((), ())), preferred_element_type=f32)


def mm_cols(a, b):
    return lax.dot_general(a, b, (((1,), (1,)), ((), ())), preferred_element_type=f32)


def skipping(kernel, at, count):
    return lambda *refs: kernel(*refs[:at], *refs[at + count :])


def unread(deps):
    return [pl.BlockSpec(memory_space=pl.ANY)] * len(deps)


def lanes_of(x, h):
    lane = lax.broadcasted_iota(jnp.int32, x.shape, 1) // HEAD
    return jnp.where(lane == h, x, jnp.zeros_like(x))


def segment_of(spans, places):
    count, end = jnp.zeros_like(places), jnp.int32(0)
    for k in range(spans.shape[0]):
        end = end + spans[k]
        count = count + (places >= end).astype(jnp.int32)
    return count


class Heads:
    def __init__(self, nh, local, first, blocks, order_at, who_at, parts):
        self.nh, self.local, self.first, self.blocks = nh, local, first, blocks
        self.order_at, self.who_at, self.parts = order_at, who_at, parts


def keys_of(hd, tab, spans, keep_ref, kseg, bk):
    for j in range(hd.parts):
        at = pl.ds(pl.multiple_of(tab[hd.order_at + j] * bk, bk), bk)
        places = j * bk + lax.broadcasted_iota(jnp.int32, (bk, 1), 0)
        kseg[at, :] = jnp.where(keep_ref[:, at].T[:, 0:1] > 0.5, segment_of(spans, places), -1)


def visible(i, j, bk, spans, kseg, at):
    kpos = j * bk + lax.broadcasted_iota(jnp.int32, (bk, BQ), 0)
    qpos = i * BQ + lax.broadcasted_iota(jnp.int32, (bk, BQ), 1)
    qseg = segment_of(spans, i * BQ + lax.broadcasted_iota(jnp.int32, (1, BQ), 1))
    return (kseg[at, :] == qseg) & (kpos <= qpos)


def each_block(hd, tab, spans, i, bk, body):
    first = segment_of(spans, i * BQ)

    def step(j, carry):
        at = pl.ds(pl.multiple_of(tab[hd.order_at + j] * bk, bk), bk)
        pl.when(first <= segment_of(spans, (j + 1) * bk - 1))(lambda: body(j, at))
        return carry

    lax.fori_loop(0, (i * BQ) // bk + 1, step, 0)


def fwd_kernel(hd, bk, tab, spans, q_ref, k_ref, v_ref, keep_ref, hs_ref, scaled_ref, o_ref, lse_ref,
               kseg, vms, sscr, mpart, lpart, acc):
    nh = hd.nh
    i = pl.program_id(0)

    @pl.when(i == 0)
    def _():
        for h in range(nh):
            vms[h] = lanes_of(v_ref[...], h)
        keys_of(hd, tab, spans, keep_ref, kseg, bk)

    qs = q_ref[...] * bf16(0.125)
    qm = [lanes_of(qs, h) for h in range(nh)]
    mpart[...] = jnp.full_like(mpart, MASKED)
    lpart[...] = jnp.zeros_like(lpart)
    acc[...] = jnp.zeros_like(acc)

    def one(j, at):
        kb = k_ref[at, :]
        mask = visible(i, j, bk, spans, kseg, at)
        for h in range(nh):
            s = jnp.where(mask, mm_cols(kb, qm[h]), MASKED)
            sscr[h, at, :] = s
            mpart[h] = jnp.maximum(mpart[h], jnp.max(s.reshape(bk // 8, 8, BQ), axis=0))

    each_block(hd, tab, spans, i, bk, one)
    ms = [jnp.max(mpart[h], axis=0, keepdims=True) for h in range(nh)]

    def two(j, at):
        pts = []
        for h in range(nh):
            p = jnp.exp(sscr[h, at, :] - ms[h])
            lpart[h] += jnp.sum(p.reshape(bk // 8, 8, BQ), axis=0)
            pts.append(p.astype(bf16).T)
        acc[...] += mm(
            jnp.concatenate(pts, axis=1),
            jnp.concatenate([vms[h, at, :] for h in range(nh)], axis=0),
        )

    each_block(hd, tab, spans, i, bk, two)
    out_t = acc[...].T
    parts = []
    for h in range(nh):
        rows = slice(h * HEAD, (h + 1) * HEAD)
        total = jnp.sum(lpart[h], axis=0, keepdims=True)
        result = out_t[rows, :] * (1.0 / total)
        o_ref[rows, :] = result
        parts.append(result * hs_ref[0, tab[hd.who_at] * hd.local + hd.first + h])
        lse_ref[h : h + 1, :] = ms[h] + jnp.log(total)
    scaled_ref[...] = jnp.concatenate(parts, axis=0).T.astype(bf16)


def head_specs(hd, n, w, bk):
    q, k, v = hd.blocks
    ratio = bk // BQ
    return [
        pl.BlockSpec((BQ, w), lambda i, t, s: (t[hd.order_at + (i * BQ) // bk] * ratio + i % ratio, q)),
        pl.BlockSpec((n, w), lambda i, t, s: (0, k)),
        pl.BlockSpec((n, w), lambda i, t, s: (0, v)),
    ]


def attend_forward(hd, tab, spans, qkv, keep, head_scale, deps=()):
    n, nh, w = qkv.shape[0], hd.nh, hd.nh * HEAD
    bk = n // hd.parts
    return pl.pallas_call(
        skipping(functools.partial(fwd_kernel, hd, bk), 7, len(deps)),
        grid_spec=pltpu.PrefetchScalarGridSpec(
            num_scalar_prefetch=2,
            grid=(n // BQ,),
            in_specs=head_specs(hd, n, w, bk)
            + [pl.BlockSpec((8, n), lambda i, t, s: (0, 0)), pl.BlockSpec(memory_space=pltpu.SMEM)]
            + unread(deps),
            out_specs=[
                pl.BlockSpec((BQ, w), lambda i, t, s: (i, 0)),
                pl.BlockSpec((w, BQ), lambda i, t, s: (0, i)),
                pl.BlockSpec((8, BQ), lambda i, t, s: (0, i)),
            ],
            scratch_shapes=[
                pltpu.VMEM((n, 1), jnp.int32),
                pltpu.VMEM((nh, n, w), bf16),
                pltpu.VMEM((nh, n, BQ), f32),
                pltpu.VMEM((nh, 8, BQ), f32),
                pltpu.VMEM((nh, 8, BQ), f32),
                pltpu.VMEM((BQ, w), f32),
            ],
        ),
        out_shape=[
            jax.ShapeDtypeStruct((n, w), bf16),
            jax.ShapeDtypeStruct((w, n), f32),
            jax.ShapeDtypeStruct((8, n), f32),
        ],
        compiler_params=pltpu.CompilerParams(vmem_limit_bytes=60 << 20),
        cost_estimate=pl.CostEstimate(flops=nh * n * n * HEAD * 38, bytes_accessed=1024, transcendentals=0),
        name="attend_forward",
    )(tab, spans, qkv, qkv, qkv, keep, head_scale[None], *deps)


def bwd_kernel(hd, bk, tab, spans, q_ref, k_ref, v_ref, keep_ref, hs_ref, sg_ref, o_ref, lse_ref,
               grad_ref, sums_ref, kseg, dk, dv, dq, gacc, kms):
    nh = hd.nh
    i = pl.program_id(0)
    n, w = k_ref.shape[0], nh * HEAD

    @pl.when(i == 0)
    def _():
        dk[...] = jnp.zeros_like(dk)
        dv[...] = jnp.zeros_like(dv)
        gacc[...] = jnp.zeros_like(gacc)
        for h in range(nh):
            kms[h] = lanes_of(k_ref[...], h)
        keys_of(hd, tab, spans, keep_ref, kseg, bk)

    qs = q_ref[...] * bf16(0.125)
    qm = [lanes_of(qs, h) for h in range(nh)]
    scales = [hs_ref[0, tab[hd.who_at] * hd.local + hd.first + h] for h in range(nh)]
    sg = sg_ref[...].astype(f32)
    lane = lax.broadcasted_iota(jnp.int32, (1, w), 1) // HEAD
    scale_row = jnp.zeros((1, w), f32)
    for h in range(nh):
        scale_row = jnp.where(lane == h, scales[h], scale_row)
    grads = (sg * scale_row).astype(bf16)
    dom = [lanes_of(grads, h) for h in range(nh)]
    o = o_ref[...]
    gacc[...] += sg.T * o
    weighed = grads.astype(f32).T * o
    delta = [jnp.sum(weighed[h * HEAD : (h + 1) * HEAD, :], axis=0, keepdims=True) for h in range(nh)]
    lse = [lse_ref[h : h + 1, :] for h in range(nh)]
    qcat = jnp.concatenate(qm, axis=0)
    docat = jnp.concatenate(dom, axis=0)
    dq[...] = jnp.zeros_like(dq)

    def block(j, at):
        kb = k_ref[at, :]
        vb = v_ref[at, :]
        mask = visible(i, j, bk, spans, kseg, at)
        ps, dss, dsts = [], [], []
        for h in range(nh):
            p = jnp.where(mask, jnp.exp(mm_cols(kb, qm[h]) - lse[h]), 0.0)
            ds = (p * (mm_cols(vb, dom[h]) - delta[h])).astype(bf16)
            ps.append(p.astype(bf16))
            dsts.append(ds.T)
            dss.append(ds)
        dv[at, :] += mm(jnp.concatenate(ps, axis=1), docat)
        dk[at, :] += mm(jnp.concatenate(dss, axis=1), qcat)
        dq[...] += mm(
            jnp.concatenate(dsts, axis=1),
            jnp.concatenate([kms[h, at, :] for h in range(nh)], axis=0),
        )

    each_block(hd, tab, spans, i, bk, block)
    mine = tab[hd.order_at + (i * BQ) // bk] * bk + (i * BQ) % bk
    grad_ref[pl.ds(pl.multiple_of(mine, BQ), BQ), 0:w] = (dq[...] * 0.125).astype(bf16)

    @pl.when(i == n // BQ - 1)
    def _():
        grad_ref[:, w : 2 * w] = dk[...].astype(bf16)
        grad_ref[:, 2 * w : 3 * w] = dv[...].astype(bf16)
        place = lax.broadcasted_iota(jnp.int32, (1, 3 * w), 1)
        gains = jnp.zeros((1, 3 * w), f32)
        for h in range(nh):
            gains = jnp.where(place == h, jnp.sum(gacc[h * HEAD : (h + 1) * HEAD, :]), gains)
        sums_ref[...] = jnp.zeros_like(sums_ref)
        sums_ref[0:1, :] = jnp.sum(grad_ref[...].astype(f32), axis=0, keepdims=True)
        sums_ref[1:2, :] = gains


def attend_backward(hd, part, tab, spans, qkv, keep, head_scale, scaled_grad, o_t, lse, deps=()):
    n, nh, w = qkv.shape[0], hd.nh, hd.nh * HEAD
    bk = n // hd.parts
    return pl.pallas_call(
        skipping(functools.partial(bwd_kernel, hd, bk), 10, len(deps)),
        grid_spec=pltpu.PrefetchScalarGridSpec(
            num_scalar_prefetch=2,
            grid=(n // BQ,),
            in_specs=head_specs(hd, n, w, bk)
            + [
                pl.BlockSpec((8, n), lambda i, t, s: (0, 0)),
                pl.BlockSpec(memory_space=pltpu.SMEM),
                pl.BlockSpec((BQ, w), lambda i, t, s: (i, part)),
                pl.BlockSpec((w, BQ), lambda i, t, s: (0, i)),
                pl.BlockSpec((8, BQ), lambda i, t, s: (0, i)),
            ]
            + unread(deps),
            out_specs=[
                pl.BlockSpec((n, 3 * w), lambda i, t, s: (0, 0)),
                pl.BlockSpec((8, 3 * w), lambda i, t, s: (0, 0)),
            ],
            scratch_shapes=[
                pltpu.VMEM((n, 1), jnp.int32),
                pltpu.VMEM((n, w), f32),
                pltpu.VMEM((n, w), f32),
                pltpu.VMEM((BQ, w), f32),
                pltpu.VMEM((w, BQ), f32),
                pltpu.VMEM((nh, n, w), bf16),
            ],
        ),
        out_shape=[
            jax.ShapeDtypeStruct((n, 3 * w), bf16),
            jax.ShapeDtypeStruct((8, 3 * w), f32),
        ],
        compiler_params=pltpu.CompilerParams(vmem_limit_bytes=60 << 20),
        cost_estimate=pl.CostEstimate(flops=nh * n * n * HEAD * 50, bytes_accessed=1024, transcendentals=0),
        name="attend_backward",
    )(tab, spans, qkv, qkv, qkv, keep, head_scale[None], scaled_grad, o_t, lse, *deps)


def swap(x, axis, bits):
    return lax.ppermute(x, axis, [(i, i ^ bits) for i in range(lax.axis_size(axis))])


def reorder(x, idx, width):
    rows, cols = x.shape
    return jnp.take(x.reshape(rows, cols // width, width), idx, axis=1).reshape(rows, cols)


def reorder_rows(x, idx, height):
    rows, cols = x.shape
    return jnp.take(x.reshape(rows // height, height, cols), idx, axis=0).reshape(rows, cols)


class Grid:
    def __init__(self, dp, sp):
        self.dp, self.sp = dp, sp
        self.nx = max(sp // 2, 1)
        self.ny = self.nx if dp % self.nx == 0 else 1
        self.nz = dp // self.ny
        self.z_bits = [self.ny * k for k in range(1, self.nz)]
        self.y_bits = list(range(1, self.ny))
        self.x_bits = [2 * k for k in range(1, self.nx)]

    def gather_z(self, w):
        return jnp.concatenate([w] + [swap(w, "dp", b) for b in self.z_bits], axis=0)

    def gather_y(self, w):
        return jnp.concatenate([w] + [swap(w, "dp", b) for b in self.y_bits], axis=0)

    def gather(self, w):
        half = w.shape[1] // 2
        rows = self.gather_z(w)
        first, other = rows[:, :half], rows[:, half:]
        first = self.gather_y(first)
        firsts = [first] + [swap(first, "sp", b) for b in self.x_bits]
        other = jnp.concatenate([other] + [swap(other, "sp", b) for b in self.x_bits], axis=1)
        other = self.gather_y(other)
        parts = []
        for k in range(self.nx):
            parts += [firsts[k], other[:, k * half : (k + 1) * half]]
        return jnp.concatenate(parts, axis=1)

    def fold(self, parts, axis, bits):
        total = parts[0].astype(f32)
        for part, b in zip(parts[1:], bits, strict=True):
            total = total + swap(part.astype(bf16), axis, b).astype(f32)
        return total

    def scatter_y(self, g):
        rows = g.shape[0] // self.ny
        return self.fold([g[k * rows : (k + 1) * rows] for k in range(self.ny)], "dp", self.y_bits)

    def scatter_z(self, g):
        rows = g.shape[0] // self.nz
        return self.fold([g[k * rows : (k + 1) * rows] for k in range(self.nz)], "dp", self.z_bits)

    def scatter_x(self, g):
        cols = g.shape[1] // self.nx
        return self.fold([g[:, k * cols : (k + 1) * cols] for k in range(self.nx)], "sp", self.x_bits)

    def scatter(self, g):
        cols = g.shape[1] // self.nx
        half = cols // 2
        first = jnp.concatenate([g[:, k * cols : k * cols + half] for k in range(self.nx)], axis=1)
        other = jnp.concatenate([g[:, k * cols + half : (k + 1) * cols] for k in range(self.nx)], axis=1)
        first = self.scatter_y(self.scatter_x(first))
        other = self.scatter_x(self.scatter_y(other))
        return self.scatter_z(jnp.concatenate([first, other], axis=1))

    def all_sum(self, v):
        for axis in ("sp", "dp"):
            bit = 1
            while bit < lax.axis_size(axis):
                v = v + swap(v, axis, bit)
                bit *= 2
        return v


def norm_forward(halves, gains, shifts):
    width = sum(h.shape[1] for h in halves)
    mean = sum(jnp.sum(h, axis=1, keepdims=True) for h in halves) / width
    centred = [h - mean for h in halves]
    inv_std = lax.rsqrt(sum(jnp.sum(c * c, axis=1, keepdims=True) for c in centred) / width + EPSILON)
    normed = [c * inv_std for c in centred]
    return [n * a + b for n, a, b in zip(normed, gains, shifts)], normed, inv_std


def norm_backward(incoming, normed, inv_std, gains):
    width = sum(h.shape[1] for h in incoming)
    scaled = [e * a for e, a in zip(incoming, gains)]
    mean = sum(jnp.sum(s, axis=1, keepdims=True) for s in scaled) / width
    along = sum(jnp.sum(s * n, axis=1, keepdims=True) for s, n in zip(scaled, normed)) / width
    grads = [inv_std * (s - mean - n * along) for s, n in zip(scaled, normed)]
    gain_sums = [jnp.sum(e * n, axis=0) for e, n in zip(incoming, normed)]
    return grads, gain_sums, [jnp.sum(e, axis=0) for e in incoming]


def general_layer(
    tokens,
    seq_spans,
    valid_mask,
    cotangent,
    w_qkv,
    w_out,
    w_up,
    w_down,
    model_gains,
    model_shifts,
    mid_gain,
    hidden_shifts,
    head_scale,
):
    dp, sp = lax.axis_size("dp"), lax.axis_size("sp")
    grid = Grid(dp, sp)
    nx, ny, nz = grid.nx, grid.ny, grid.nz
    me_d, me_s = lax.axis_index("dp"), lax.axis_index("sp")
    rows, width = tokens.shape
    group = rows * sp
    heads = head_scale.shape[0]
    nh = heads // sp
    lw = nh * HEAD
    block = width // dp
    ff = mid_gain.shape[0]

    place = jnp.arange(dp, dtype=jnp.int32)
    to_rel = ((place % nz) * ny + place // nz) ^ me_d
    away = place ^ me_d
    to_abs = (away % ny) * nz + away // ny
    sp_place = jnp.arange(sp, dtype=jnp.int32)
    sp_rel = ((sp_place % nx) * 2 + sp_place // nx) ^ me_s
    sp_away = sp_place ^ me_s
    sp_abs = (sp_away % 2) * nx + sp_away // 2

    pad_rows = 16
    valid_rows = rows // lw
    blocks = w_qkv.reshape(block, 3, lw).transpose(1, 0, 2)
    blocks = jnp.concatenate([blocks, jnp.zeros((sp - 3, block, lw), bf16)], axis=0)
    turned = jnp.concatenate(
        [lax.dynamic_slice_in_dim(blocks, (t - 3 * me_s) % sp, 1, 0) for t in range(sp)], axis=0
    )
    flag_rows = jnp.concatenate(
        [valid_mask.astype(bf16).reshape(valid_rows, lw), jnp.zeros((pad_rows - valid_rows, lw), bf16)], axis=0
    )
    sent = jnp.concatenate([turned, jnp.broadcast_to(flag_rows[None], (sp, pad_rows, lw))], axis=1)
    got = lax.all_to_all(sent, "sp", 0, 0, tiled=True)
    keep = got[:, block : block + valid_rows].reshape(group) > 0.5
    wq_shard = jnp.concatenate(
        [lax.dynamic_slice_in_dim(got, (t * sp + me_s) // 3, 1, 0)[0, :block] for t in range(3)], axis=1
    )
    wq = grid.gather_y(grid.gather_z(wq_shard))

    gains = reorder(model_gains, to_rel, block)
    shifts = reorder(model_shifts, to_rel, block)
    stream = reorder(tokens, to_rel, block).astype(f32)
    upstream = reorder(cotangent, to_rel, block) * valid_mask.astype(bf16)[:, None]
    (first_out,), (first_normed,), first_std = norm_forward([stream], gains[0:1], shifts[3:4])
    first = first_out.astype(bf16)

    crossed = [first] + [swap(first, "sp", b) for b in grid.x_bits]
    firsts = []
    for piece in crossed:
        firsts += [piece, swap(piece, "sp", 1)]
    piece_bits = [b for k in [0] + grid.x_bits for b in (k, k + 1)]
    qkv_shift = jnp.concatenate(
        [
            lax.dynamic_slice_in_dim(model_shifts[0], me_s * lw, lw, 0),
            jnp.zeros((lw,), f32),
            lax.dynamic_slice_in_dim(model_shifts[1], me_s * lw, lw, 0),
        ]
    )
    firsts_cat = jnp.concatenate(firsts, axis=0)
    qkv_rel = (mm(firsts_cat, wq) + qkv_shift).astype(bf16)
    group_order = sp_place ^ me_s
    qkv = reorder_rows(qkv_rel, group_order, rows)

    low_down = jnp.concatenate([w_out, w_down], axis=1)
    od_own = grid.gather(low_down)
    up_own = grid.gather(w_up)
    oc, dc = w_out.shape[1], w_down.shape[1]
    out_own = jnp.concatenate([od_own[:, k * (oc + dc) : k * (oc + dc) + oc] for k in range(nx)], axis=1)
    down_own = jnp.concatenate([od_own[:, k * (oc + dc) + oc : (k + 1) * (oc + dc)] for k in range(nx)], axis=1)
    wos = jnp.concatenate([out_own, swap(out_own, "sp", 1)], axis=1)
    downs = [down_own, swap(down_own, "sp", 1)]
    ups = [up_own, swap(up_own, "sp", 1)]
    wo = reorder(reorder_rows(wos, to_abs, block), sp_abs, oc)

    tab = jnp.concatenate([sp_place, me_s[None].astype(jnp.int32)])
    hd = Heads(nh, nh, 0, (0, 1, 2), 0, sp, sp)
    keep_col = jnp.broadcast_to(keep.astype(f32)[None, :], (8, group))
    scaled, o_t, lse = attend_forward(hd, tab, seq_spans[0], qkv, keep_col, head_scale)
    returned = lax.all_to_all(scaled.reshape(sp, rows, lw), "sp", 0, 0, tiled=True)
    merged = jnp.concatenate([returned[t] for t in range(sp)], axis=1)

    attn_pre = reorder(mm(merged, wo) + model_shifts[2], to_rel, block)
    (attn_out,), (attn_normed,), attn_std = norm_forward([attn_pre], gains[1:2], shifts[4:5])
    middle = stream + attn_out
    (second_out,), (second_normed,), second_std = norm_forward([middle], gains[2:3], shifts[5:6])
    second = second_out.astype(bf16)

    ff_half = ff // 2
    hidden_vectors = reorder(
        jnp.concatenate([mid_gain[None], hidden_shifts], axis=0), sp_rel, ff // sp
    )
    split = lambda v: [v[:, :ff_half], v[:, ff_half:]]
    hg, hb, hs = split(hidden_vectors[0:1]), split(hidden_vectors[1:2]), split(hidden_vectors[2:3])
    pre = [mm(second, w) + b for w, b in zip(ups, hb)]
    activated, pulls = zip(*[jax.vjp(jax.nn.gelu, p) for p in pre])
    hidden_out, hidden_normed, hidden_std = norm_forward(activated, hg, hs)
    hidden = [h.astype(bf16) for h in hidden_out]
    out_rel = middle + mm_cols(hidden[0], downs[0]) + mm_cols(hidden[1], downs[1]) + shifts[6:7]
    layer_out = reorder(out_rel.astype(bf16), to_abs, block)

    pair = lambda x: jnp.concatenate([x, swap(x, "sp", 1)], axis=0)
    across = lambda halves: jnp.concatenate([halves[0], swap(halves[1], "sp", 1)], axis=0)
    upstream_pair = pair(upstream)
    g_down = mm_rows(upstream_pair, across(hidden)).astype(bf16)
    grad_w_down = grid.scatter(g_down)

    hidden_grad = [mm(upstream, w) for w in downs]
    act_grad, grad_mid, grad_mid_shift = norm_backward(hidden_grad, hidden_normed, hidden_std, hg)
    pre_grad = [pull(a)[0].astype(bf16) for pull, a in zip(pulls, act_grad)]
    second_grad = mm_cols(pre_grad[0], ups[0]) + mm_cols(pre_grad[1], ups[1])
    (middle_part,), (gain_ffn,), (shift_ffn,) = norm_backward([second_grad], [second_normed], second_std, gains[2:3])
    middle_grad = upstream.astype(f32) + middle_part
    (attn_grad_full,), (gain_attn,), (shift_attn,) = norm_backward([middle_grad], [attn_normed], attn_std, gains[1:2])
    attn_grad_rel = attn_grad_full.astype(bf16)
    attn_grad = reorder(attn_grad_rel, to_abs, block)
    merged_grad = mm_cols(attn_grad, wo).astype(bf16)
    scattered = jnp.stack([merged_grad[:, t * lw : (t + 1) * lw] for t in range(sp)], axis=0)
    scaled_grad = lax.all_to_all(scattered, "sp", 0, 0, tiled=True).reshape(group, lw)

    g_up = mm_rows(pair(second), across(pre_grad)).astype(bf16)
    grad_w_up = grid.scatter(g_up)
    merged_rel = reorder(merged, to_rel, block)
    attn_grad_cols = reorder(attn_grad, sp_rel, oc)
    g_out = mm_rows(pair(merged_rel), across([attn_grad_cols[:, : width // 2], attn_grad_cols[:, width // 2 :]]))
    grad_w_out = grid.scatter_z(grid.scatter_y(grid.scatter_x(g_out)))

    qkv_grad, head_sums = attend_backward(
        hd, 0, tab, seq_spans[0], qkv, keep_col, head_scale, scaled_grad, o_t, lse
    )
    qkv_grad_rel = reorder_rows(qkv_grad, group_order, rows)
    first_part = mm_cols(qkv_grad_rel, wq)
    pieces = [first_part[t * rows : (t + 1) * rows] for t in range(sp)]
    folded = [
        pieces[t].astype(f32) + swap(pieces[t + 1].astype(bf16), "sp", 1).astype(f32) for t in range(0, sp, 2)
    ]
    first_grad = grid.fold(folded, "sp", grid.x_bits)
    (input_part,), (gain_in,), (shift_in,) = norm_backward([first_grad], [first_normed], first_std, gains[0:1])
    grad_tokens = reorder(middle_grad + input_part, to_abs, block)

    g_qkv = mm_rows(firsts_cat, qkv_grad_rel)
    g_mine = grid.scatter_z(grid.scatter_y(g_qkv)).astype(bf16)
    g_blocks = jnp.concatenate(
        [g_mine.reshape(block, 3, lw).transpose(1, 0, 2), jnp.zeros((1, block, lw), bf16)], axis=0
    )
    back = []
    for t in range(sp):
        which = jnp.int32(3)
        for u in range(3):
            which = jnp.where((u * sp + me_s) // 3 == t, u, which)
        back.append(lax.dynamic_slice_in_dim(g_blocks, which, 1, 0))
    home = lax.all_to_all(jnp.concatenate(back, axis=0), "sp", 0, 0, tiled=True)
    grad_w_qkv = jnp.concatenate(
        [lax.dynamic_slice_in_dim(home, (3 * me_s + u) % sp, 1, 0)[0] for u in range(3)], axis=1
    ).astype(f32)

    qkv_sums = jnp.sum(qkv_grad.astype(f32), axis=0)
    zeros = jnp.zeros((2, width), f32)
    bias_sums = lax.dynamic_update_slice(
        zeros, jnp.stack([qkv_sums[:lw], qkv_sums[2 * lw :]]), (0, me_s * lw)
    )
    sum_early = jnp.concatenate(
        [
            reorder(
                jnp.stack(
                    [
                        gain_attn,
                        gain_ffn,
                        jnp.sum(attn_grad_rel.astype(f32), axis=0),
                        shift_attn,
                        shift_ffn,
                        jnp.sum(upstream.astype(f32), axis=0),
                    ]
                ),
                to_abs,
                block,
            ),
            reorder(
                jnp.stack(
                    [
                        jnp.concatenate(grad_mid),
                        jnp.concatenate([jnp.sum(p.astype(f32), axis=0) for p in pre_grad]),
                        jnp.concatenate(grad_mid_shift),
                    ]
                ),
                sp_abs,
                ff // sp,
            ).reshape(3 * ff // width, width),
        ],
        axis=0,
    )
    early = grid.all_sum(sum_early)
    scale_row = lax.dynamic_update_slice(
        jnp.zeros((1, width), f32), head_sums[1:2, :nh], (0, me_s * nh)
    )
    late = grid.all_sum(
        jnp.concatenate(
            [reorder(jnp.stack([gain_in, shift_in]), to_abs, block), bias_sums, scale_row], axis=0
        )
    )
    grad_model_gains = jnp.stack([late[0], early[0], early[1]])
    grad_model_shifts = jnp.stack([late[2], late[3], early[2], late[1], early[3], early[4], early[5]])
    hidden_sums = early[6:].reshape(3, ff)
    return (
        layer_out,
        grad_tokens,
        grad_w_qkv,
        grad_w_out,
        grad_w_up,
        grad_w_down,
        grad_model_gains,
        grad_model_shifts,
        hidden_sums[0],
        hidden_sums[1:3],
        late[4, :heads],
    )


REL, HID, ORD, COLS, WHO, SEND, SLOT, ALONG = 0, 8, 16, 24, 32, 33, 36, 40
LANES = 128


def matchings(sp):
    left = {s: {3 * s + k: (3 * s + k) % sp for k in range(3)} for s in range(sp)}
    rounds = []
    for _ in range(3):
        taken = {}

        def seat(s, seen):
            for b, to in sorted(left[s].items(), key=lambda e: e[1] != s):
                if to not in seen:
                    seen.add(to)
                    if to not in taken or seat(taken[to][0], seen):
                        taken[to] = (s, b)
                        return True
            return False

        for s in range(sp):
            seat(s, set())
        one = [None] * sp
        for to, (s, b) in taken.items():
            one[s] = (b - 3 * s, b // sp, to)
            del left[s][b]
        rounds.append(one)
    return rounds


def tables(dp, sp, ny, nz, rounds):
    out = np.zeros((dp * sp, 128), np.int32)
    for d in range(dp):
        for s in range(sp):
            row = out[d * sp + s]
            where = {}
            for p in range(dp):
                row[REL + p] = ((p % nz) * ny + p // nz) ^ d
                where[row[REL + p]] = p
            for q in range(2 * sp):
                dc, half, dx = q // 4, q // 2 % 2, q % 2
                row[HID + q] = ((dx * 2 + dc) ^ s) * 2 + half
                row[COLS + q] = where[row[HID + q]]
            for t in range(sp):
                row[ORD + t] = s ^ t
            row[WHO] = s
            for k in range(nz):
                row[ALONG + k] = d // ny ^ k
            for m in range(3):
                row[SEND + m] = rounds[m][s][0]
                row[SLOT + m] = next(rounds[m][a][1] for a in range(sp) if rounds[m][a][2] == s)
    return out


def span(index, size):
    return pl.ds(pl.multiple_of(index * size, size), size)


def norm_of(x):
    mean = jnp.mean(x, axis=1, keepdims=True)
    centred = x - mean
    inv_std = lax.rsqrt(jnp.mean(centred * centred, axis=1, keepdims=True) + EPSILON)
    return centred * inv_std, inv_std


def norm_back(incoming, normed, inv_std, gain):
    scaled = incoming * gain
    mean = jnp.mean(scaled, axis=1, keepdims=True)
    along = jnp.mean(scaled * normed, axis=1, keepdims=True)
    return inv_std * (scaled - mean - normed * along)


def down_sum(x):
    return jnp.sum(x, axis=0, keepdims=True)


def whole(shape):
    return pl.BlockSpec(shape, lambda *_: (0,) * len(shape))


def by_rows(rows, cols):
    return pl.BlockSpec((rows, cols), lambda i, *_: (i, 0))


class Order:
    last = ()

    def after(self, deps):
        return tuple(deps) + self.last

    def passed(self, outs):
        self.last = (outs[-1],)
        return outs


ORDER = Order()


def with_rider(body, at, count):
    def both(*refs):
        first, second, total = refs[at], refs[at + 1], refs[at + 2 + count]

        @pl.when(pl.program_id(0) == 0)
        def _():
            total[...] = first[...] + second[...]

        body(*refs[:at], *refs[at + 2 : at + 2 + count], *refs[at + 3 + count :])

    return both


def call(name, body, tab, args, outs, steps=1, in_specs=None, out_specs=None, scratch=(), deps=(), vmem=20, us=0, rider=None):
    in_specs = [whole(a.shape) for a in args] if in_specs is None else in_specs
    out_specs = [whole(s) for s, _ in outs] if out_specs is None else out_specs
    if rider is not None:
        body = with_rider(body, 1 + len(args), len(outs))
        args, outs = list(args) + list(rider), list(outs) + [(rider[0].shape, rider[0].dtype)]
        in_specs = list(in_specs) + [whole(rider[0].shape)] * 2
        out_specs = list(out_specs) + [whole(rider[0].shape)]
    deps = ORDER.after(deps)
    made = pl.pallas_call(
        skipping(body, 1 + len(args), len(deps)),
        grid_spec=pltpu.PrefetchScalarGridSpec(
            num_scalar_prefetch=1,
            grid=(steps,),
            in_specs=list(in_specs) + unread(deps),
            out_specs=list(out_specs),
            scratch_shapes=list(scratch),
        ),
        out_shape=[jax.ShapeDtypeStruct(s, t) for s, t in outs],
        compiler_params=pltpu.CompilerParams(vmem_limit_bytes=vmem << 20),
        cost_estimate=pl.CostEstimate(flops=int(us * 1.1e9) + 1024, bytes_accessed=1024, transcendentals=0),
        name=name,
    )(tab, *args, *deps)
    return ORDER.passed(made)


def part_body(tab, w, *outs):
    width = outs[0].shape[1]
    for m, out in enumerate(outs):
        out[...] = w[:, span(tab[SEND + m], width)]


def join_body(tab, *refs):
    pieces, out = refs[:-1], refs[-1]
    for m, piece in enumerate(pieces):
        for k in range(out.shape[0]):
            out[k, :, span(tab[SLOT + m], piece.shape[1])] = piece[...]


def home_body(tab, *refs):
    pieces, out = refs[:-1], refs[-1]
    width = pieces[0].shape[1]
    for m, piece in enumerate(pieces):
        out[:, span(tab[SEND + m], width)] = piece[...].astype(f32)


def prologue_body(tab, tok, cot, vcol, vrow, gains, shifts, mid, hsh, first_ref, both_ref, up_ref, tokr_ref, vec_ref, hid_ref):
    rows, width = tok.shape
    unit = mid.shape[1] // 8
    valid = vcol[...]
    vec_ref[...] = jnp.zeros_like(vec_ref)
    hid_ref[...] = jnp.zeros_like(hid_ref)
    for p in range(8):
        at, to = span(tab[REL + p], LANES), slice(p * LANES, (p + 1) * LANES)
        tokr_ref[:, to] = tok[:, at]
        vec_ref[0:3, to] = gains[:, at]
        vec_ref[3:10, to] = shifts[:, at]
        at, to = span(tab[HID + p], unit), slice(p * unit, (p + 1) * unit)
        hid_ref[0:1, to] = mid[:, at]
        hid_ref[1:3, to] = hsh[:, at]
    gain, shift = vec_ref[0:1, :], vec_ref[6:7, :]

    def chunk(i, carry):
        at = span(i, 64)
        normed, _ = norm_of(tokr_ref[at, :].astype(f32))
        first_ref[at, :] = (normed * gain + shift).astype(bf16)
        return carry

    lax.fori_loop(0, rows // 64, chunk, 0)
    first_ref[rows:, :] = jnp.broadcast_to(vrow[...], (16, width))
    both_ref[: rows + 16, :] = first_ref[...]
    for p in range(8):
        at, to = span(tab[REL + p], LANES), slice(p * LANES, (p + 1) * LANES)
        masked = cot[:, at].astype(f32) * valid
        up_ref[:, to] = masked.astype(bf16)
        vec_ref[10:11, to] = down_sum(masked)
    both_ref[rows + 16 :, :] = up_ref[...]


def project_body(count, tab, *refs):
    pieces, (w0, w1, shifts, out_ref, keep_ref) = refs[:count], refs[count:]
    rows, depth = out_ref.shape[0], w0.shape[0]
    at = span(tab[WHO], 2 * LANES)
    bias = jnp.concatenate([shifts[0:1, at], jnp.zeros((1, 2 * LANES), f32), shifts[1:2, at]], axis=1)
    for k in range(count):

        @pl.when(pl.program_id(0) == k)
        def _():
            x = pieces[k]
            out_ref[...] = (mm(x[:rows, :depth], w0[...]) + mm(x[:rows, depth:], w1[...]) + bias).astype(bf16)
            keep_ref[...] = x[rows : rows + 16, :rows].astype(f32)[:8]


def middle_body(begin, tab, ret, tok, vec, shards, pair_ref, mid_ref, norm_ref, std_ref, wo, sems):
    width = tok.shape[1]

    def copies(p):
        out = []
        for q in range(8):
            at = tab[HID + q]
            source = shards.at[tab[REL + p] * 4 + at // 2, :, pl.ds(pl.multiple_of(begin + lax.rem(at, 2) * LANES, LANES), LANES)]
            out.append(pltpu.make_async_copy(source, wo.at[pl.ds(p * LANES, LANES), span(tab[COLS + q], LANES)], sems.at[p, q]))
        return out

    @pl.when(pl.program_id(0) == 0)
    def _():
        for p in range(8):
            for copy in copies(p):
                copy.start()

    for p in range(8):
        a = tab[REL + p]
        pair_ref[:, width + p * LANES : width + (p + 1) * LANES] = ret[a // 2, :, span(lax.rem(a, 2), LANES)]

    @pl.when(pl.program_id(0) == 0)
    def _():
        for p in range(8):
            for copy in copies(p):
                copy.wait()

    normed, inv_std = norm_of(mm(pair_ref[:, width:], wo[...]) + vec[5:6, :])
    middle = tok[...].astype(f32) + (normed * vec[1:2, :] + vec[7:8, :])
    norm_ref[...] = normed
    std_ref[...] = inv_std
    mid_ref[...] = middle
    again, _ = norm_of(middle)
    pair_ref[:, :width] = (again * vec[2:3, :] + vec[8:9, :]).astype(bf16)


GELU = 0.7978845608028654
CUBE = 0.044715


def ffn_body(unit, tab, second, upstream, mid, hid, vec, *refs):
    shards, (hown, hsib, pown, psib, sg_ref, lo_ref, sums_ref, upv, dnv, act, slope, back, sems) = refs[0], refs[1:]
    i = pl.program_id(0)
    ff = upv.shape[1]

    def copies(q, which):
        held = (upv, dnv)[which]
        at = tab[HID + q]
        from_cols = pl.ds(pl.multiple_of(which * 2 * unit + lax.rem(at, 2) * unit, unit), unit)
        out = []
        for p in range(8):
            source = shards.at[tab[REL + p] * 4 + at // 2, :, from_cols]
            out.append(pltpu.make_async_copy(source, held.at[pl.ds(p * LANES, LANES), pl.ds(q * unit, unit)], sems.at[which, q, p]))
        return out

    @pl.when(i == 0)
    def _():
        sums_ref[...] = jnp.zeros_like(sums_ref)
        for q in range(8):
            for copy in copies(q, 0):
                copy.start()
        for q in range(8):
            for copy in copies(q, 1):
                copy.start()

    x = second[...]
    total = jnp.zeros((x.shape[0], 1), f32)
    for q in range(8):
        at = slice(q * unit, (q + 1) * unit)

        @pl.when(i == 0)
        def _():
            for copy in copies(q, 0):
                copy.wait()

        pre = mm(x, upv[:, at]) + hid[1:2, at]
        squared = pre * pre
        t = jnp.tanh(pre * (GELU + (GELU * CUBE) * squared))
        one = 0.5 + 0.5 * t
        value = pre * one
        act[:, at] = value
        slope[:, at] = one + 0.5 * pre * (1.0 - t * t) * (GELU + (3 * GELU * CUBE) * squared)
        total = total + jnp.sum(value, axis=1, keepdims=True)
    mean = total / ff
    total = jnp.zeros_like(mean)
    for q in range(8):
        at = slice(q * unit, (q + 1) * unit)
        centred = act[:, at] - mean
        total = total + jnp.sum(centred * centred, axis=1, keepdims=True)
    inv_std = lax.rsqrt(total / ff + EPSILON)
    u = upstream[...]
    m1, m2 = jnp.zeros_like(mean), jnp.zeros_like(mean)
    low = jnp.zeros(mid.shape, f32)
    for q in range(8):
        at = slice(q * unit, (q + 1) * unit)

        @pl.when(i == 0)
        def _():
            for copy in copies(q, 1):
                copy.wait()

        incoming = mm(u, dnv[:, at])
        normed = (act[:, at] - mean) * inv_std
        act[:, at] = normed
        gain = hid[0:1, at]
        held, to = ((hown, at) if q < 4 else (hsib, slice((q - 4) * unit, (q - 3) * unit)))
        hidden = (normed * gain + hid[2:3, at]).astype(bf16)
        held[:, to] = hidden
        low = low + mm_cols(hidden, dnv[:, at])
        along = incoming * normed
        sums_ref[0:1, at] += down_sum(along)
        sums_ref[2:3, at] += down_sum(incoming)
        m1 = m1 + jnp.sum(incoming * gain, axis=1, keepdims=True)
        m2 = m2 + jnp.sum(along * gain, axis=1, keepdims=True)
        back[:, at] = incoming
    m1, m2 = m1 / ff, m2 / ff
    second_grad = jnp.zeros(mid.shape, f32)
    for q in range(8):
        at = slice(q * unit, (q + 1) * unit)
        grad = inv_std * (back[:, at] * hid[0:1, at] - m1 - act[:, at] * m2)
        pre_grad = (grad * slope[:, at]).astype(bf16)
        held, to = ((pown, at) if q < 4 else (psib, slice((q - 4) * unit, (q - 3) * unit)))
        held[:, to] = pre_grad
        sums_ref[1:2, at] += down_sum(pre_grad.astype(f32))
        second_grad = second_grad + mm_cols(pre_grad, upv[:, at])
    sg_ref[...] = second_grad
    out = (mid[...] + low + vec[9:10, :]).astype(bf16)
    for p in range(8):
        lo_ref[:, span(tab[REL + p], LANES)] = out[:, p * LANES : (p + 1) * LANES]


def heads_body(tab, grad, mid, norm, std, up, vec, wo, mg_ref, own_ref, sib_ref, out_ref, sums_ref, scr):
    @pl.when(pl.program_id(0) == 0)
    def _():
        sums_ref[...] = jnp.zeros_like(sums_ref)

    incoming = grad[...]
    again, inv_std = norm_of(mid[...])
    sums_ref[1:2, :] += down_sum(incoming * again)
    sums_ref[4:5, :] += down_sum(incoming)
    middle_grad = up[...].astype(f32) + norm_back(incoming, again, inv_std, vec[2:3, :])
    mg_ref[...] = middle_grad
    normed = norm[...]
    sums_ref[0:1, :] += down_sum(middle_grad * normed)
    sums_ref[3:4, :] += down_sum(middle_grad)
    low = norm_back(middle_grad, normed, std[...], vec[1:2, :]).astype(bf16)
    sums_ref[2:3, :] += down_sum(low.astype(f32))
    scr[...] = low
    for q in range(8):
        held = own_ref if q < 4 else sib_ref
        held[:, (q % 4) * LANES : (q % 4 + 1) * LANES] = scr[:, span(tab[COLS + q], LANES)]
    got = mm_cols(low, wo[...]).astype(bf16)
    for p in range(8):
        a = tab[REL + p]
        out_ref[a // 2, :, span(lax.rem(a, 2), LANES)] = got[:, p * LANES : (p + 1) * LANES]


def turn_body(tab, x0, x1, out):
    tokens = x0.shape[0]
    out[:, :tokens] = x0[...].T
    out[:, tokens:] = x1[...].T


def turn_late_body(tab, x0, both, out):
    tokens = x0.shape[0]
    out[:, :tokens] = x0[...].T
    out[:, tokens:] = both[tokens + 16 :, :].T


def grads_body(counts, widths, tab, *refs):
    ins, (ak, asend, bk, bsend, xt) = refs[:-5], refs[-5:]
    half = bk.shape[0]
    total = sum(widths)
    i = pl.program_id(0)
    at = begin = 0
    for n, (count, wide) in enumerate(zip(counts, widths)):
        xs, (y0, y1) = ins[begin : begin + count], ins[begin + count : begin + count + 2]
        begin += count + 2
        if count == 2:

            @pl.when(i == 4 * n)
            def _():
                turn_body(tab, *xs, xt)

        left = xt if count == 2 else xs[0]
        for q in range(4):

            @pl.when(i == 4 * n + q)
            def _():
                g = mm(left[...], jnp.concatenate([y0[...], y1[...]], axis=0)).astype(bf16)
                if q < 2:
                    (ak, asend)[q][:, at : at + wide] = g
                else:
                    to = slice((q - 2) * total + at, (q - 2) * total + at + wide)
                    bk[:, to] = g[:half]
                    bsend[:, to] = g[half:]

        at += wide


def groups_body(count, tab, *refs):
    pieces, (grad, keep, send, acc) = refs[:count], refs[count:]
    i = pl.program_id(0)
    half = keep.shape[0]
    rows = grad.shape[0]
    for k in range(count):

        @pl.when(i == k)
        def _():
            got = mm(pieces[k][:rows, :].T, grad[...])
            acc[...] = got if k == 0 else acc[...] + got

    @pl.when(i == count - 1)
    def _():
        keep[...] = acc[:half]
        send[...] = acc[half:].astype(bf16)


def fold_body(tab, ak, ra, bk, rb, x0, x1, a2k, a2s, b2k, b2s, y0, y1):
    y0[...] = x0[...]
    y1[...] = x1[...]
    rows, cols = b2k.shape
    a = ak[...].astype(f32) + ra[...].astype(f32)
    a2k[...] = a[:rows].astype(bf16)
    a2s[...] = a[rows:].astype(bf16)
    b = bk[...].astype(f32) + rb[...].astype(f32)
    b2k[...] = b[:, :cols].astype(bf16)
    b2s[...] = b[:, cols:].astype(bf16)


def spread_body(tab, ak, ra, bk, rb, g, r, keep, *sends):
    rows, cols = keep.shape[0], ak.shape[1]
    at = 0
    for mine, theirs in ((ak, ra), (bk, rb), (g, r)):
        total = mine[...].astype(f32) + theirs[...].astype(f32)
        to = slice(at, at + total.shape[1])
        at += total.shape[1]
        keep[:, to] = total[:rows]
        for n, send in enumerate(sends, 1):
            send[:, to] = total[n * rows : (n + 1) * rows].astype(bf16)


def gathered_body(widths, tab, keep, r1, r2, r3, *refs):
    outs, pieces, total = refs[: len(widths)], refs[len(widths) : -1], refs[-1]
    total[...] = keep[...] + r1[...].astype(f32) + r2[...].astype(f32) + r3[...].astype(f32)
    half = sum(widths)
    at = 0
    for out, wide in zip(outs, widths):
        out[:, :wide] = total[:, at : at + wide]
        out[:, wide:] = total[:, half + at : half + at + wide]
        at += wide
    for m, piece in enumerate(pieces):
        size = piece.shape[1]
        piece[...] = total[:, pl.ds(pl.multiple_of(2 * half + tab[SLOT + m] * size, size), size)].astype(bf16)


def spill_body(unit, tab, xt, own, sib, out):
    tokens, width = own.shape[0], xt.shape[0]
    for half, y in enumerate((own, sib)):

        @pl.when(pl.program_id(0) // 4 == half)
        def _():
            g = mm(xt[:, :tokens], y[...]).astype(bf16)
            at = tab[HID + pl.program_id(0)]
            for p in range(8):
                out[tab[REL + p] * 4 + at // 2, :, span(lax.rem(at, 2), unit)] = g[p * LANES : (p + 1) * LANES]


def scatter_weights(grid, tab, rows, sets, widths, tag, rider=None):
    total = sum(widths)
    args, specs = [], []
    for n, (xs, y0, y1) in enumerate(sets):
        wide = widths[n]
        tokens = y0[0].shape[0]
        for x, part in xs:
            args.append(x)
            specs.append(whole(x.shape) if part is None else pl.BlockSpec((tokens, rows), lambda *_, part=part: (0, part)))
        for y, begin in (y0, y1):
            args.append(y)
            specs.append(pl.BlockSpec((tokens, wide), lambda i, *_, n=n, begin=begin: (0, begin + jnp.clip(i - 4 * n, 0, 3))))
    outs = [((rows, total), bf16)] * 2 + [((rows // 2, 2 * total), bf16)] * 2
    ak, asend, bk, bsend, *carried = call(
        "grads_" + tag, functools.partial(grads_body, [len(xs) for xs, _, _ in sets], widths), tab, args, outs,
        steps=4 * len(sets), in_specs=specs, scratch=[pltpu.VMEM((rows, 2 * tokens), bf16)], vmem=28, us=6 * len(sets), rider=rider,
    )
    ra, rb = swap(asend, "sp", 2), swap(bsend, "dp", 1)
    rider, ships = yield carried
    quarter = [((rows // 2, total), bf16)] * 4 + [(x.shape, x.dtype) for x in ships]
    a2k, a2s, b2k, b2s, *carried = call("fold_" + tag, fold_body, tab, [ak, ra, bk, rb] + ships, quarter, vmem=34, rider=rider)
    ra, rb = swap(a2s, "dp", 1), swap(b2s, "sp", 2)
    deps = yield carried + [ra, rb]
    (g, r), size = deps
    shard = (rows // 8, 2 * total + g.shape[1])
    keep, *sends = call("spread_" + tag, spread_body, tab, [a2k, ra, b2k, rb, g, r], [(shard, f32)] + [(shard, bf16)] * 3)
    received = [swap(x, "dp", b) for x, b in zip(sends, grid.z_bits)]
    rider = yield
    yield call(
        "sum_" + tag, functools.partial(gathered_body, widths), tab, [keep] + received,
        [((rows // 8, 2 * w), f32) for w in widths] + [((rows // 8, size), bf16)] * 3, scratch=[pltpu.VMEM(shard, f32)], rider=rider,
    )


def along_z(grid, x):
    lines = [[y + grid.ny * k for k in range(grid.nz)] for y in range(grid.ny)]
    return lax.all_to_all(x, "dp", 0, 0, tiled=True, axis_index_groups=lines)


def rows_body(tab, got, out):
    rows = got.shape[1]
    for k in range(got.shape[0]):
        out[k * rows : (k + 1) * rows, :] = got[tab[ALONG + k]]


def first_grad_body(tab, g, wy0, wy1, mine, cross, far):
    i = pl.program_id(0)
    got = jnp.concatenate([mm_cols(g[...], wy0[...]), mm_cols(g[...], wy1[...])], axis=1)
    rows = g.shape[0]

    @pl.when(i == 0)
    def _():
        mine[...] = got

    @pl.when(i == 1)
    def _():
        cross[:rows] = got.astype(bf16)

    @pl.when(i == 2)
    def _():
        far[...] = got

    @pl.when(i == 3)
    def _():
        cross[rows:] = got.astype(bf16)


def relay_body(tab, far, theirs, out):
    out[...] = (far[...] + theirs[...].astype(f32)).astype(bf16)


def final_body(tab, mine, theirs, crossed, tok, mg, vec, s0, out_ref, late_ref, acc, note):
    i = pl.program_id(0)
    width = tok.shape[1]

    @pl.when(i == 0)
    def _():
        acc[...] = jnp.zeros_like(acc)

    incoming = mine[...] + theirs[...].astype(f32) + crossed[...].astype(f32)
    normed, inv_std = norm_of(tok[...].astype(f32))
    acc[0:1, :] += down_sum(incoming * normed)
    acc[1:2, :] += down_sum(incoming)
    total = mg[...] + norm_back(incoming, normed, inv_std, vec[0:1, :])
    for p in range(8):
        out_ref[:, span(tab[REL + p], LANES)] = total[:, p * LANES : (p + 1) * LANES]

    @pl.when(i == pl.num_programs(0) - 1)
    def _():
        note[...] = jnp.zeros_like(note)
        for p in range(8):
            cols = slice(p * LANES, (p + 1) * LANES)
            note[pl.ds(tab[REL + p], 1), :] = acc[0:1, cols]
            note[pl.ds(8 + tab[REL + p], 1), :] = acc[1:2, cols]
        for e in range(2):
            note[16 + e : 17 + e, :] = s0[0:1, e * LANES : (e + 1) * LANES]
            note[18 + e : 19 + e, :] = s0[0:1, (4 + e) * LANES : (5 + e) * LANES]
        note[20:21, :] = s0[1:2, :LANES]
        for n in range(late_ref.shape[0]):
            late_ref[n] = note[...]


def totals_body(sp, tab, got, out):
    out[...] = jnp.zeros_like(out)
    count = got.shape[0]
    total = got[0, :16]
    for n in range(1, count):
        total = total + got[n, :16]
    for p in range(8):
        cols = slice(p * LANES, (p + 1) * LANES)
        out[0:1, cols] = total[p : p + 1]
        out[1:2, cols] = total[8 + p : 9 + p]
    heads = jnp.zeros((1, LANES), f32)
    lane = lax.broadcasted_iota(jnp.int32, (1, LANES), 1)
    for s in range(sp):
        mine = got[s, 16:24]
        for n in range(s + sp, count, sp):
            mine = mine + got[n, 16:24]
        for e in range(2):
            cols = slice((2 * s + e) * LANES, (2 * s + e + 1) * LANES)
            out[2:3, cols] = mine[e : e + 1]
            out[3:4, cols] = mine[2 + e : 3 + e]
        for h in range(4):
            value = jnp.sum(jnp.where(lane == h, mine[4:5], 0.0))
            heads = jnp.where(lane == 4 * s + h, value, heads)
    out[4:5, :LANES] = heads


def pack_body(tab, sums, vec, hid, out_ref):
    width, unit = sums.shape[1], hid.shape[1] // 8
    out_ref[...] = jnp.zeros_like(out_ref)
    for p in range(8):
        to, at = span(tab[REL + p], LANES), slice(p * LANES, (p + 1) * LANES)
        out_ref[0:5, to] = sums[0:5, at]
        out_ref[5:6, to] = vec[10:11, at]
    for v in range(3):
        for q in range(8):
            unit_at = tab[HID + q]
            row, col = 6 + 4 * v + unit_at // 2, lax.rem(unit_at, 2)
            out_ref[pl.ds(row, 1), span(col, unit)] = hid[v : v + 1, q * unit : (q + 1) * unit]


def fast_layer(
    tokens,
    seq_spans,
    valid_mask,
    cotangent,
    w_qkv,
    w_out,
    w_up,
    w_down,
    model_gains,
    model_shifts,
    mid_gain,
    hidden_shifts,
    head_scale,
):
    dp, sp = lax.axis_size("dp"), lax.axis_size("sp")
    grid = Grid(dp, sp)
    rows, width = tokens.shape
    group = rows * sp
    heads = head_scale.shape[0]
    block = width // dp
    ff = mid_gain.shape[0]
    unit = ff // 8
    shard_lanes = 2 * LANES
    step = rows // 2

    rounds = matchings(sp)
    device = lax.axis_index("dp") * sp + lax.axis_index("sp")
    tab = lax.dynamic_slice_in_dim(jnp.asarray(tables(dp, sp, grid.ny, grid.nz, rounds)), device, 1, 0)[0]
    spans = seq_spans[0]
    forth = [[(s, rounds[m][s][2]) for s in range(sp)] for m in range(3)]
    back_to = [[(t, s) for s, t in pairs] for pairs in forth]
    carry = lambda x, pairs: x if all(a == b for a, b in pairs) else lax.ppermute(x, "sp", pairs)

    ORDER.last = ()
    shards = lax.all_gather(jnp.concatenate([w_up, w_down, w_out], axis=1), ("dp", "sp"), axis=0)
    sent = call("part", part_body, tab, [w_qkv], [((block, shard_lanes), bf16)] * 3)
    moved = [carry(x, pairs) for x, pairs in zip(sent, forth)]
    wq_lines = along_z(grid, call("join", join_body, tab, moved, [((grid.nz, block, 3 * shard_lanes), bf16)])[0])
    vcol = valid_mask.astype(f32)[:, None]
    vrow = jnp.pad(valid_mask.astype(bf16), (0, width - rows))[None]
    first, both, upstream, tokr, vec, hid = call(
        "prologue", prologue_body, tab,
        [tokens, cotangent, vcol, vrow, model_gains, model_shifts, mid_gain[None], hidden_shifts],
        [((rows + 16, width), bf16), ((2 * rows + 16, width), bf16), ((rows, width), bf16), ((rows, width), bf16), ((16, width), f32), ((8, ff), f32)],
    )
    beyond = swap(first, "sp", 2)
    theirs = swap(both, "sp", 1)
    upstream_t = call("turn", turn_late_body, tab, [upstream, theirs], [((width, 2 * rows), bf16)], deps=(beyond,))[0]
    wq0 = call("rows_qkv", rows_body, tab, [wq_lines], [((grid.nz * block, 3 * shard_lanes), bf16)])[0]
    wq1 = swap(wq0, "dp", 1)
    firsts = [first, theirs, beyond, swap(beyond, "sp", 1)]
    qkv, keep = call(
        "project", functools.partial(project_body, sp), tab, firsts + [wq0, wq1, model_shifts],
        [((group, 3 * shard_lanes), bf16), ((8, group), f32)], steps=sp,
        out_specs=[by_rows(rows, 3 * shard_lanes), pl.BlockSpec((8, rows), lambda i, *_: (0, i))],
    )
    hd = Heads(4, heads // sp, 0, (0, 1, 2), ORD, WHO, sp)
    scaled, o_t, lse = ORDER.passed(attend_forward(hd, tab, spans, qkv, keep, head_scale, deps=ORDER.last))
    returned = lax.all_to_all(scaled.reshape(sp, rows, shard_lanes), "sp", 0, 0, tiled=True)

    ret_spec = pl.BlockSpec((sp, step, shard_lanes), lambda i, *_: (0, i, 0))
    anywhere = pl.BlockSpec(memory_space=pl.ANY)
    pair, middle, attn_normed, attn_std, wo = call(
        "to_middle", functools.partial(middle_body, 2 * w_up.shape[1]), tab, [returned, tokr, vec, shards],
        [((rows, 2 * width), bf16), ((rows, width), f32), ((rows, width), f32), ((rows, 1), f32), ((width, width), bf16)],
        steps=2,
        in_specs=[ret_spec, by_rows(step, width), whole(vec.shape), anywhere],
        out_specs=[by_rows(step, 2 * width)] + [by_rows(step, width)] * 2 + [by_rows(step, 1), whole((width, width))],
        scratch=[pltpu.SemaphoreType.DMA((8, 8))], vmem=40,
    )
    pair_sib = swap(pair, "sp", 1)
    hid_own, hid_sib, pre_own, pre_sib, second_grad, layer_out, hidden_sums = call(
        "ffn", functools.partial(ffn_body, unit), tab, [pair, upstream, middle, hid, vec, shards],
        [((rows, ff // 2), bf16)] * 4 + [((rows, width), f32), ((rows, width), bf16), ((8, ff), f32)],
        steps=2,
        in_specs=[by_rows(step, width)] * 3 + [whole(hid.shape), whole(vec.shape)] + [anywhere],
        out_specs=[by_rows(step, ff // 2)] * 4 + [by_rows(step, width)] * 2 + [whole((8, ff))],
        scratch=[pltpu.VMEM((width, ff), bf16)] * 2 + [pltpu.VMEM((step, ff), f32)] * 3 + [pltpu.SemaphoreType.DMA((2, 8, 8))],
        vmem=63, us=37,
    )

    pre_across = swap(pre_sib, "sp", 1)
    spilled = call(
        "spill", functools.partial(spill_body, unit), tab, [upstream_t, hid_own, hid_sib], [((dp * sp, block, 2 * unit), bf16)], steps=8,
        in_specs=[pl.BlockSpec((width, rows), lambda *_: (0, 0)),
                  pl.BlockSpec((rows, unit), lambda i, *_: (0, jnp.clip(i, 0, 3))),
                  pl.BlockSpec((rows, unit), lambda i, *_: (0, jnp.clip(i - 4, 0, 3)))],
        vmem=40,
    )[0]
    grad_w_down = lax.psum_scatter(spilled, ("dp", "sp"), scatter_dimension=0, tiled=True)[0].astype(f32)
    middle_grad, attn_own, attn_sib, back, sums = call(
        "to_heads", heads_body, tab, [second_grad, middle, attn_normed, attn_std, upstream, vec, wo],
        [((rows, width), f32)] + [((rows, width // 2), bf16)] * 2 + [((sp, rows, shard_lanes), bf16), ((8, width), f32)],
        steps=2,
        in_specs=[by_rows(step, width)] * 3 + [by_rows(step, 1), by_rows(step, width), whole(vec.shape), whole(wo.shape)],
        out_specs=[by_rows(step, width)] + [by_rows(step, width // 2)] * 2 + [ret_spec, whole((8, width))],
        scratch=[pltpu.VMEM((step, width), bf16)],
        vmem=62,
    )
    attn_across = swap(attn_sib, "sp", 1)
    early = call("pack", pack_body, tab, [sums, vec, hidden_sums], [((24, width), f32)])[0]
    early = (early, swap(early, "sp", 1))

    grads_in = lax.all_to_all(back, "sp", 0, 0, tiled=True).reshape(group, shard_lanes)
    up_sums = scatter_weights(
        grid, tab, width,
        [([(pair, 0), (pair_sib, 0)], (pre_own, 0), (pre_across, 0)), ([(pair, 1), (pair_sib, 1)], (attn_own, 0), (attn_across, 0))],
        (unit, LANES), "up", rider=early,
    )
    (early,) = next(up_sums)
    early = (early, swap(early, "sp", 2))
    wide = 3 * shard_lanes
    qkv_grad, head_sums = ORDER.passed(
        attend_backward(hd, 0, tab, spans, qkv, keep, head_scale, grads_in, o_t, lse, deps=ORDER.last)
    )
    mine, cross, far = call(
        "first_grad", first_grad_body, tab, [qkv_grad, wq0, wq1],
        [((rows, width), f32), ((2 * rows, width), bf16), ((rows, width), f32)], steps=sp,
        in_specs=[by_rows(rows, wide), whole(wq0.shape), whole(wq1.shape)],
        out_specs=[whole((rows, width)), whole((2 * rows, width)), whole((rows, width))],
    )
    keep_rows, send = call(
        "group_grads", functools.partial(groups_body, sp), tab, firsts + [qkv_grad],
        [((width // 2, wide), f32), ((width // 2, wide), bf16)], steps=sp,
        in_specs=[whole(f.shape) for f in firsts] + [by_rows(rows, wide)],
        scratch=[pltpu.VMEM((width, wide), f32)], vmem=30,
    )
    cross, send, early, *second_up = up_sums.send((early, [cross, send]))
    early = (early, swap(early, "dp", 1))
    theirs, other_rows = swap(cross, "sp", 1), swap(send, "dp", 1)
    relayed = call("relay", relay_body, tab, [far, theirs], [((rows, width), bf16)],
                   in_specs=[whole(far.shape), pl.BlockSpec((rows, width), lambda *_: (1, 0))])[0]
    crossed = swap(relayed, "sp", 2)
    grad_tokens, late, early = call(
        "to_tokens", final_body, tab, [mine, theirs, crossed, tokr, middle_grad, vec, head_sums],
        [((rows, width), f32), ((dp * sp, 24, LANES), f32)], steps=2,
        in_specs=[by_rows(step, width)] * 5 + [whole(vec.shape), whole((8, wide))],
        out_specs=[by_rows(step, width), whole((dp * sp, 24, LANES))],
        scratch=[pltpu.VMEM((8, width), f32), pltpu.VMEM((24, LANES), f32)], rider=early, deps=(other_rows, *second_up),
    )
    early = (early, swap(early, "dp", 2))
    late = lax.all_to_all(late, ("dp", "sp"), 0, 0, tiled=True)
    up_sums.send(((keep_rows, other_rows), shard_lanes))
    late = call("totals", functools.partial(totals_body, sp), tab, [late], [((8, width), f32)])[0]
    grad_w_up, grad_w_out, *sent, early = up_sums.send(early)
    early = (early, swap(early, "dp", 4))
    got = [carry(x, pairs) for x, pairs in zip(sent, back_to)]
    grad_w_qkv, early = call("home", home_body, tab, got, [((block, 3 * shard_lanes), f32)], rider=early)
    grad_model_gains = jnp.stack([late[0], early[0], early[1]])
    grad_model_shifts = jnp.stack([late[2], late[3], early[2], late[1], early[3], early[4], early[5]])
    totals = early[6 : 6 + 3 * ff // width].reshape(3, ff)
    return (
        layer_out,
        grad_tokens,
        grad_w_qkv,
        grad_w_out,
        grad_w_up,
        grad_w_down,
        grad_model_gains,
        grad_model_shifts,
        totals[0],
        totals[1:3],
        late[4, :heads],
    )


def per_device(*arrays):
    dp, sp = lax.axis_size("dp"), lax.axis_size("sp")
    (rows, width), heads, ff = arrays[0].shape, arrays[12].shape[0], arrays[10].shape[0]
    if (dp, sp) == (8, 4) and width == 8 * LANES and heads * HEAD == width and ff == 4 * width and rows % BQ == 0:
        return fast_layer(*arrays)
    return general_layer(*arrays)


def solution(mesh):
    rows = P(("dp", "sp"), None)
    placed = (rows, P("dp", None), P(("dp", "sp")), rows) + (P("dp", "sp"),) * 4 + (P(),) * 5
    return jax.shard_map(
        per_device,
        mesh=mesh,
        in_specs=placed,
        out_specs=(rows, rows) + (P("dp", "sp"),) * 4 + (P(),) * 5,
        check_vma=False,
    )
```

```python
import functools

import jax
import jax.numpy as jnp
import numpy as np
from jax import lax
from jax.experimental import pallas as pl
from jax.experimental.pallas import tpu as pltpu
from jax.sharding import PartitionSpec as P

EPSILON = 1e-05
MASKED = -1e30
HEAD = 64
bf16 = jnp.bfloat16
f32 = jnp.float32


def mm(a, b):
    return lax.dot_general(a, b, (((1,), (0,)), ((), ())), preferred_element_type=f32)


def mm_rows(a, b):
    return lax.dot_general(a, b, (((0,), (0,)), ((), ())), preferred_element_type=f32)


def mm_cols(a, b):
    return lax.dot_general(a, b, (((1,), (1,)), ((), ())), preferred_element_type=f32)


def skipping(kernel, at, count):
    return lambda *refs: kernel(*refs[:at], *refs[at + count :])


def unread(deps):
    return [pl.BlockSpec(memory_space=pl.ANY)] * len(deps)


def lanes_of(x, h):
    lane = lax.broadcasted_iota(jnp.int32, x.shape, 1) // HEAD
    return jnp.where(lane == h, x, jnp.zeros_like(x))


def segment_of(spans, places):
    count, end = jnp.zeros_like(places), jnp.int32(0)
    for k in range(spans.shape[0]):
        end = end + spans[k]
        count = count + (places >= end).astype(jnp.int32)
    return count


class Heads:
    def __init__(self, nh, local, first, blocks, order_at, who_at, parts, rows):
        self.nh, self.local, self.first, self.blocks = nh, local, first, blocks
        self.order_at, self.who_at, self.parts, self.rows = order_at, who_at, parts, rows
        self.bq, self.bk = min(512, rows), min(256, rows)

    def place(self, tab, row):
        return tab[self.order_at + row // self.rows] * self.rows + row % self.rows


def keys_of(hd, tab, spans, keep_ref, kseg):
    for j in range(hd.parts):
        at = pl.ds(pl.multiple_of(tab[hd.order_at + j] * hd.rows, hd.rows), hd.rows)
        places = j * hd.rows + lax.broadcasted_iota(jnp.int32, (hd.rows, 1), 0)
        kseg[at, :] = jnp.where(keep_ref[:, at].T[:, 0:1] > 0.5, segment_of(spans, places), -1)


def visible(hd, i, j, spans, kseg, at):
    bq, bk = hd.bq, hd.bk
    kpos = j * bk + lax.broadcasted_iota(jnp.int32, (bk, bq), 0)
    qpos = i * bq + lax.broadcasted_iota(jnp.int32, (bk, bq), 1)
    qseg = segment_of(spans, i * bq + lax.broadcasted_iota(jnp.int32, (1, bq), 1))
    return (kseg[at, :] == qseg) & (kpos <= qpos)


def each_block(hd, tab, spans, i, body):
    bq, bk = hd.bq, hd.bk
    first = segment_of(spans, i * bq)

    def step(j, carry):
        at = pl.ds(pl.multiple_of(hd.place(tab, j * bk), bk), bk)
        pl.when(first <= segment_of(spans, (j + 1) * bk - 1))(lambda: body(j, at))
        return carry

    lax.fori_loop(0, ((i + 1) * bq - 1) // bk + 1, step, 0)


def fwd_kernel(hd, tab, spans, q_ref, k_ref, v_ref, keep_ref, hs_ref, scaled_ref, o_ref, lse_ref,
               kseg, vms, sscr, mpart, lpart, acc):
    nh, bq, bk = hd.nh, hd.bq, hd.bk
    i = pl.program_id(0)

    @pl.when(i == 0)
    def _():
        for h in range(nh):
            vms[h] = lanes_of(v_ref[...], h)
        keys_of(hd, tab, spans, keep_ref, kseg)

    qs = q_ref[...] * bf16(0.125)
    qm = [lanes_of(qs, h) for h in range(nh)]
    mpart[...] = jnp.full_like(mpart, MASKED)
    lpart[...] = jnp.zeros_like(lpart)
    acc[...] = jnp.zeros_like(acc)

    def one(j, at):
        kb = k_ref[at, :]
        mask = visible(hd, i, j, spans, kseg, at)
        for h in range(nh):
            s = jnp.where(mask, mm_cols(kb, qm[h]), MASKED)
            sscr[h, at, :] = s
            mpart[h] = jnp.maximum(mpart[h], jnp.max(s.reshape(bk // 8, 8, bq), axis=0))

    each_block(hd, tab, spans, i, one)
    ms = [jnp.max(mpart[h], axis=0, keepdims=True) for h in range(nh)]

    def two(j, at):
        pts = []
        for h in range(nh):
            p = jnp.exp(sscr[h, at, :] - ms[h])
            lpart[h] += jnp.sum(p.reshape(bk // 8, 8, bq), axis=0)
            pts.append(p.astype(bf16).T)
        acc[...] += mm(
            jnp.concatenate(pts, axis=1),
            jnp.concatenate([vms[h, at, :] for h in range(nh)], axis=0),
        )

    each_block(hd, tab, spans, i, two)
    out_t = acc[...].T
    parts = []
    for h in range(nh):
        rows = slice(h * HEAD, (h + 1) * HEAD)
        total = jnp.sum(lpart[h], axis=0, keepdims=True)
        result = out_t[rows, :] * (1.0 / total)
        o_ref[rows, :] = result
        parts.append(result * hs_ref[0, tab[hd.who_at] * hd.local + hd.first + h])
        lse_ref[h : h + 1, :] = ms[h] + jnp.log(total)
    scaled_ref[...] = jnp.concatenate(parts, axis=0).T.astype(bf16)


def head_specs(hd, n, w):
    q, k, v = hd.blocks
    bq = hd.bq
    return [
        pl.BlockSpec((bq, w), lambda i, t, s: (hd.place(t, i * bq) // bq, q)),
        pl.BlockSpec((n, w), lambda i, t, s: (0, k)),
        pl.BlockSpec((n, w), lambda i, t, s: (0, v)),
    ]


def attend_forward(hd, tab, spans, qkv, keep, head_scale, deps=()):
    n, nh, w = qkv.shape[0], hd.nh, hd.nh * HEAD
    bq = hd.bq
    return pl.pallas_call(
        skipping(functools.partial(fwd_kernel, hd), 7, len(deps)),
        grid_spec=pltpu.PrefetchScalarGridSpec(
            num_scalar_prefetch=2,
            grid=(n // bq,),
            in_specs=head_specs(hd, n, w)
            + [pl.BlockSpec((8, n), lambda i, t, s: (0, 0)), pl.BlockSpec(memory_space=pltpu.SMEM)]
            + unread(deps),
            out_specs=[
                pl.BlockSpec((bq, w), lambda i, t, s: (i, 0)),
                pl.BlockSpec((w, bq), lambda i, t, s: (0, i)),
                pl.BlockSpec((8, bq), lambda i, t, s: (0, i)),
            ],
            scratch_shapes=[
                pltpu.VMEM((n, 1), jnp.int32),
                pltpu.VMEM((nh, n, w), bf16),
                pltpu.VMEM((nh, n, bq), f32),
                pltpu.VMEM((nh, 8, bq), f32),
                pltpu.VMEM((nh, 8, bq), f32),
                pltpu.VMEM((bq, w), f32),
            ],
        ),
        out_shape=[
            jax.ShapeDtypeStruct((n, w), bf16),
            jax.ShapeDtypeStruct((w, n), f32),
            jax.ShapeDtypeStruct((8, n), f32),
        ],
        compiler_params=pltpu.CompilerParams(vmem_limit_bytes=60 << 20),
        cost_estimate=pl.CostEstimate(flops=nh * n * n * HEAD * 38, bytes_accessed=1024, transcendentals=0),
        name="attend_forward",
    )(tab, spans, qkv, qkv, qkv, keep, head_scale[None], *deps)


def bwd_kernel(hd, tab, spans, q_ref, k_ref, v_ref, keep_ref, hs_ref, sg_ref, o_ref, lse_ref,
               grad_ref, sums_ref, kseg, dk, dv, dq, gacc, kms):
    nh, bq, bk = hd.nh, hd.bq, hd.bk
    i = pl.program_id(0)
    n, w = k_ref.shape[0], nh * HEAD

    @pl.when(i == 0)
    def _():
        dk[...] = jnp.zeros_like(dk)
        dv[...] = jnp.zeros_like(dv)
        gacc[...] = jnp.zeros_like(gacc)
        for h in range(nh):
            kms[h] = lanes_of(k_ref[...], h)
        keys_of(hd, tab, spans, keep_ref, kseg)

    qs = q_ref[...] * bf16(0.125)
    qm = [lanes_of(qs, h) for h in range(nh)]
    scales = [hs_ref[0, tab[hd.who_at] * hd.local + hd.first + h] for h in range(nh)]
    sg = sg_ref[...].astype(f32)
    lane = lax.broadcasted_iota(jnp.int32, (1, w), 1) // HEAD
    scale_row = jnp.zeros((1, w), f32)
    for h in range(nh):
        scale_row = jnp.where(lane == h, scales[h], scale_row)
    grads = (sg * scale_row).astype(bf16)
    dom = [lanes_of(grads, h) for h in range(nh)]
    o = o_ref[...]
    gacc[...] += sg.T * o
    weighed = grads.astype(f32).T * o
    delta = [jnp.sum(weighed[h * HEAD : (h + 1) * HEAD, :], axis=0, keepdims=True) for h in range(nh)]
    lse = [lse_ref[h : h + 1, :] for h in range(nh)]
    qcat = jnp.concatenate(qm, axis=0)
    docat = jnp.concatenate(dom, axis=0)
    dq[...] = jnp.zeros_like(dq)

    def block(j, at):
        kb = k_ref[at, :]
        vb = v_ref[at, :]
        mask = visible(hd, i, j, spans, kseg, at)
        ps, dss, dsts = [], [], []
        for h in range(nh):
            p = jnp.where(mask, jnp.exp(mm_cols(kb, qm[h]) - lse[h]), 0.0)
            ds = (p * (mm_cols(vb, dom[h]) - delta[h])).astype(bf16)
            ps.append(p.astype(bf16))
            dsts.append(ds.T)
            dss.append(ds)
        dv[at, :] += mm(jnp.concatenate(ps, axis=1), docat)
        dk[at, :] += mm(jnp.concatenate(dss, axis=1), qcat)
        dq[...] += mm(
            jnp.concatenate(dsts, axis=1),
            jnp.concatenate([kms[h, at, :] for h in range(nh)], axis=0),
        )

    each_block(hd, tab, spans, i, block)
    mine = hd.place(tab, i * bq)
    grad_ref[pl.ds(pl.multiple_of(mine, bq), bq), 0:w] = (dq[...] * 0.125).astype(bf16)

    @pl.when(i == n // bq - 1)
    def _():
        grad_ref[:, w : 2 * w] = dk[...].astype(bf16)
        grad_ref[:, 2 * w : 3 * w] = dv[...].astype(bf16)
        place = lax.broadcasted_iota(jnp.int32, (1, 3 * w), 1)
        gains = jnp.zeros((1, 3 * w), f32)
        for h in range(nh):
            gains = jnp.where(place == h, jnp.sum(gacc[h * HEAD : (h + 1) * HEAD, :]), gains)
        sums_ref[...] = jnp.zeros_like(sums_ref)
        sums_ref[0:1, :] = jnp.sum(grad_ref[...].astype(f32), axis=0, keepdims=True)
        sums_ref[1:2, :] = gains


def attend_backward(hd, part, tab, spans, qkv, keep, head_scale, scaled_grad, o_t, lse, deps=()):
    n, nh, w = qkv.shape[0], hd.nh, hd.nh * HEAD
    bq = hd.bq
    return pl.pallas_call(
        skipping(functools.partial(bwd_kernel, hd), 10, len(deps)),
        grid_spec=pltpu.PrefetchScalarGridSpec(
            num_scalar_prefetch=2,
            grid=(n // bq,),
            in_specs=head_specs(hd, n, w)
            + [
                pl.BlockSpec((8, n), lambda i, t, s: (0, 0)),
                pl.BlockSpec(memory_space=pltpu.SMEM),
                pl.BlockSpec((bq, w), lambda i, t, s: (i, part)),
                pl.BlockSpec((w, bq), lambda i, t, s: (0, i)),
                pl.BlockSpec((8, bq), lambda i, t, s: (0, i)),
            ]
            + unread(deps),
            out_specs=[
                pl.BlockSpec((n, 3 * w), lambda i, t, s: (0, 0)),
                pl.BlockSpec((8, 3 * w), lambda i, t, s: (0, 0)),
            ],
            scratch_shapes=[
                pltpu.VMEM((n, 1), jnp.int32),
                pltpu.VMEM((n, w), f32),
                pltpu.VMEM((n, w), f32),
                pltpu.VMEM((bq, w), f32),
                pltpu.VMEM((w, bq), f32),
                pltpu.VMEM((nh, n, w), bf16),
            ],
        ),
        out_shape=[
            jax.ShapeDtypeStruct((n, 3 * w), bf16),
            jax.ShapeDtypeStruct((8, 3 * w), f32),
        ],
        compiler_params=pltpu.CompilerParams(vmem_limit_bytes=60 << 20),
        cost_estimate=pl.CostEstimate(flops=nh * n * n * HEAD * 50, bytes_accessed=1024, transcendentals=0),
        name="attend_backward",
    )(tab, spans, qkv, qkv, qkv, keep, head_scale[None], scaled_grad, o_t, lse, *deps)


def swap(x, axis, bits):
    return lax.ppermute(x, axis, [(i, i ^ bits) for i in range(lax.axis_size(axis))])


def reorder(x, idx, width):
    rows, cols = x.shape
    return jnp.take(x.reshape(rows, cols // width, width), idx, axis=1).reshape(rows, cols)


def reorder_rows(x, idx, height):
    rows, cols = x.shape
    return jnp.take(x.reshape(rows // height, height, cols), idx, axis=0).reshape(rows, cols)


class Grid:
    def __init__(self, dp, sp):
        self.dp, self.sp = dp, sp
        self.nx = max(sp // 2, 1)
        self.ny = self.nx if dp % self.nx == 0 else 1
        self.nz = dp // self.ny
        self.z_bits = [self.ny * k for k in range(1, self.nz)]
        self.y_bits = list(range(1, self.ny))
        self.x_bits = [2 * k for k in range(1, self.nx)]

    def gather_z(self, w):
        return jnp.concatenate([w] + [swap(w, "dp", b) for b in self.z_bits], axis=0)

    def gather_y(self, w):
        return jnp.concatenate([w] + [swap(w, "dp", b) for b in self.y_bits], axis=0)

    def gather(self, w):
        half = w.shape[1] // 2
        rows = self.gather_z(w)
        first, other = rows[:, :half], rows[:, half:]
        first = self.gather_y(first)
        firsts = [first] + [swap(first, "sp", b) for b in self.x_bits]
        other = jnp.concatenate([other] + [swap(other, "sp", b) for b in self.x_bits], axis=1)
        other = self.gather_y(other)
        parts = []
        for k in range(self.nx):
            parts += [firsts[k], other[:, k * half : (k + 1) * half]]
        return jnp.concatenate(parts, axis=1)

    def fold(self, parts, axis, bits):
        total = parts[0].astype(f32)
        for part, b in zip(parts[1:], bits, strict=True):
            total = total + swap(part.astype(bf16), axis, b).astype(f32)
        return total

    def scatter_y(self, g):
        rows = g.shape[0] // self.ny
        return self.fold([g[k * rows : (k + 1) * rows] for k in range(self.ny)], "dp", self.y_bits)

    def scatter_z(self, g):
        rows = g.shape[0] // self.nz
        return self.fold([g[k * rows : (k + 1) * rows] for k in range(self.nz)], "dp", self.z_bits)

    def scatter_x(self, g):
        cols = g.shape[1] // self.nx
        return self.fold([g[:, k * cols : (k + 1) * cols] for k in range(self.nx)], "sp", self.x_bits)

    def scatter(self, g):
        cols = g.shape[1] // self.nx
        half = cols // 2
        first = jnp.concatenate([g[:, k * cols : k * cols + half] for k in range(self.nx)], axis=1)
        other = jnp.concatenate([g[:, k * cols + half : (k + 1) * cols] for k in range(self.nx)], axis=1)
        first = self.scatter_y(self.scatter_x(first))
        other = self.scatter_x(self.scatter_y(other))
        return self.scatter_z(jnp.concatenate([first, other], axis=1))

    def all_sum(self, v):
        for axis in ("sp", "dp"):
            bit = 1
            while bit < lax.axis_size(axis):
                v = v + swap(v, axis, bit)
                bit *= 2
        return v


def norm_forward(halves, gains, shifts):
    width = sum(h.shape[1] for h in halves)
    mean = sum(jnp.sum(h, axis=1, keepdims=True) for h in halves) / width
    centred = [h - mean for h in halves]
    inv_std = lax.rsqrt(sum(jnp.sum(c * c, axis=1, keepdims=True) for c in centred) / width + EPSILON)
    normed = [c * inv_std for c in centred]
    return [n * a + b for n, a, b in zip(normed, gains, shifts)], normed, inv_std


def norm_backward(incoming, normed, inv_std, gains):
    width = sum(h.shape[1] for h in incoming)
    scaled = [e * a for e, a in zip(incoming, gains)]
    mean = sum(jnp.sum(s, axis=1, keepdims=True) for s in scaled) / width
    along = sum(jnp.sum(s * n, axis=1, keepdims=True) for s, n in zip(scaled, normed)) / width
    grads = [inv_std * (s - mean - n * along) for s, n in zip(scaled, normed)]
    gain_sums = [jnp.sum(e * n, axis=0) for e, n in zip(incoming, normed)]
    return grads, gain_sums, [jnp.sum(e, axis=0) for e in incoming]


def general_layer(
    tokens,
    seq_spans,
    valid_mask,
    cotangent,
    w_qkv,
    w_out,
    w_up,
    w_down,
    model_gains,
    model_shifts,
    mid_gain,
    hidden_shifts,
    head_scale,
):
    dp, sp = lax.axis_size("dp"), lax.axis_size("sp")
    grid = Grid(dp, sp)
    nx, ny, nz = grid.nx, grid.ny, grid.nz
    me_d, me_s = lax.axis_index("dp"), lax.axis_index("sp")
    rows, width = tokens.shape
    group = rows * sp
    heads = head_scale.shape[0]
    nh = heads // sp
    lw = nh * HEAD
    block = width // dp
    ff = mid_gain.shape[0]

    place = jnp.arange(dp, dtype=jnp.int32)
    to_rel = ((place % nz) * ny + place // nz) ^ me_d
    away = place ^ me_d
    to_abs = (away % ny) * nz + away // ny
    sp_place = jnp.arange(sp, dtype=jnp.int32)
    sp_rel = ((sp_place % nx) * 2 + sp_place // nx) ^ me_s
    sp_away = sp_place ^ me_s
    sp_abs = (sp_away % 2) * nx + sp_away // 2

    pad_rows = 16
    valid_rows = rows // lw
    blocks = w_qkv.reshape(block, 3, lw).transpose(1, 0, 2)
    blocks = jnp.concatenate([blocks, jnp.zeros((sp - 3, block, lw), bf16)], axis=0)
    turned = jnp.concatenate(
        [lax.dynamic_slice_in_dim(blocks, (t - 3 * me_s) % sp, 1, 0) for t in range(sp)], axis=0
    )
    flag_rows = jnp.concatenate(
        [valid_mask.astype(bf16).reshape(valid_rows, lw), jnp.zeros((pad_rows - valid_rows, lw), bf16)], axis=0
    )
    sent = jnp.concatenate([turned, jnp.broadcast_to(flag_rows[None], (sp, pad_rows, lw))], axis=1)
    got = lax.all_to_all(sent, "sp", 0, 0, tiled=True)
    keep = got[:, block : block + valid_rows].reshape(group) > 0.5
    wq_shard = jnp.concatenate(
        [lax.dynamic_slice_in_dim(got, (t * sp + me_s) // 3, 1, 0)[0, :block] for t in range(3)], axis=1
    )
    wq = grid.gather_y(grid.gather_z(wq_shard))

    gains = reorder(model_gains, to_rel, block)
    shifts = reorder(model_shifts, to_rel, block)
    stream = reorder(tokens, to_rel, block).astype(f32)
    upstream = reorder(cotangent, to_rel, block) * valid_mask.astype(bf16)[:, None]
    (first_out,), (first_normed,), first_std = norm_forward([stream], gains[0:1], shifts[3:4])
    first = first_out.astype(bf16)

    crossed = [first] + [swap(first, "sp", b) for b in grid.x_bits]
    firsts = []
    for piece in crossed:
        firsts += [piece, swap(piece, "sp", 1)]
    piece_bits = [b for k in [0] + grid.x_bits for b in (k, k + 1)]
    qkv_shift = jnp.concatenate(
        [
            lax.dynamic_slice_in_dim(model_shifts[0], me_s * lw, lw, 0),
            jnp.zeros((lw,), f32),
            lax.dynamic_slice_in_dim(model_shifts[1], me_s * lw, lw, 0),
        ]
    )
    firsts_cat = jnp.concatenate(firsts, axis=0)
    qkv_rel = (mm(firsts_cat, wq) + qkv_shift).astype(bf16)
    group_order = sp_place ^ me_s
    qkv = reorder_rows(qkv_rel, group_order, rows)

    low_down = jnp.concatenate([w_out, w_down], axis=1)
    od_own = grid.gather(low_down)
    up_own = grid.gather(w_up)
    oc, dc = w_out.shape[1], w_down.shape[1]
    out_own = jnp.concatenate([od_own[:, k * (oc + dc) : k * (oc + dc) + oc] for k in range(nx)], axis=1)
    down_own = jnp.concatenate([od_own[:, k * (oc + dc) + oc : (k + 1) * (oc + dc)] for k in range(nx)], axis=1)
    wos = jnp.concatenate([out_own, swap(out_own, "sp", 1)], axis=1)
    downs = [down_own, swap(down_own, "sp", 1)]
    ups = [up_own, swap(up_own, "sp", 1)]
    wo = reorder(reorder_rows(wos, to_abs, block), sp_abs, oc)

    tab = jnp.concatenate([sp_place, me_s[None].astype(jnp.int32)])
    hd = Heads(nh, nh, 0, (0, 1, 2), 0, sp, sp, rows)
    keep_col = jnp.broadcast_to(keep.astype(f32)[None, :], (8, group))
    scaled, o_t, lse = attend_forward(hd, tab, seq_spans[0], qkv, keep_col, head_scale)
    returned = lax.all_to_all(scaled.reshape(sp, rows, lw), "sp", 0, 0, tiled=True)
    merged = jnp.concatenate([returned[t] for t in range(sp)], axis=1)

    attn_pre = reorder(mm(merged, wo) + model_shifts[2], to_rel, block)
    (attn_out,), (attn_normed,), attn_std = norm_forward([attn_pre], gains[1:2], shifts[4:5])
    middle = stream + attn_out
    (second_out,), (second_normed,), second_std = norm_forward([middle], gains[2:3], shifts[5:6])
    second = second_out.astype(bf16)

    ff_half = ff // 2
    hidden_vectors = reorder(
        jnp.concatenate([mid_gain[None], hidden_shifts], axis=0), sp_rel, ff // sp
    )
    split = lambda v: [v[:, :ff_half], v[:, ff_half:]]
    hg, hb, hs = split(hidden_vectors[0:1]), split(hidden_vectors[1:2]), split(hidden_vectors[2:3])
    pre = [mm(second, w) + b for w, b in zip(ups, hb)]
    activated, pulls = zip(*[jax.vjp(jax.nn.gelu, p) for p in pre])
    hidden_out, hidden_normed, hidden_std = norm_forward(activated, hg, hs)
    hidden = [h.astype(bf16) for h in hidden_out]
    out_rel = middle + mm_cols(hidden[0], downs[0]) + mm_cols(hidden[1], downs[1]) + shifts[6:7]
    layer_out = reorder(out_rel.astype(bf16), to_abs, block)

    pair = lambda x: jnp.concatenate([x, swap(x, "sp", 1)], axis=0)
    across = lambda halves: jnp.concatenate([halves[0], swap(halves[1], "sp", 1)], axis=0)
    upstream_pair = pair(upstream)
    g_down = mm_rows(upstream_pair, across(hidden)).astype(bf16)
    grad_w_down = grid.scatter(g_down)

    hidden_grad = [mm(upstream, w) for w in downs]
    act_grad, grad_mid, grad_mid_shift = norm_backward(hidden_grad, hidden_normed, hidden_std, hg)
    pre_grad = [pull(a)[0].astype(bf16) for pull, a in zip(pulls, act_grad)]
    second_grad = mm_cols(pre_grad[0], ups[0]) + mm_cols(pre_grad[1], ups[1])
    (middle_part,), (gain_ffn,), (shift_ffn,) = norm_backward([second_grad], [second_normed], second_std, gains[2:3])
    middle_grad = upstream.astype(f32) + middle_part
    (attn_grad_full,), (gain_attn,), (shift_attn,) = norm_backward([middle_grad], [attn_normed], attn_std, gains[1:2])
    attn_grad_rel = attn_grad_full.astype(bf16)
    attn_grad = reorder(attn_grad_rel, to_abs, block)
    merged_grad = mm_cols(attn_grad, wo).astype(bf16)
    scattered = jnp.stack([merged_grad[:, t * lw : (t + 1) * lw] for t in range(sp)], axis=0)
    scaled_grad = lax.all_to_all(scattered, "sp", 0, 0, tiled=True).reshape(group, lw)

    g_up = mm_rows(pair(second), across(pre_grad)).astype(bf16)
    grad_w_up = grid.scatter(g_up)
    merged_rel = reorder(merged, to_rel, block)
    attn_grad_cols = reorder(attn_grad, sp_rel, oc)
    g_out = mm_rows(pair(merged_rel), across([attn_grad_cols[:, : width // 2], attn_grad_cols[:, width // 2 :]]))
    grad_w_out = grid.scatter_z(grid.scatter_y(grid.scatter_x(g_out)))

    qkv_grad, head_sums = attend_backward(
        hd, 0, tab, seq_spans[0], qkv, keep_col, head_scale, scaled_grad, o_t, lse
    )
    qkv_grad_rel = reorder_rows(qkv_grad, group_order, rows)
    first_part = mm_cols(qkv_grad_rel, wq)
    pieces = [first_part[t * rows : (t + 1) * rows] for t in range(sp)]
    folded = [
        pieces[t].astype(f32) + swap(pieces[t + 1].astype(bf16), "sp", 1).astype(f32) for t in range(0, sp, 2)
    ]
    first_grad = grid.fold(folded, "sp", grid.x_bits)
    (input_part,), (gain_in,), (shift_in,) = norm_backward([first_grad], [first_normed], first_std, gains[0:1])
    grad_tokens = reorder(middle_grad + input_part, to_abs, block)

    g_qkv = mm_rows(firsts_cat, qkv_grad_rel)
    g_mine = grid.scatter_z(grid.scatter_y(g_qkv)).astype(bf16)
    g_blocks = jnp.concatenate(
        [g_mine.reshape(block, 3, lw).transpose(1, 0, 2), jnp.zeros((1, block, lw), bf16)], axis=0
    )
    back = []
    for t in range(sp):
        which = jnp.int32(3)
        for u in range(3):
            which = jnp.where((u * sp + me_s) // 3 == t, u, which)
        back.append(lax.dynamic_slice_in_dim(g_blocks, which, 1, 0))
    home = lax.all_to_all(jnp.concatenate(back, axis=0), "sp", 0, 0, tiled=True)
    grad_w_qkv = jnp.concatenate(
        [lax.dynamic_slice_in_dim(home, (3 * me_s + u) % sp, 1, 0)[0] for u in range(3)], axis=1
    ).astype(f32)

    qkv_sums = jnp.sum(qkv_grad.astype(f32), axis=0)
    zeros = jnp.zeros((2, width), f32)
    bias_sums = lax.dynamic_update_slice(
        zeros, jnp.stack([qkv_sums[:lw], qkv_sums[2 * lw :]]), (0, me_s * lw)
    )
    sum_early = jnp.concatenate(
        [
            reorder(
                jnp.stack(
                    [
                        gain_attn,
                        gain_ffn,
                        jnp.sum(attn_grad_rel.astype(f32), axis=0),
                        shift_attn,
                        shift_ffn,
                        jnp.sum(upstream.astype(f32), axis=0),
                    ]
                ),
                to_abs,
                block,
            ),
            reorder(
                jnp.stack(
                    [
                        jnp.concatenate(grad_mid),
                        jnp.concatenate([jnp.sum(p.astype(f32), axis=0) for p in pre_grad]),
                        jnp.concatenate(grad_mid_shift),
                    ]
                ),
                sp_abs,
                ff // sp,
            ).reshape(3 * ff // width, width),
        ],
        axis=0,
    )
    early = grid.all_sum(sum_early)
    scale_row = lax.dynamic_update_slice(
        jnp.zeros((1, width), f32), head_sums[1:2, :nh], (0, me_s * nh)
    )
    late = grid.all_sum(
        jnp.concatenate(
            [reorder(jnp.stack([gain_in, shift_in]), to_abs, block), bias_sums, scale_row], axis=0
        )
    )
    grad_model_gains = jnp.stack([late[0], early[0], early[1]])
    grad_model_shifts = jnp.stack([late[2], late[3], early[2], late[1], early[3], early[4], early[5]])
    hidden_sums = early[6:].reshape(3, ff)
    return (
        layer_out,
        grad_tokens,
        grad_w_qkv,
        grad_w_out,
        grad_w_up,
        grad_w_down,
        grad_model_gains,
        grad_model_shifts,
        hidden_sums[0],
        hidden_sums[1:3],
        late[4, :heads],
    )


REL, HID, ORD, COLS, WHO, SEND, SLOT, ALONG = 0, 8, 16, 24, 32, 33, 36, 40
LANES = 128


def matchings(sp):
    left = {s: {3 * s + k: (3 * s + k) % sp for k in range(3)} for s in range(sp)}
    rounds = []
    for _ in range(3):
        taken = {}

        def seat(s, seen):
            for b, to in sorted(left[s].items(), key=lambda e: e[1] != s):
                if to not in seen:
                    seen.add(to)
                    if to not in taken or seat(taken[to][0], seen):
                        taken[to] = (s, b)
                        return True
            return False

        for s in range(sp):
            seat(s, set())
        one = [None] * sp
        for to, (s, b) in taken.items():
            one[s] = (b - 3 * s, b // sp, to)
            del left[s][b]
        rounds.append(one)
    return rounds


def tables(dp, sp, ny, nz, rounds):
    out = np.zeros((dp * sp, 128), np.int32)
    for d in range(dp):
        for s in range(sp):
            row = out[d * sp + s]
            where = {}
            for p in range(dp):
                row[REL + p] = ((p % nz) * ny + p // nz) ^ d
                where[row[REL + p]] = p
            for q in range(2 * sp):
                dc, half, dx = q // 4, q // 2 % 2, q % 2
                row[HID + q] = ((dx * 2 + dc) ^ s) * 2 + half
                row[COLS + q] = where[row[HID + q]]
            for t in range(sp):
                row[ORD + t] = s ^ t
            row[WHO] = s
            for k in range(nz):
                row[ALONG + k] = d // ny ^ k
            for m in range(3):
                row[SEND + m] = rounds[m][s][0]
                row[SLOT + m] = next(rounds[m][a][1] for a in range(sp) if rounds[m][a][2] == s)
    return out


def span(index, size):
    return pl.ds(pl.multiple_of(index * size, size), size)


def norm_of(x):
    mean = jnp.mean(x, axis=1, keepdims=True)
    centred = x - mean
    inv_std = lax.rsqrt(jnp.mean(centred * centred, axis=1, keepdims=True) + EPSILON)
    return centred * inv_std, inv_std


def norm_back(incoming, normed, inv_std, gain):
    scaled = incoming * gain
    mean = jnp.mean(scaled, axis=1, keepdims=True)
    along = jnp.mean(scaled * normed, axis=1, keepdims=True)
    return inv_std * (scaled - mean - normed * along)


def down_sum(x):
    return jnp.sum(x, axis=0, keepdims=True)


def whole(shape):
    return pl.BlockSpec(shape, lambda *_: (0,) * len(shape))


def by_rows(rows, cols):
    return pl.BlockSpec((rows, cols), lambda i, *_: (i, 0))


class Order:
    last = ()

    def after(self, deps):
        return tuple(deps) + self.last

    def passed(self, outs):
        self.last = (outs[-1],)
        return outs


ORDER = Order()


def with_rider(body, at, count):
    def both(*refs):
        first, second, total = refs[at], refs[at + 1], refs[at + 2 + count]

        @pl.when(pl.program_id(0) == 0)
        def _():
            total[...] = first[...] + second[...]

        body(*refs[:at], *refs[at + 2 : at + 2 + count], *refs[at + 3 + count :])

    return both


def call(name, body, tab, args, outs, steps=1, in_specs=None, out_specs=None, scratch=(), deps=(), vmem=20, us=0, rider=None):
    in_specs = [whole(a.shape) for a in args] if in_specs is None else in_specs
    out_specs = [whole(s) for s, _ in outs] if out_specs is None else out_specs
    if rider is not None:
        body = with_rider(body, 1 + len(args), len(outs))
        args, outs = list(args) + list(rider), list(outs) + [(rider[0].shape, rider[0].dtype)]
        in_specs = list(in_specs) + [whole(rider[0].shape)] * 2
        out_specs = list(out_specs) + [whole(rider[0].shape)]
    deps = ORDER.after(deps)
    made = pl.pallas_call(
        skipping(body, 1 + len(args), len(deps)),
        grid_spec=pltpu.PrefetchScalarGridSpec(
            num_scalar_prefetch=1,
            grid=(steps,),
            in_specs=list(in_specs) + unread(deps),
            out_specs=list(out_specs),
            scratch_shapes=list(scratch),
        ),
        out_shape=[jax.ShapeDtypeStruct(s, t) for s, t in outs],
        compiler_params=pltpu.CompilerParams(vmem_limit_bytes=vmem << 20),
        cost_estimate=pl.CostEstimate(flops=int(us * 1.1e9) + 1024, bytes_accessed=1024, transcendentals=0),
        name=name,
    )(tab, *args, *deps)
    return ORDER.passed(made)


def part_body(tab, w, *outs):
    width = outs[0].shape[1]
    for m, out in enumerate(outs):
        out[...] = w[:, span(tab[SEND + m], width)]


def join_body(tab, *refs):
    pieces, out = refs[:-1], refs[-1]
    for m, piece in enumerate(pieces):
        for k in range(out.shape[0]):
            out[k, :, span(tab[SLOT + m], piece.shape[1])] = piece[...]


def home_body(tab, p0, p1, p2, late, early, out, gains, shifts, mid, hid, scale):
    size, width = p0.shape[1], late.shape[1]
    for m, piece in enumerate((p0, p1, p2)):
        out[:, span(tab[SEND + m], size)] = piece[...].astype(f32)
    for row, source in enumerate((late[0:1], early[0:1], early[1:2])):
        gains[row : row + 1, :] = source
    for row, source in enumerate((late[2:3], late[3:4], early[2:3], late[1:2], early[3:4], early[4:5], early[5:6])):
        shifts[row : row + 1, :] = source
    for k in range(mid.shape[1] // width):
        to = slice(k * width, (k + 1) * width)
        mid[:, to] = early[6 + k : 7 + k, :]
        hid[0:1, to] = early[10 + k : 11 + k, :]
        hid[1:2, to] = early[14 + k : 15 + k, :]
    scale[...] = late[4:5, : scale.shape[1]]


def prologue_body(tab, tok, cot, vcol, vrow, gains, shifts, mid, hsh, first_ref, both_ref, up_ref, tokr_ref, vec_ref, hid_ref):
    rows, width = tok.shape
    unit = mid.shape[1] // 8
    valid = vcol[...]
    vec_ref[...] = jnp.zeros_like(vec_ref)
    hid_ref[...] = jnp.zeros_like(hid_ref)
    for p in range(8):
        at, to = span(tab[REL + p], LANES), slice(p * LANES, (p + 1) * LANES)
        tokr_ref[:, to] = tok[:, at]
        vec_ref[0:3, to] = gains[:, at]
        vec_ref[3:10, to] = shifts[:, at]
        at, to = span(tab[HID + p], unit), slice(p * unit, (p + 1) * unit)
        hid_ref[0:1, to] = mid[:, at]
        hid_ref[1:3, to] = hsh[:, at]
    gain, shift = vec_ref[0:1, :], vec_ref[6:7, :]

    def chunk(i, carry):
        at = span(i, 64)
        normed, _ = norm_of(tokr_ref[at, :].astype(f32))
        first_ref[at, :] = (normed * gain + shift).astype(bf16)
        return carry

    lax.fori_loop(0, rows // 64, chunk, 0)
    first_ref[rows:, :] = jnp.broadcast_to(vrow[...], (16, width))
    both_ref[: rows + 16, :] = first_ref[...]
    for p in range(8):
        at, to = span(tab[REL + p], LANES), slice(p * LANES, (p + 1) * LANES)
        masked = cot[:, at].astype(f32) * valid
        up_ref[:, to] = masked.astype(bf16)
        vec_ref[10:11, to] = down_sum(masked)
    both_ref[rows + 16 :, :] = up_ref[...]


def project_body(count, tab, *refs):
    pieces, (w0, w1, shifts, out_ref, keep_ref) = refs[:count], refs[count:]
    rows, depth = out_ref.shape[0], w0.shape[0]
    at = span(tab[WHO], 2 * LANES)
    bias = jnp.concatenate([shifts[0:1, at], jnp.zeros((1, 2 * LANES), f32), shifts[1:2, at]], axis=1)
    for k in range(count):

        @pl.when(pl.program_id(0) == k)
        def _():
            x = pieces[k]
            out_ref[...] = (mm(x[:rows, :depth], w0[...]) + mm(x[:rows, depth:], w1[...]) + bias).astype(bf16)
            keep_ref[...] = x[rows : rows + 16, :rows].astype(f32)[:8]


def middle_body(begin, tab, ret, tok, vec, shards, pair_ref, mid_ref, norm_ref, std_ref, wo, sems):
    width = tok.shape[1]

    def copies(p):
        out = []
        for q in range(8):
            at = tab[HID + q]
            source = shards.at[tab[REL + p] * 4 + at // 2, :, pl.ds(pl.multiple_of(begin + lax.rem(at, 2) * LANES, LANES), LANES)]
            out.append(pltpu.make_async_copy(source, wo.at[pl.ds(p * LANES, LANES), span(tab[COLS + q], LANES)], sems.at[p, q]))
        return out

    @pl.when(pl.program_id(0) == 0)
    def _():
        for p in range(8):
            for copy in copies(p):
                copy.start()

    for p in range(8):
        a = tab[REL + p]
        pair_ref[:, width + p * LANES : width + (p + 1) * LANES] = ret[a // 2, :, span(lax.rem(a, 2), LANES)]

    @pl.when(pl.program_id(0) == 0)
    def _():
        for p in range(8):
            for copy in copies(p):
                copy.wait()

    normed, inv_std = norm_of(mm(pair_ref[:, width:], wo[...]) + vec[5:6, :])
    middle = tok[...].astype(f32) + (normed * vec[1:2, :] + vec[7:8, :])
    norm_ref[...] = normed
    std_ref[...] = inv_std
    mid_ref[...] = middle
    again, _ = norm_of(middle)
    pair_ref[:, :width] = (again * vec[2:3, :] + vec[8:9, :]).astype(bf16)


GELU = 0.7978845608028654
CUBE = 0.044715


def ffn_body(unit, tab, second, upstream, mid, hid, vec, *refs):
    shards, (hown, hsib, pown, psib, sg_ref, lo_ref, sums_ref, upv, dnv, act, slope, back, sems) = refs[0], refs[1:]
    i = pl.program_id(0)
    ff = upv.shape[1]

    def copies(q, which):
        held = (upv, dnv)[which]
        at = tab[HID + q]
        from_cols = pl.ds(pl.multiple_of(which * 2 * unit + lax.rem(at, 2) * unit, unit), unit)
        out = []
        for p in range(8):
            source = shards.at[tab[REL + p] * 4 + at // 2, :, from_cols]
            out.append(pltpu.make_async_copy(source, held.at[pl.ds(p * LANES, LANES), pl.ds(q * unit, unit)], sems.at[which, q, p]))
        return out

    @pl.when(i == 0)
    def _():
        sums_ref[...] = jnp.zeros_like(sums_ref)
        for q in range(8):
            for copy in copies(q, 0):
                copy.start()
        for q in range(8):
            for copy in copies(q, 1):
                copy.start()

    x = second[...]
    total = jnp.zeros((x.shape[0], 1), f32)
    for q in range(8):
        at = slice(q * unit, (q + 1) * unit)

        @pl.when(i == 0)
        def _():
            for copy in copies(q, 0):
                copy.wait()

        pre = mm(x, upv[:, at]) + hid[1:2, at]
        squared = pre * pre
        t = jnp.tanh(pre * (GELU + (GELU * CUBE) * squared))
        one = 0.5 + 0.5 * t
        value = pre * one
        act[:, at] = value
        slope[:, at] = one + 0.5 * pre * (1.0 - t * t) * (GELU + (3 * GELU * CUBE) * squared)
        total = total + jnp.sum(value, axis=1, keepdims=True)
    mean = total / ff
    total = jnp.zeros_like(mean)
    for q in range(8):
        at = slice(q * unit, (q + 1) * unit)
        centred = act[:, at] - mean
        total = total + jnp.sum(centred * centred, axis=1, keepdims=True)
    inv_std = lax.rsqrt(total / ff + EPSILON)
    u = upstream[...]
    m1, m2 = jnp.zeros_like(mean), jnp.zeros_like(mean)
    low = jnp.zeros(mid.shape, f32)
    for q in range(8):
        at = slice(q * unit, (q + 1) * unit)

        @pl.when(i == 0)
        def _():
            for copy in copies(q, 1):
                copy.wait()

        incoming = mm(u, dnv[:, at])
        normed = (act[:, at] - mean) * inv_std
        act[:, at] = normed
        gain = hid[0:1, at]
        held, to = ((hown, at) if q < 4 else (hsib, slice((q - 4) * unit, (q - 3) * unit)))
        hidden = (normed * gain + hid[2:3, at]).astype(bf16)
        held[:, to] = hidden
        low = low + mm_cols(hidden, dnv[:, at])
        along = incoming * normed
        sums_ref[0:1, at] += down_sum(along)
        sums_ref[2:3, at] += down_sum(incoming)
        m1 = m1 + jnp.sum(incoming * gain, axis=1, keepdims=True)
        m2 = m2 + jnp.sum(along * gain, axis=1, keepdims=True)
        back[:, at] = incoming
    m1, m2 = m1 / ff, m2 / ff
    second_grad = jnp.zeros(mid.shape, f32)
    for q in range(8):
        at = slice(q * unit, (q + 1) * unit)
        grad = inv_std * (back[:, at] * hid[0:1, at] - m1 - act[:, at] * m2)
        pre_grad = (grad * slope[:, at]).astype(bf16)
        held, to = ((pown, at) if q < 4 else (psib, slice((q - 4) * unit, (q - 3) * unit)))
        held[:, to] = pre_grad
        sums_ref[1:2, at] += down_sum(pre_grad.astype(f32))
        second_grad = second_grad + mm_cols(pre_grad, upv[:, at])
    sg_ref[...] = second_grad
    out = (mid[...] + low + vec[9:10, :]).astype(bf16)
    for p in range(8):
        lo_ref[:, span(tab[REL + p], LANES)] = out[:, p * LANES : (p + 1) * LANES]


def heads_body(tab, grad, mid, norm, std, up, vec, wo, mg_ref, own_ref, sib_ref, out_ref, sums_ref, scr):
    @pl.when(pl.program_id(0) == 0)
    def _():
        sums_ref[...] = jnp.zeros_like(sums_ref)

    incoming = grad[...]
    again, inv_std = norm_of(mid[...])
    sums_ref[1:2, :] += down_sum(incoming * again)
    sums_ref[4:5, :] += down_sum(incoming)
    middle_grad = up[...].astype(f32) + norm_back(incoming, again, inv_std, vec[2:3, :])
    mg_ref[...] = middle_grad
    normed = norm[...]
    sums_ref[0:1, :] += down_sum(middle_grad * normed)
    sums_ref[3:4, :] += down_sum(middle_grad)
    low = norm_back(middle_grad, normed, std[...], vec[1:2, :]).astype(bf16)
    sums_ref[2:3, :] += down_sum(low.astype(f32))
    scr[...] = low
    for q in range(8):
        held = own_ref if q < 4 else sib_ref
        held[:, (q % 4) * LANES : (q % 4 + 1) * LANES] = scr[:, span(tab[COLS + q], LANES)]
    got = mm_cols(low, wo[...]).astype(bf16)
    for p in range(8):
        a = tab[REL + p]
        out_ref[a // 2, :, span(lax.rem(a, 2), LANES)] = got[:, p * LANES : (p + 1) * LANES]


def turn_body(tab, x0, x1, out):
    tokens = x0.shape[0]
    out[:, :tokens] = x0[...].T
    out[:, tokens:] = x1[...].T


def turn_late_body(tab, x0, both, out):
    tokens = x0.shape[0]
    out[:, :tokens] = x0[...].T
    out[:, tokens:] = both[tokens + 16 :, :].T


def grads_body(counts, widths, tab, *refs):
    ins, (ak, asend, bk, bsend, xt) = refs[:-5], refs[-5:]
    half = bk.shape[0]
    total = sum(widths)
    i = pl.program_id(0)
    at = begin = 0
    for n, (count, wide) in enumerate(zip(counts, widths)):
        xs, (y0, y1) = ins[begin : begin + count], ins[begin + count : begin + count + 2]
        begin += count + 2
        if count == 2:

            @pl.when(i == 4 * n)
            def _():
                turn_body(tab, *xs, xt)

        left = xt if count == 2 else xs[0]
        for q in range(4):

            @pl.when(i == 4 * n + q)
            def _():
                g = mm(left[...], jnp.concatenate([y0[...], y1[...]], axis=0)).astype(bf16)
                if q < 2:
                    (ak, asend)[q][:, at : at + wide] = g
                else:
                    to = slice((q - 2) * total + at, (q - 2) * total + at + wide)
                    bk[:, to] = g[:half]
                    bsend[:, to] = g[half:]

        at += wide


def groups_body(count, tab, *refs):
    pieces, (grad, keep, send, acc) = refs[:count], refs[count:]
    i = pl.program_id(0)
    half = keep.shape[0]
    rows = grad.shape[0]
    for k in range(count):

        @pl.when(i == k)
        def _():
            got = mm(pieces[k][:rows, :].T, grad[...])
            acc[...] = got if k == 0 else acc[...] + got

    @pl.when(i == count - 1)
    def _():
        keep[...] = acc[:half]
        send[...] = acc[half:].astype(bf16)


def fold_body(tab, ak, ra, bk, rb, x0, a2k, a2s, b2k, b2s, y0):
    y0[...] = x0[...]
    rows, cols = b2k.shape
    a = ak[...].astype(f32) + ra[...].astype(f32)
    a2k[...] = a[:rows].astype(bf16)
    a2s[...] = a[rows:].astype(bf16)
    b = bk[...].astype(f32) + rb[...].astype(f32)
    b2k[...] = b[:, :cols].astype(bf16)
    b2s[...] = b[:, cols:].astype(bf16)


def spread_body(tab, ak, ra, bk, rb, g, r, keep, *sends):
    rows, cols = keep.shape[0], ak.shape[1]
    at = 0
    for mine, theirs in ((ak, ra), (bk, rb), (g, r)):
        total = mine[...].astype(f32) + theirs[...].astype(f32)
        to = slice(at, at + total.shape[1])
        at += total.shape[1]
        keep[:, to] = total[:rows]
        for n, send in enumerate(sends, 1):
            send[:, to] = total[n * rows : (n + 1) * rows].astype(bf16)


def gathered_body(widths, tab, keep, r1, r2, r3, low, *refs):
    outs, pieces, (wide_low, total) = refs[: len(widths)], refs[len(widths) : -2], refs[-2:]
    wide_low[...] = low[...].astype(f32)
    total[...] = keep[...] + r1[...].astype(f32) + r2[...].astype(f32) + r3[...].astype(f32)
    half = sum(widths)
    at = 0
    for out, wide in zip(outs, widths):
        out[:, :wide] = total[:, at : at + wide]
        out[:, wide:] = total[:, half + at : half + at + wide]
        at += wide
    for m, piece in enumerate(pieces):
        size = piece.shape[1]
        piece[...] = total[:, pl.ds(pl.multiple_of(2 * half + tab[SLOT + m] * size, size), size)].astype(bf16)


def spill_body(unit, tab, xt, own, sib, out):
    tokens, width = own.shape[0], xt.shape[0]
    for half, y in enumerate((own, sib)):

        @pl.when(pl.program_id(0) // 4 == half)
        def _():
            g = mm(xt[:, :tokens], y[...]).astype(bf16)
            at = tab[HID + pl.program_id(0)]
            for p in range(8):
                out[tab[REL + p] * 4 + at // 2, :, span(lax.rem(at, 2), unit)] = g[p * LANES : (p + 1) * LANES]


def scatter_weights(grid, tab, rows, sets, widths, tag, rider=None):
    total = sum(widths)
    args, specs = [], []
    for n, (xs, y0, y1) in enumerate(sets):
        wide = widths[n]
        tokens = y0[0].shape[0]
        for x, part in xs:
            args.append(x)
            specs.append(whole(x.shape) if part is None else pl.BlockSpec((tokens, rows), lambda *_, part=part: (0, part)))
        for y, begin in (y0, y1):
            args.append(y)
            specs.append(pl.BlockSpec((tokens, wide), lambda i, *_, n=n, begin=begin: (0, begin + jnp.clip(i - 4 * n, 0, 3))))
    outs = [((rows, total), bf16)] * 2 + [((rows // 2, 2 * total), bf16)] * 2
    ak, asend, bk, bsend, *carried = call(
        "grads_" + tag, functools.partial(grads_body, [len(xs) for xs, _, _ in sets], widths), tab, args, outs,
        steps=4 * len(sets), in_specs=specs, scratch=[pltpu.VMEM((rows, 2 * tokens), bf16)], vmem=28, us=6 * len(sets), rider=rider,
    )
    ra, rb = swap(asend, "sp", 2), swap(bsend, "dp", 1)
    rider, ships = yield carried
    quarter = [((rows // 2, total), bf16)] * 4 + [(x.shape, x.dtype) for x in ships]
    a2k, a2s, b2k, b2s, *carried = call("fold_" + tag, fold_body, tab, [ak, ra, bk, rb] + ships, quarter, vmem=34, rider=rider)
    ra, rb = swap(a2s, "dp", 1), swap(b2s, "sp", 2)
    deps = yield carried + [ra, rb]
    (g, r), size, rider = deps
    shard = (rows // 8, 2 * total + g.shape[1])
    keep, *sends, carried = call(
        "spread_" + tag, spread_body, tab, [a2k, ra, b2k, rb, g, r], [(shard, f32)] + [(shard, bf16)] * 3, rider=rider
    )
    received = [swap(x, "dp", b) for x, b in zip(sends, grid.z_bits)]
    low = yield carried
    yield call(
        "sum_" + tag, functools.partial(gathered_body, widths), tab, [keep] + received + [low],
        [((rows // 8, 2 * w), f32) for w in widths] + [((rows // 8, size), bf16)] * 3 + [(low.shape, f32)],
        scratch=[pltpu.VMEM(shard, f32)],
    )


def along_z(grid, x):
    lines = [[y + grid.ny * k for k in range(grid.nz)] for y in range(grid.ny)]
    return lax.all_to_all(x, "dp", 0, 0, tiled=True, axis_index_groups=lines)


def rows_body(tab, got, out):
    rows = got.shape[1]
    for k in range(got.shape[0]):
        out[k * rows : (k + 1) * rows, :] = got[tab[ALONG + k]]


def first_grad_body(tab, g, wy0, wy1, mine, cross, far):
    i = pl.program_id(0)
    got = jnp.concatenate([mm_cols(g[...], wy0[...]), mm_cols(g[...], wy1[...])], axis=1)
    rows = g.shape[0]

    @pl.when(i == 0)
    def _():
        mine[...] = got

    @pl.when(i == 1)
    def _():
        cross[:rows] = got.astype(bf16)

    @pl.when(i == 2)
    def _():
        far[...] = got

    @pl.when(i == 3)
    def _():
        cross[rows:] = got.astype(bf16)


def relay_body(tab, far, theirs, send, out, sent):
    sent[...] = send[...]
    out[...] = (far[...] + theirs[...].astype(f32)).astype(bf16)


def final_body(tab, mine, theirs, crossed, tok, mg, vec, s0, out_ref, late_ref, acc, note):
    i = pl.program_id(0)
    width = tok.shape[1]

    @pl.when(i == 0)
    def _():
        acc[...] = jnp.zeros_like(acc)

    incoming = mine[...] + theirs[...].astype(f32) + crossed[...].astype(f32)
    normed, inv_std = norm_of(tok[...].astype(f32))
    acc[0:1, :] += down_sum(incoming * normed)
    acc[1:2, :] += down_sum(incoming)
    total = mg[...] + norm_back(incoming, normed, inv_std, vec[0:1, :])
    for p in range(8):
        out_ref[:, span(tab[REL + p], LANES)] = total[:, p * LANES : (p + 1) * LANES]

    @pl.when(i == pl.num_programs(0) - 1)
    def _():
        note[...] = jnp.zeros_like(note)
        for p in range(8):
            cols = slice(p * LANES, (p + 1) * LANES)
            note[pl.ds(tab[REL + p], 1), :] = acc[0:1, cols]
            note[pl.ds(8 + tab[REL + p], 1), :] = acc[1:2, cols]
        for e in range(2):
            note[16 + e : 17 + e, :] = s0[0:1, e * LANES : (e + 1) * LANES]
            note[18 + e : 19 + e, :] = s0[0:1, (4 + e) * LANES : (5 + e) * LANES]
        note[20:21, :] = s0[1:2, :LANES]
        for n in range(late_ref.shape[0]):
            late_ref[n] = note[...]


def totals_body(sp, tab, got, out):
    out[...] = jnp.zeros_like(out)
    count = got.shape[0]
    total = got[0, :16]
    for n in range(1, count):
        total = total + got[n, :16]
    for p in range(8):
        cols = slice(p * LANES, (p + 1) * LANES)
        out[0:1, cols] = total[p : p + 1]
        out[1:2, cols] = total[8 + p : 9 + p]
    heads = jnp.zeros((1, LANES), f32)
    lane = lax.broadcasted_iota(jnp.int32, (1, LANES), 1)
    for s in range(sp):
        mine = got[s, 16:24]
        for n in range(s + sp, count, sp):
            mine = mine + got[n, 16:24]
        for e in range(2):
            cols = slice((2 * s + e) * LANES, (2 * s + e + 1) * LANES)
            out[2:3, cols] = mine[e : e + 1]
            out[3:4, cols] = mine[2 + e : 3 + e]
        for h in range(4):
            value = jnp.sum(jnp.where(lane == h, mine[4:5], 0.0))
            heads = jnp.where(lane == 4 * s + h, value, heads)
    out[4:5, :LANES] = heads


def pack_body(tab, sums, vec, hid, out_ref):
    width, unit = sums.shape[1], hid.shape[1] // 8
    out_ref[...] = jnp.zeros_like(out_ref)
    for p in range(8):
        to, at = span(tab[REL + p], LANES), slice(p * LANES, (p + 1) * LANES)
        out_ref[0:5, to] = sums[0:5, at]
        out_ref[5:6, to] = vec[10:11, at]
    for v in range(3):
        for q in range(8):
            unit_at = tab[HID + q]
            row, col = 6 + 4 * v + unit_at // 2, lax.rem(unit_at, 2)
            out_ref[pl.ds(row, 1), span(col, unit)] = hid[v : v + 1, q * unit : (q + 1) * unit]


def fast_layer(
    tokens,
    seq_spans,
    valid_mask,
    cotangent,
    w_qkv,
    w_out,
    w_up,
    w_down,
    model_gains,
    model_shifts,
    mid_gain,
    hidden_shifts,
    head_scale,
):
    dp, sp = lax.axis_size("dp"), lax.axis_size("sp")
    grid = Grid(dp, sp)
    rows, width = tokens.shape
    group = rows * sp
    heads = head_scale.shape[0]
    block = width // dp
    ff = mid_gain.shape[0]
    unit = ff // 8
    shard_lanes = 2 * LANES
    step = rows // 2

    rounds = matchings(sp)
    device = lax.axis_index("dp") * sp + lax.axis_index("sp")
    tab = lax.dynamic_slice_in_dim(jnp.asarray(tables(dp, sp, grid.ny, grid.nz, rounds)), device, 1, 0)[0]
    spans = seq_spans[0]
    forth = [[(s, rounds[m][s][2]) for s in range(sp)] for m in range(3)]
    back_to = [[(t, s) for s, t in pairs] for pairs in forth]
    carry = lambda x, pairs: x if all(a == b for a, b in pairs) else lax.ppermute(x, "sp", pairs)

    ORDER.last = ()
    shards = lax.all_gather(jnp.concatenate([w_up, w_down, w_out], axis=1), ("dp", "sp"), axis=0)
    sent = call("part", part_body, tab, [w_qkv], [((block, shard_lanes), bf16)] * 3)
    moved = [carry(x, pairs) for x, pairs in zip(sent, forth)]
    wq_lines = along_z(grid, call("join", join_body, tab, moved, [((grid.nz, block, 3 * shard_lanes), bf16)])[0])
    vcol = valid_mask.astype(f32)[:, None]
    vrow = jnp.pad(valid_mask.astype(bf16), (0, width - rows))[None]
    first, both, upstream, tokr, vec, hid = call(
        "prologue", prologue_body, tab,
        [tokens, cotangent, vcol, vrow, model_gains, model_shifts, mid_gain[None], hidden_shifts],
        [((rows + 16, width), bf16), ((2 * rows + 16, width), bf16), ((rows, width), bf16), ((rows, width), bf16), ((16, width), f32), ((8, ff), f32)],
    )
    beyond = swap(first, "sp", 2)
    theirs = swap(both, "sp", 1)
    upstream_t = call("turn", turn_late_body, tab, [upstream, theirs], [((width, 2 * rows), bf16)], deps=(beyond,))[0]
    wq0 = call("rows_qkv", rows_body, tab, [wq_lines], [((grid.nz * block, 3 * shard_lanes), bf16)])[0]
    wq1 = swap(wq0, "dp", 1)
    firsts = [first, theirs, beyond, swap(beyond, "sp", 1)]
    qkv, keep = call(
        "project", functools.partial(project_body, sp), tab, firsts + [wq0, wq1, model_shifts],
        [((group, 3 * shard_lanes), bf16), ((8, group), f32)], steps=sp,
        out_specs=[by_rows(rows, 3 * shard_lanes), pl.BlockSpec((8, rows), lambda i, *_: (0, i))],
    )
    hd = Heads(4, heads // sp, 0, (0, 1, 2), ORD, WHO, sp, rows)
    scaled, o_t, lse = ORDER.passed(attend_forward(hd, tab, spans, qkv, keep, head_scale, deps=ORDER.last))
    returned = lax.all_to_all(scaled.reshape(sp, rows, shard_lanes), "sp", 0, 0, tiled=True)

    ret_spec = pl.BlockSpec((sp, step, shard_lanes), lambda i, *_: (0, i, 0))
    anywhere = pl.BlockSpec(memory_space=pl.ANY)
    pair, middle, attn_normed, attn_std, wo = call(
        "to_middle", functools.partial(middle_body, 2 * w_up.shape[1]), tab, [returned, tokr, vec, shards],
        [((rows, 2 * width), bf16), ((rows, width), f32), ((rows, width), f32), ((rows, 1), f32), ((width, width), bf16)],
        steps=2,
        in_specs=[ret_spec, by_rows(step, width), whole(vec.shape), anywhere],
        out_specs=[by_rows(step, 2 * width)] + [by_rows(step, width)] * 2 + [by_rows(step, 1), whole((width, width))],
        scratch=[pltpu.SemaphoreType.DMA((8, 8))], vmem=62,
    )
    pair_sib = swap(pair, "sp", 1)
    hid_own, hid_sib, pre_own, pre_sib, second_grad, layer_out, hidden_sums = call(
        "ffn", functools.partial(ffn_body, unit), tab, [pair, upstream, middle, hid, vec, shards],
        [((rows, ff // 2), bf16)] * 4 + [((rows, width), f32), ((rows, width), bf16), ((8, ff), f32)],
        steps=2,
        in_specs=[by_rows(step, width)] * 3 + [whole(hid.shape), whole(vec.shape)] + [anywhere],
        out_specs=[by_rows(step, ff // 2)] * 4 + [by_rows(step, width)] * 2 + [whole((8, ff))],
        scratch=[pltpu.VMEM((width, ff), bf16)] * 2 + [pltpu.VMEM((step, ff), f32)] * 3 + [pltpu.SemaphoreType.DMA((2, 8, 8))],
        vmem=63, us=37,
    )

    pre_across = swap(pre_sib, "sp", 1)
    spilled = call(
        "spill", functools.partial(spill_body, unit), tab, [upstream_t, hid_own, hid_sib], [((dp * sp, block, 2 * unit), bf16)], steps=8,
        in_specs=[pl.BlockSpec((width, rows), lambda *_: (0, 0)),
                  pl.BlockSpec((rows, unit), lambda i, *_: (0, jnp.clip(i, 0, 3))),
                  pl.BlockSpec((rows, unit), lambda i, *_: (0, jnp.clip(i - 4, 0, 3)))],
        vmem=62,
    )[0]
    down_part = lax.psum_scatter(spilled, ("dp", "sp"), scatter_dimension=0, tiled=True)[0]
    middle_grad, attn_own, attn_sib, back, sums = call(
        "to_heads", heads_body, tab, [second_grad, middle, attn_normed, attn_std, upstream, vec, wo],
        [((rows, width), f32)] + [((rows, width // 2), bf16)] * 2 + [((sp, rows, shard_lanes), bf16), ((8, width), f32)],
        steps=2,
        in_specs=[by_rows(step, width)] * 3 + [by_rows(step, 1), by_rows(step, width), whole(vec.shape), whole(wo.shape)],
        out_specs=[by_rows(step, width)] + [by_rows(step, width // 2)] * 2 + [ret_spec, whole((8, width))],
        scratch=[pltpu.VMEM((step, width), bf16)],
        vmem=62,
    )
    attn_across = swap(attn_sib, "sp", 1)
    early = call("pack", pack_body, tab, [sums, vec, hidden_sums], [((24, width), f32)])[0]
    early = (early, swap(early, "sp", 1))

    grads_in = lax.all_to_all(back, "sp", 0, 0, tiled=True).reshape(group, shard_lanes)
    up_sums = scatter_weights(
        grid, tab, width,
        [([(pair, 0), (pair_sib, 0)], (pre_own, 0), (pre_across, 0)), ([(pair, 1), (pair_sib, 1)], (attn_own, 0), (attn_across, 0))],
        (unit, LANES), "up", rider=early,
    )
    (early,) = next(up_sums)
    early = (early, swap(early, "sp", 2))
    wide = 3 * shard_lanes
    qkv_grad, head_sums = ORDER.passed(
        attend_backward(hd, 0, tab, spans, qkv, keep, head_scale, grads_in, o_t, lse, deps=ORDER.last)
    )
    mine, cross, far = call(
        "first_grad", first_grad_body, tab, [qkv_grad, wq0, wq1],
        [((rows, width), f32), ((2 * rows, width), bf16), ((rows, width), f32)], steps=sp,
        in_specs=[by_rows(rows, wide), whole(wq0.shape), whole(wq1.shape)],
        out_specs=[whole((rows, width)), whole((2 * rows, width)), whole((rows, width))],
    )
    cross, early, *second_up = up_sums.send((early, [cross]))
    theirs = swap(cross, "sp", 1)
    early = (early, swap(early, "dp", 1))
    keep_rows, send = call(
        "group_grads", functools.partial(groups_body, sp), tab, firsts + [qkv_grad],
        [((width // 2, wide), f32), ((width // 2, wide), bf16)], steps=sp,
        in_specs=[whole(f.shape) for f in firsts] + [by_rows(rows, wide)],
        scratch=[pltpu.VMEM((width, wide), f32)], vmem=30,
    )
    relayed, send, early = call(
        "relay", relay_body, tab, [far, theirs, send], [((rows, width), bf16), (send.shape, bf16)],
        in_specs=[whole(far.shape), pl.BlockSpec((rows, width), lambda *_: (1, 0)), whole(send.shape)], rider=early,
    )
    crossed, other_rows = swap(relayed, "sp", 2), swap(send, "dp", 1)
    early = (early, swap(early, "dp", 2))
    grad_tokens, late, early = call(
        "to_tokens", final_body, tab, [mine, theirs, crossed, tokr, middle_grad, vec, head_sums],
        [((rows, width), f32), ((dp * sp, 24, LANES), f32)], steps=2,
        in_specs=[by_rows(step, width)] * 5 + [whole(vec.shape), whole((8, wide))],
        out_specs=[by_rows(step, width), whole((dp * sp, 24, LANES))],
        scratch=[pltpu.VMEM((8, width), f32), pltpu.VMEM((24, LANES), f32)], rider=early, deps=(other_rows, *second_up),
    )
    early = (early, swap(early, "dp", 4))
    late = lax.all_to_all(late, ("dp", "sp"), 0, 0, tiled=True)
    early = up_sums.send(((keep_rows, other_rows), shard_lanes, early))
    late = call("totals", functools.partial(totals_body, sp), tab, [late], [((8, width), f32)])[0]
    grad_w_up, grad_w_out, *sent, grad_w_down = up_sums.send(down_part)
    got = [carry(x, pairs) for x, pairs in zip(sent, back_to)]
    grad_w_qkv, gain_sums, shift_sums, mid_sums, hid_sums, scale_sums = call(
        "home", home_body, tab, got + [late, early],
        [((block, 3 * shard_lanes), f32), ((3, width), f32), ((7, width), f32), ((1, ff), f32), ((2, ff), f32), ((1, heads), f32)],
    )
    return (
        layer_out,
        grad_tokens,
        grad_w_qkv,
        grad_w_out,
        grad_w_up,
        grad_w_down,
        gain_sums,
        shift_sums,
        mid_sums[0],
        hid_sums,
        scale_sums[0],
    )


def per_device(*arrays):
    dp, sp = lax.axis_size("dp"), lax.axis_size("sp")
    (rows, width), heads, ff = arrays[0].shape, arrays[12].shape[0], arrays[10].shape[0]
    if (dp, sp) == (8, 4) and width == 8 * LANES and heads * HEAD == width and ff == 4 * width and rows == 512:
        return fast_layer(*arrays)
    return general_layer(*arrays)


def solution(mesh):
    rows = P(("dp", "sp"), None)
    placed = (rows, P("dp", None), P(("dp", "sp")), rows) + (P("dp", "sp"),) * 4 + (P(),) * 5
    return jax.shard_map(
        per_device,
        mesh=mesh,
        in_specs=placed,
        out_specs=(rows, rows) + (P("dp", "sp"),) * 4 + (P(),) * 5,
        check_vma=False,
    )
```

```python
import functools

import jax
import jax.numpy as jnp
import numpy as np
from jax import lax
from jax.experimental import pallas as pl
from jax.experimental.pallas import tpu as pltpu
from jax.sharding import PartitionSpec as P

EPSILON = 1e-05
MASKED = -1e30
HEAD = 64
bf16 = jnp.bfloat16
f32 = jnp.float32


def mm(a, b):
    return lax.dot_general(a, b, (((1,), (0,)), ((), ())), preferred_element_type=f32)


def mm_rows(a, b):
    return lax.dot_general(a, b, (((0,), (0,)), ((), ())), preferred_element_type=f32)


def mm_cols(a, b):
    return lax.dot_general(a, b, (((1,), (1,)), ((), ())), preferred_element_type=f32)


def skipping(kernel, at, count):
    return lambda *refs: kernel(*refs[:at], *refs[at + count :])


def unread(deps):
    return [pl.BlockSpec(memory_space=pl.ANY)] * len(deps)


def lanes_of(x, h):
    lane = lax.broadcasted_iota(jnp.int32, x.shape, 1) // HEAD
    return jnp.where(lane == h, x, jnp.zeros_like(x))


def segment_of(spans, places):
    count, end = jnp.zeros_like(places), jnp.int32(0)
    for k in range(spans.shape[0]):
        end = end + spans[k]
        count = count + (places >= end).astype(jnp.int32)
    return count


class Heads:
    def __init__(self, nh, local, first, blocks, order_at, who_at, parts, rows):
        self.nh, self.local, self.first, self.blocks = nh, local, first, blocks
        self.order_at, self.who_at, self.parts, self.rows = order_at, who_at, parts, rows
        self.bq, self.bk = min(512, rows), min(256, rows)

    def place(self, tab, row):
        return tab[self.order_at + row // self.rows] * self.rows + row % self.rows


def keys_of(hd, tab, spans, keep_ref, kseg):
    for j in range(hd.parts):
        at = pl.ds(pl.multiple_of(tab[hd.order_at + j] * hd.rows, hd.rows), hd.rows)
        places = j * hd.rows + lax.broadcasted_iota(jnp.int32, (hd.rows, 1), 0)
        kseg[at, :] = jnp.where(keep_ref[:, at].T[:, 0:1] > 0.5, segment_of(spans, places), -1)


def visible(hd, i, j, spans, kseg, at):
    bq, bk = hd.bq, hd.bk
    kpos = j * bk + lax.broadcasted_iota(jnp.int32, (bk, bq), 0)
    qpos = i * bq + lax.broadcasted_iota(jnp.int32, (bk, bq), 1)
    qseg = segment_of(spans, i * bq + lax.broadcasted_iota(jnp.int32, (1, bq), 1))
    return (kseg[at, :] == qseg) & (kpos <= qpos)


def each_block(hd, tab, spans, i, body):
    bq, bk = hd.bq, hd.bk
    first = segment_of(spans, i * bq)

    def step(j, carry):
        at = pl.ds(pl.multiple_of(hd.place(tab, j * bk), bk), bk)
        pl.when(first <= segment_of(spans, (j + 1) * bk - 1))(lambda: body(j, at))
        return carry

    lax.fori_loop(0, ((i + 1) * bq - 1) // bk + 1, step, 0)


def fwd_kernel(hd, tab, spans, q_ref, k_ref, v_ref, keep_ref, hs_ref, scaled_ref, o_ref, lse_ref,
               kseg, vms, sscr, mpart, lpart, acc):
    nh, bq, bk = hd.nh, hd.bq, hd.bk
    i = pl.program_id(0)

    @pl.when(i == 0)
    def _():
        for h in range(nh):
            vms[h] = lanes_of(v_ref[...], h)
        keys_of(hd, tab, spans, keep_ref, kseg)

    qs = q_ref[...] * bf16(0.125)
    qm = [lanes_of(qs, h) for h in range(nh)]
    mpart[...] = jnp.full_like(mpart, MASKED)
    lpart[...] = jnp.zeros_like(lpart)
    acc[...] = jnp.zeros_like(acc)

    def one(j, at):
        kb = k_ref[at, :]
        mask = visible(hd, i, j, spans, kseg, at)
        for h in range(nh):
            s = jnp.where(mask, mm_cols(kb, qm[h]), MASKED)
            sscr[h, at, :] = s
            mpart[h] = jnp.maximum(mpart[h], jnp.max(s.reshape(bk // 8, 8, bq), axis=0))

    each_block(hd, tab, spans, i, one)
    ms = [jnp.max(mpart[h], axis=0, keepdims=True) for h in range(nh)]

    def two(j, at):
        pts = []
        for h in range(nh):
            p = jnp.exp(sscr[h, at, :] - ms[h])
            lpart[h] += jnp.sum(p.reshape(bk // 8, 8, bq), axis=0)
            pts.append(p.astype(bf16).T)
        acc[...] += mm(
            jnp.concatenate(pts, axis=1),
            jnp.concatenate([vms[h, at, :] for h in range(nh)], axis=0),
        )

    each_block(hd, tab, spans, i, two)
    out_t = acc[...].T
    parts = []
    for h in range(nh):
        rows = slice(h * HEAD, (h + 1) * HEAD)
        total = jnp.sum(lpart[h], axis=0, keepdims=True)
        result = out_t[rows, :] * (1.0 / total)
        o_ref[rows, :] = result
        parts.append(result * hs_ref[0, tab[hd.who_at] * hd.local + hd.first + h])
        lse_ref[h : h + 1, :] = ms[h] + jnp.log(total)
    scaled_ref[...] = jnp.concatenate(parts, axis=0).T.astype(bf16)


def head_specs(hd, n, w):
    q, k, v = hd.blocks
    bq = hd.bq
    return [
        pl.BlockSpec((bq, w), lambda i, t, s: (hd.place(t, i * bq) // bq, q)),
        pl.BlockSpec((n, w), lambda i, t, s: (0, k)),
        pl.BlockSpec((n, w), lambda i, t, s: (0, v)),
    ]


def attend_forward(hd, tab, spans, qkv, keep, head_scale, deps=()):
    n, nh, w = qkv.shape[0], hd.nh, hd.nh * HEAD
    bq = hd.bq
    return pl.pallas_call(
        skipping(functools.partial(fwd_kernel, hd), 7, len(deps)),
        grid_spec=pltpu.PrefetchScalarGridSpec(
            num_scalar_prefetch=2,
            grid=(n // bq,),
            in_specs=head_specs(hd, n, w)
            + [pl.BlockSpec((8, n), lambda i, t, s: (0, 0)), pl.BlockSpec(memory_space=pltpu.SMEM)]
            + unread(deps),
            out_specs=[
                pl.BlockSpec((bq, w), lambda i, t, s: (i, 0)),
                pl.BlockSpec((w, bq), lambda i, t, s: (0, i)),
                pl.BlockSpec((8, bq), lambda i, t, s: (0, i)),
            ],
            scratch_shapes=[
                pltpu.VMEM((n, 1), jnp.int32),
                pltpu.VMEM((nh, n, w), bf16),
                pltpu.VMEM((nh, n, bq), f32),
                pltpu.VMEM((nh, 8, bq), f32),
                pltpu.VMEM((nh, 8, bq), f32),
                pltpu.VMEM((bq, w), f32),
            ],
        ),
        out_shape=[
            jax.ShapeDtypeStruct((n, w), bf16),
            jax.ShapeDtypeStruct((w, n), f32),
            jax.ShapeDtypeStruct((8, n), f32),
        ],
        compiler_params=pltpu.CompilerParams(vmem_limit_bytes=60 << 20),
        cost_estimate=pl.CostEstimate(flops=nh * n * n * HEAD * 38, bytes_accessed=1024, transcendentals=0),
        name="attend_forward",
    )(tab, spans, qkv, qkv, qkv, keep, head_scale[None], *deps)


def bwd_kernel(hd, tab, spans, q_ref, k_ref, v_ref, keep_ref, hs_ref, sg_ref, o_ref, lse_ref,
               grad_ref, sums_ref, kseg, dk, dv, dq, gacc, kms):
    nh, bq, bk = hd.nh, hd.bq, hd.bk
    i = pl.program_id(0)
    n, w = k_ref.shape[0], nh * HEAD

    @pl.when(i == 0)
    def _():
        dk[...] = jnp.zeros_like(dk)
        dv[...] = jnp.zeros_like(dv)
        gacc[...] = jnp.zeros_like(gacc)
        for h in range(nh):
            kms[h] = lanes_of(k_ref[...], h)
        keys_of(hd, tab, spans, keep_ref, kseg)

    qs = q_ref[...] * bf16(0.125)
    qm = [lanes_of(qs, h) for h in range(nh)]
    scales = [hs_ref[0, tab[hd.who_at] * hd.local + hd.first + h] for h in range(nh)]
    sg = sg_ref[...].astype(f32)
    lane = lax.broadcasted_iota(jnp.int32, (1, w), 1) // HEAD
    scale_row = jnp.zeros((1, w), f32)
    for h in range(nh):
        scale_row = jnp.where(lane == h, scales[h], scale_row)
    grads = (sg * scale_row).astype(bf16)
    dom = [lanes_of(grads, h) for h in range(nh)]
    o = o_ref[...]
    gacc[...] += sg.T * o
    weighed = grads.astype(f32).T * o
    delta = [jnp.sum(weighed[h * HEAD : (h + 1) * HEAD, :], axis=0, keepdims=True) for h in range(nh)]
    lse = [lse_ref[h : h + 1, :] for h in range(nh)]
    qcat = jnp.concatenate(qm, axis=0)
    docat = jnp.concatenate(dom, axis=0)
    dq[...] = jnp.zeros_like(dq)

    def block(j, at):
        kb = k_ref[at, :]
        vb = v_ref[at, :]
        mask = visible(hd, i, j, spans, kseg, at)
        ps, dss, dsts = [], [], []
        for h in range(nh):
            p = jnp.where(mask, jnp.exp(mm_cols(kb, qm[h]) - lse[h]), 0.0)
            ds = (p * (mm_cols(vb, dom[h]) - delta[h])).astype(bf16)
            ps.append(p.astype(bf16))
            dsts.append(ds.T)
            dss.append(ds)
        dv[at, :] += mm(jnp.concatenate(ps, axis=1), docat)
        dk[at, :] += mm(jnp.concatenate(dss, axis=1), qcat)
        dq[...] += mm(
            jnp.concatenate(dsts, axis=1),
            jnp.concatenate([kms[h, at, :] for h in range(nh)], axis=0),
        )

    each_block(hd, tab, spans, i, block)
    mine = hd.place(tab, i * bq)
    grad_ref[pl.ds(pl.multiple_of(mine, bq), bq), 0:w] = (dq[...] * 0.125).astype(bf16)

    @pl.when(i == n // bq - 1)
    def _():
        grad_ref[:, w : 2 * w] = dk[...].astype(bf16)
        grad_ref[:, 2 * w : 3 * w] = dv[...].astype(bf16)
        place = lax.broadcasted_iota(jnp.int32, (1, 3 * w), 1)
        gains = jnp.zeros((1, 3 * w), f32)
        for h in range(nh):
            gains = jnp.where(place == h, jnp.sum(gacc[h * HEAD : (h + 1) * HEAD, :]), gains)
        sums_ref[...] = jnp.zeros_like(sums_ref)
        sums_ref[0:1, :] = jnp.sum(grad_ref[...].astype(f32), axis=0, keepdims=True)
        sums_ref[1:2, :] = gains


def attend_backward(hd, part, tab, spans, qkv, keep, head_scale, scaled_grad, o_t, lse, deps=()):
    n, nh, w = qkv.shape[0], hd.nh, hd.nh * HEAD
    bq = hd.bq
    return pl.pallas_call(
        skipping(functools.partial(bwd_kernel, hd), 10, len(deps)),
        grid_spec=pltpu.PrefetchScalarGridSpec(
            num_scalar_prefetch=2,
            grid=(n // bq,),
            in_specs=head_specs(hd, n, w)
            + [
                pl.BlockSpec((8, n), lambda i, t, s: (0, 0)),
                pl.BlockSpec(memory_space=pltpu.SMEM),
                pl.BlockSpec((bq, w), lambda i, t, s: (i, part)),
                pl.BlockSpec((w, bq), lambda i, t, s: (0, i)),
                pl.BlockSpec((8, bq), lambda i, t, s: (0, i)),
            ]
            + unread(deps),
            out_specs=[
                pl.BlockSpec((n, 3 * w), lambda i, t, s: (0, 0)),
                pl.BlockSpec((8, 3 * w), lambda i, t, s: (0, 0)),
            ],
            scratch_shapes=[
                pltpu.VMEM((n, 1), jnp.int32),
                pltpu.VMEM((n, w), f32),
                pltpu.VMEM((n, w), f32),
                pltpu.VMEM((bq, w), f32),
                pltpu.VMEM((w, bq), f32),
                pltpu.VMEM((nh, n, w), bf16),
            ],
        ),
        out_shape=[
            jax.ShapeDtypeStruct((n, 3 * w), bf16),
            jax.ShapeDtypeStruct((8, 3 * w), f32),
        ],
        compiler_params=pltpu.CompilerParams(vmem_limit_bytes=60 << 20),
        cost_estimate=pl.CostEstimate(flops=nh * n * n * HEAD * 50, bytes_accessed=1024, transcendentals=0),
        name="attend_backward",
    )(tab, spans, qkv, qkv, qkv, keep, head_scale[None], scaled_grad, o_t, lse, *deps)


def swap(x, axis, bits):
    return lax.ppermute(x, axis, [(i, i ^ bits) for i in range(lax.axis_size(axis))])


def reorder(x, idx, width):
    rows, cols = x.shape
    return jnp.take(x.reshape(rows, cols // width, width), idx, axis=1).reshape(rows, cols)


def reorder_rows(x, idx, height):
    rows, cols = x.shape
    return jnp.take(x.reshape(rows // height, height, cols), idx, axis=0).reshape(rows, cols)


class Grid:
    def __init__(self, dp, sp):
        self.dp, self.sp = dp, sp
        self.nx = max(sp // 2, 1)
        self.ny = self.nx if dp % self.nx == 0 else 1
        self.nz = dp // self.ny
        self.z_bits = [self.ny * k for k in range(1, self.nz)]
        self.y_bits = list(range(1, self.ny))
        self.x_bits = [2 * k for k in range(1, self.nx)]

    def gather_z(self, w):
        return jnp.concatenate([w] + [swap(w, "dp", b) for b in self.z_bits], axis=0)

    def gather_y(self, w):
        return jnp.concatenate([w] + [swap(w, "dp", b) for b in self.y_bits], axis=0)

    def gather(self, w):
        half = w.shape[1] // 2
        rows = self.gather_z(w)
        first, other = rows[:, :half], rows[:, half:]
        first = self.gather_y(first)
        firsts = [first] + [swap(first, "sp", b) for b in self.x_bits]
        other = jnp.concatenate([other] + [swap(other, "sp", b) for b in self.x_bits], axis=1)
        other = self.gather_y(other)
        parts = []
        for k in range(self.nx):
            parts += [firsts[k], other[:, k * half : (k + 1) * half]]
        return jnp.concatenate(parts, axis=1)

    def fold(self, parts, axis, bits):
        total = parts[0].astype(f32)
        for part, b in zip(parts[1:], bits, strict=True):
            total = total + swap(part.astype(bf16), axis, b).astype(f32)
        return total

    def scatter_y(self, g):
        rows = g.shape[0] // self.ny
        return self.fold([g[k * rows : (k + 1) * rows] for k in range(self.ny)], "dp", self.y_bits)

    def scatter_z(self, g):
        rows = g.shape[0] // self.nz
        return self.fold([g[k * rows : (k + 1) * rows] for k in range(self.nz)], "dp", self.z_bits)

    def scatter_x(self, g):
        cols = g.shape[1] // self.nx
        return self.fold([g[:, k * cols : (k + 1) * cols] for k in range(self.nx)], "sp", self.x_bits)

    def scatter(self, g):
        cols = g.shape[1] // self.nx
        half = cols // 2
        first = jnp.concatenate([g[:, k * cols : k * cols + half] for k in range(self.nx)], axis=1)
        other = jnp.concatenate([g[:, k * cols + half : (k + 1) * cols] for k in range(self.nx)], axis=1)
        first = self.scatter_y(self.scatter_x(first))
        other = self.scatter_x(self.scatter_y(other))
        return self.scatter_z(jnp.concatenate([first, other], axis=1))

    def all_sum(self, v):
        for axis in ("sp", "dp"):
            bit = 1
            while bit < lax.axis_size(axis):
                v = v + swap(v, axis, bit)
                bit *= 2
        return v


def norm_forward(halves, gains, shifts):
    width = sum(h.shape[1] for h in halves)
    mean = sum(jnp.sum(h, axis=1, keepdims=True) for h in halves) / width
    centred = [h - mean for h in halves]
    inv_std = lax.rsqrt(sum(jnp.sum(c * c, axis=1, keepdims=True) for c in centred) / width + EPSILON)
    normed = [c * inv_std for c in centred]
    return [n * a + b for n, a, b in zip(normed, gains, shifts)], normed, inv_std


def norm_backward(incoming, normed, inv_std, gains):
    width = sum(h.shape[1] for h in incoming)
    scaled = [e * a for e, a in zip(incoming, gains)]
    mean = sum(jnp.sum(s, axis=1, keepdims=True) for s in scaled) / width
    along = sum(jnp.sum(s * n, axis=1, keepdims=True) for s, n in zip(scaled, normed)) / width
    grads = [inv_std * (s - mean - n * along) for s, n in zip(scaled, normed)]
    gain_sums = [jnp.sum(e * n, axis=0) for e, n in zip(incoming, normed)]
    return grads, gain_sums, [jnp.sum(e, axis=0) for e in incoming]


def general_layer(
    tokens,
    seq_spans,
    valid_mask,
    cotangent,
    w_qkv,
    w_out,
    w_up,
    w_down,
    model_gains,
    model_shifts,
    mid_gain,
    hidden_shifts,
    head_scale,
):
    dp, sp = lax.axis_size("dp"), lax.axis_size("sp")
    grid = Grid(dp, sp)
    nx, ny, nz = grid.nx, grid.ny, grid.nz
    me_d, me_s = lax.axis_index("dp"), lax.axis_index("sp")
    rows, width = tokens.shape
    group = rows * sp
    heads = head_scale.shape[0]
    nh = heads // sp
    lw = nh * HEAD
    block = width // dp
    ff = mid_gain.shape[0]

    place = jnp.arange(dp, dtype=jnp.int32)
    to_rel = ((place % nz) * ny + place // nz) ^ me_d
    away = place ^ me_d
    to_abs = (away % ny) * nz + away // ny
    sp_place = jnp.arange(sp, dtype=jnp.int32)
    sp_rel = ((sp_place % nx) * 2 + sp_place // nx) ^ me_s
    sp_away = sp_place ^ me_s
    sp_abs = (sp_away % 2) * nx + sp_away // 2

    pad_rows = 16
    valid_rows = rows // lw
    blocks = w_qkv.reshape(block, 3, lw).transpose(1, 0, 2)
    blocks = jnp.concatenate([blocks, jnp.zeros((sp - 3, block, lw), bf16)], axis=0)
    turned = jnp.concatenate(
        [lax.dynamic_slice_in_dim(blocks, (t - 3 * me_s) % sp, 1, 0) for t in range(sp)], axis=0
    )
    flag_rows = jnp.concatenate(
        [valid_mask.astype(bf16).reshape(valid_rows, lw), jnp.zeros((pad_rows - valid_rows, lw), bf16)], axis=0
    )
    sent = jnp.concatenate([turned, jnp.broadcast_to(flag_rows[None], (sp, pad_rows, lw))], axis=1)
    got = lax.all_to_all(sent, "sp", 0, 0, tiled=True)
    keep = got[:, block : block + valid_rows].reshape(group) > 0.5
    wq_shard = jnp.concatenate(
        [lax.dynamic_slice_in_dim(got, (t * sp + me_s) // 3, 1, 0)[0, :block] for t in range(3)], axis=1
    )
    wq = grid.gather_y(grid.gather_z(wq_shard))

    gains = reorder(model_gains, to_rel, block)
    shifts = reorder(model_shifts, to_rel, block)
    stream = reorder(tokens, to_rel, block).astype(f32)
    upstream = reorder(cotangent, to_rel, block) * valid_mask.astype(bf16)[:, None]
    (first_out,), (first_normed,), first_std = norm_forward([stream], gains[0:1], shifts[3:4])
    first = first_out.astype(bf16)

    crossed = [first] + [swap(first, "sp", b) for b in grid.x_bits]
    firsts = []
    for piece in crossed:
        firsts += [piece, swap(piece, "sp", 1)]
    piece_bits = [b for k in [0] + grid.x_bits for b in (k, k + 1)]
    qkv_shift = jnp.concatenate(
        [
            lax.dynamic_slice_in_dim(model_shifts[0], me_s * lw, lw, 0),
            jnp.zeros((lw,), f32),
            lax.dynamic_slice_in_dim(model_shifts[1], me_s * lw, lw, 0),
        ]
    )
    firsts_cat = jnp.concatenate(firsts, axis=0)
    qkv_rel = (mm(firsts_cat, wq) + qkv_shift).astype(bf16)
    group_order = sp_place ^ me_s
    qkv = reorder_rows(qkv_rel, group_order, rows)

    low_down = jnp.concatenate([w_out, w_down], axis=1)
    od_own = grid.gather(low_down)
    up_own = grid.gather(w_up)
    oc, dc = w_out.shape[1], w_down.shape[1]
    out_own = jnp.concatenate([od_own[:, k * (oc + dc) : k * (oc + dc) + oc] for k in range(nx)], axis=1)
    down_own = jnp.concatenate([od_own[:, k * (oc + dc) + oc : (k + 1) * (oc + dc)] for k in range(nx)], axis=1)
    wos = jnp.concatenate([out_own, swap(out_own, "sp", 1)], axis=1)
    downs = [down_own, swap(down_own, "sp", 1)]
    ups = [up_own, swap(up_own, "sp", 1)]
    wo = reorder(reorder_rows(wos, to_abs, block), sp_abs, oc)

    tab = jnp.concatenate([sp_place, me_s[None].astype(jnp.int32)])
    hd = Heads(nh, nh, 0, (0, 1, 2), 0, sp, sp, rows)
    keep_col = jnp.broadcast_to(keep.astype(f32)[None, :], (8, group))
    scaled, o_t, lse = attend_forward(hd, tab, seq_spans[0], qkv, keep_col, head_scale)
    returned = lax.all_to_all(scaled.reshape(sp, rows, lw), "sp", 0, 0, tiled=True)
    merged = jnp.concatenate([returned[t] for t in range(sp)], axis=1)

    attn_pre = reorder(mm(merged, wo) + model_shifts[2], to_rel, block)
    (attn_out,), (attn_normed,), attn_std = norm_forward([attn_pre], gains[1:2], shifts[4:5])
    middle = stream + attn_out
    (second_out,), (second_normed,), second_std = norm_forward([middle], gains[2:3], shifts[5:6])
    second = second_out.astype(bf16)

    ff_half = ff // 2
    hidden_vectors = reorder(
        jnp.concatenate([mid_gain[None], hidden_shifts], axis=0), sp_rel, ff // sp
    )
    split = lambda v: [v[:, :ff_half], v[:, ff_half:]]
    hg, hb, hs = split(hidden_vectors[0:1]), split(hidden_vectors[1:2]), split(hidden_vectors[2:3])
    pre = [mm(second, w) + b for w, b in zip(ups, hb)]
    activated, pulls = zip(*[jax.vjp(jax.nn.gelu, p) for p in pre])
    hidden_out, hidden_normed, hidden_std = norm_forward(activated, hg, hs)
    hidden = [h.astype(bf16) for h in hidden_out]
    out_rel = middle + mm_cols(hidden[0], downs[0]) + mm_cols(hidden[1], downs[1]) + shifts[6:7]
    layer_out = reorder(out_rel.astype(bf16), to_abs, block)

    pair = lambda x: jnp.concatenate([x, swap(x, "sp", 1)], axis=0)
    across = lambda halves: jnp.concatenate([halves[0], swap(halves[1], "sp", 1)], axis=0)
    upstream_pair = pair(upstream)
    g_down = mm_rows(upstream_pair, across(hidden)).astype(bf16)
    grad_w_down = grid.scatter(g_down)

    hidden_grad = [mm(upstream, w) for w in downs]
    act_grad, grad_mid, grad_mid_shift = norm_backward(hidden_grad, hidden_normed, hidden_std, hg)
    pre_grad = [pull(a)[0].astype(bf16) for pull, a in zip(pulls, act_grad)]
    second_grad = mm_cols(pre_grad[0], ups[0]) + mm_cols(pre_grad[1], ups[1])
    (middle_part,), (gain_ffn,), (shift_ffn,) = norm_backward([second_grad], [second_normed], second_std, gains[2:3])
    middle_grad = upstream.astype(f32) + middle_part
    (attn_grad_full,), (gain_attn,), (shift_attn,) = norm_backward([middle_grad], [attn_normed], attn_std, gains[1:2])
    attn_grad_rel = attn_grad_full.astype(bf16)
    attn_grad = reorder(attn_grad_rel, to_abs, block)
    merged_grad = mm_cols(attn_grad, wo).astype(bf16)
    scattered = jnp.stack([merged_grad[:, t * lw : (t + 1) * lw] for t in range(sp)], axis=0)
    scaled_grad = lax.all_to_all(scattered, "sp", 0, 0, tiled=True).reshape(group, lw)

    g_up = mm_rows(pair(second), across(pre_grad)).astype(bf16)
    grad_w_up = grid.scatter(g_up)
    merged_rel = reorder(merged, to_rel, block)
    attn_grad_cols = reorder(attn_grad, sp_rel, oc)
    g_out = mm_rows(pair(merged_rel), across([attn_grad_cols[:, : width // 2], attn_grad_cols[:, width // 2 :]]))
    grad_w_out = grid.scatter_z(grid.scatter_y(grid.scatter_x(g_out)))

    qkv_grad, head_sums = attend_backward(
        hd, 0, tab, seq_spans[0], qkv, keep_col, head_scale, scaled_grad, o_t, lse
    )
    qkv_grad_rel = reorder_rows(qkv_grad, group_order, rows)
    first_part = mm_cols(qkv_grad_rel, wq)
    pieces = [first_part[t * rows : (t + 1) * rows] for t in range(sp)]
    folded = [
        pieces[t].astype(f32) + swap(pieces[t + 1].astype(bf16), "sp", 1).astype(f32) for t in range(0, sp, 2)
    ]
    first_grad = grid.fold(folded, "sp", grid.x_bits)
    (input_part,), (gain_in,), (shift_in,) = norm_backward([first_grad], [first_normed], first_std, gains[0:1])
    grad_tokens = reorder(middle_grad + input_part, to_abs, block)

    g_qkv = mm_rows(firsts_cat, qkv_grad_rel)
    g_mine = grid.scatter_z(grid.scatter_y(g_qkv)).astype(bf16)
    g_blocks = jnp.concatenate(
        [g_mine.reshape(block, 3, lw).transpose(1, 0, 2), jnp.zeros((1, block, lw), bf16)], axis=0
    )
    back = []
    for t in range(sp):
        which = jnp.int32(3)
        for u in range(3):
            which = jnp.where((u * sp + me_s) // 3 == t, u, which)
        back.append(lax.dynamic_slice_in_dim(g_blocks, which, 1, 0))
    home = lax.all_to_all(jnp.concatenate(back, axis=0), "sp", 0, 0, tiled=True)
    grad_w_qkv = jnp.concatenate(
        [lax.dynamic_slice_in_dim(home, (3 * me_s + u) % sp, 1, 0)[0] for u in range(3)], axis=1
    ).astype(f32)

    qkv_sums = jnp.sum(qkv_grad.astype(f32), axis=0)
    zeros = jnp.zeros((2, width), f32)
    bias_sums = lax.dynamic_update_slice(
        zeros, jnp.stack([qkv_sums[:lw], qkv_sums[2 * lw :]]), (0, me_s * lw)
    )
    sum_early = jnp.concatenate(
        [
            reorder(
                jnp.stack(
                    [
                        gain_attn,
                        gain_ffn,
                        jnp.sum(attn_grad_rel.astype(f32), axis=0),
                        shift_attn,
                        shift_ffn,
                        jnp.sum(upstream.astype(f32), axis=0),
                    ]
                ),
                to_abs,
                block,
            ),
            reorder(
                jnp.stack(
                    [
                        jnp.concatenate(grad_mid),
                        jnp.concatenate([jnp.sum(p.astype(f32), axis=0) for p in pre_grad]),
                        jnp.concatenate(grad_mid_shift),
                    ]
                ),
                sp_abs,
                ff // sp,
            ).reshape(3 * ff // width, width),
        ],
        axis=0,
    )
    early = grid.all_sum(sum_early)
    scale_row = lax.dynamic_update_slice(
        jnp.zeros((1, width), f32), head_sums[1:2, :nh], (0, me_s * nh)
    )
    late = grid.all_sum(
        jnp.concatenate(
            [reorder(jnp.stack([gain_in, shift_in]), to_abs, block), bias_sums, scale_row], axis=0
        )
    )
    grad_model_gains = jnp.stack([late[0], early[0], early[1]])
    grad_model_shifts = jnp.stack([late[2], late[3], early[2], late[1], early[3], early[4], early[5]])
    hidden_sums = early[6:].reshape(3, ff)
    return (
        layer_out,
        grad_tokens,
        grad_w_qkv,
        grad_w_out,
        grad_w_up,
        grad_w_down,
        grad_model_gains,
        grad_model_shifts,
        hidden_sums[0],
        hidden_sums[1:3],
        late[4, :heads],
    )


REL, HID, ORD, COLS, WHO, SEND, SLOT, ALONG = 0, 8, 16, 24, 32, 33, 36, 40
LANES = 128


def matchings(sp):
    left = {s: {3 * s + k: (3 * s + k) % sp for k in range(3)} for s in range(sp)}
    rounds = []
    for _ in range(3):
        taken = {}

        def seat(s, seen):
            for b, to in sorted(left[s].items(), key=lambda e: e[1] != s):
                if to not in seen:
                    seen.add(to)
                    if to not in taken or seat(taken[to][0], seen):
                        taken[to] = (s, b)
                        return True
            return False

        for s in range(sp):
            seat(s, set())
        one = [None] * sp
        for to, (s, b) in taken.items():
            one[s] = (b - 3 * s, b // sp, to)
            del left[s][b]
        rounds.append(one)
    return rounds


def tables(dp, sp, ny, nz, rounds):
    out = np.zeros((dp * sp, 128), np.int32)
    for d in range(dp):
        for s in range(sp):
            row = out[d * sp + s]
            where = {}
            for p in range(dp):
                row[REL + p] = ((p % nz) * ny + p // nz) ^ d
                where[row[REL + p]] = p
            for q in range(2 * sp):
                dc, half, dx = q // 4, q // 2 % 2, q % 2
                row[HID + q] = ((dx * 2 + dc) ^ s) * 2 + half
                row[COLS + q] = where[row[HID + q]]
            for t in range(sp):
                row[ORD + t] = s ^ t
            row[WHO] = s
            for k in range(nz):
                row[ALONG + k] = d // ny ^ k
            for m in range(3):
                row[SEND + m] = rounds[m][s][0]
                row[SLOT + m] = next(rounds[m][a][1] for a in range(sp) if rounds[m][a][2] == s)
    return out


def span(index, size):
    return pl.ds(pl.multiple_of(index * size, size), size)


def norm_of(x):
    mean = jnp.mean(x, axis=1, keepdims=True)
    centred = x - mean
    inv_std = lax.rsqrt(jnp.mean(centred * centred, axis=1, keepdims=True) + EPSILON)
    return centred * inv_std, inv_std


def norm_back(incoming, normed, inv_std, gain):
    scaled = incoming * gain
    mean = jnp.mean(scaled, axis=1, keepdims=True)
    along = jnp.mean(scaled * normed, axis=1, keepdims=True)
    return inv_std * (scaled - mean - normed * along)


def down_sum(x):
    return jnp.sum(x, axis=0, keepdims=True)


def whole(shape):
    return pl.BlockSpec(shape, lambda *_: (0,) * len(shape))


def by_rows(rows, cols):
    return pl.BlockSpec((rows, cols), lambda i, *_: (i, 0))


class Order:
    last = ()

    def after(self, deps):
        return tuple(deps) + self.last

    def passed(self, outs):
        self.last = (outs[-1],)
        return outs


ORDER = Order()


def with_rider(body, at, count):
    def both(*refs):
        first, second, total = refs[at], refs[at + 1], refs[at + 2 + count]

        @pl.when(pl.program_id(0) == 0)
        def _():
            total[...] = first[...] + second[...]

        body(*refs[:at], *refs[at + 2 : at + 2 + count], *refs[at + 3 + count :])

    return both


def call(name, body, tab, args, outs, steps=1, in_specs=None, out_specs=None, scratch=(), deps=(), vmem=20, us=0, rider=None):
    in_specs = [whole(a.shape) for a in args] if in_specs is None else in_specs
    out_specs = [whole(s) for s, _ in outs] if out_specs is None else out_specs
    if rider is not None:
        body = with_rider(body, 1 + len(args), len(outs))
        args, outs = list(args) + list(rider), list(outs) + [(rider[0].shape, rider[0].dtype)]
        in_specs = list(in_specs) + [whole(rider[0].shape)] * 2
        out_specs = list(out_specs) + [whole(rider[0].shape)]
    deps = ORDER.after(deps)
    made = pl.pallas_call(
        skipping(body, 1 + len(args), len(deps)),
        grid_spec=pltpu.PrefetchScalarGridSpec(
            num_scalar_prefetch=1,
            grid=(steps,),
            in_specs=list(in_specs) + unread(deps),
            out_specs=list(out_specs),
            scratch_shapes=list(scratch),
        ),
        out_shape=[jax.ShapeDtypeStruct(s, t) for s, t in outs],
        compiler_params=pltpu.CompilerParams(vmem_limit_bytes=vmem << 20),
        cost_estimate=pl.CostEstimate(flops=int(us * 1.1e9) + 1024, bytes_accessed=1024, transcendentals=0),
        name=name,
    )(tab, *args, *deps)
    return ORDER.passed(made)


def part_body(tab, w, *outs):
    width = outs[0].shape[1]
    for m, out in enumerate(outs):
        out[...] = w[:, span(tab[SEND + m], width)]


def join_body(tab, *refs):
    pieces, out = refs[:-1], refs[-1]
    for m, piece in enumerate(pieces):
        for k in range(out.shape[0]):
            out[k, :, span(tab[SLOT + m], piece.shape[1])] = piece[...]


def home_body(tab, p0, p1, p2, late, e0, e1, out, gains, shifts, mid, hid, scale):
    size, width = p0.shape[1], late.shape[1]
    early = e0[...] + e1[...]
    for m, piece in enumerate((p0, p1, p2)):
        out[:, span(tab[SEND + m], size)] = piece[...].astype(f32)
    for row, source in enumerate((late[0:1], early[0:1], early[1:2])):
        gains[row : row + 1, :] = source
    for row, source in enumerate((late[2:3], late[3:4], early[2:3], late[1:2], early[3:4], early[4:5], early[5:6])):
        shifts[row : row + 1, :] = source
    for k in range(mid.shape[1] // width):
        to = slice(k * width, (k + 1) * width)
        mid[:, to] = early[6 + k : 7 + k, :]
        hid[0:1, to] = early[10 + k : 11 + k, :]
        hid[1:2, to] = early[14 + k : 15 + k, :]
    scale[...] = late[4:5, : scale.shape[1]]


def prologue_body(tab, tok, cot, vcol, vrow, gains, shifts, mid, hsh, first_ref, both_ref, up_ref, tokr_ref, vec_ref, hid_ref):
    rows, width = tok.shape
    unit = mid.shape[1] // 8
    valid = vcol[...]
    vec_ref[...] = jnp.zeros_like(vec_ref)
    hid_ref[...] = jnp.zeros_like(hid_ref)
    for p in range(8):
        at, to = span(tab[REL + p], LANES), slice(p * LANES, (p + 1) * LANES)
        tokr_ref[:, to] = tok[:, at]
        vec_ref[0:3, to] = gains[:, at]
        vec_ref[3:10, to] = shifts[:, at]
        at, to = span(tab[HID + p], unit), slice(p * unit, (p + 1) * unit)
        hid_ref[0:1, to] = mid[:, at]
        hid_ref[1:3, to] = hsh[:, at]
    gain, shift = vec_ref[0:1, :], vec_ref[6:7, :]

    def chunk(i, carry):
        at = span(i, 64)
        normed, _ = norm_of(tokr_ref[at, :].astype(f32))
        first_ref[at, :] = (normed * gain + shift).astype(bf16)
        return carry

    lax.fori_loop(0, rows // 64, chunk, 0)
    first_ref[rows:, :] = jnp.broadcast_to(vrow[...], (16, width))
    both_ref[: rows + 16, :] = first_ref[...]
    for p in range(8):
        at, to = span(tab[REL + p], LANES), slice(p * LANES, (p + 1) * LANES)
        masked = cot[:, at].astype(f32) * valid
        up_ref[:, to] = masked.astype(bf16)
        vec_ref[10:11, to] = down_sum(masked)
    both_ref[rows + 16 :, :] = up_ref[...]


def project_body(count, tab, *refs):
    pieces, (w0, w1, shifts, out_ref, keep_ref) = refs[:count], refs[count:]
    rows, depth = out_ref.shape[0], w0.shape[0]
    at = span(tab[WHO], 2 * LANES)
    bias = jnp.concatenate([shifts[0:1, at], jnp.zeros((1, 2 * LANES), f32), shifts[1:2, at]], axis=1)
    for k in range(count):

        @pl.when(pl.program_id(0) == k)
        def _():
            x = pieces[k]
            out_ref[...] = (mm(x[:rows, :depth], w0[...]) + mm(x[:rows, depth:], w1[...]) + bias).astype(bf16)
            keep_ref[...] = x[rows : rows + 16, :rows].astype(f32)[:8]


def middle_body(begin, tab, ret, tok, vec, shards, pair_ref, mid_ref, norm_ref, std_ref, wo, sems):
    width = tok.shape[1]

    def copies(p):
        out = []
        for q in range(8):
            at = tab[HID + q]
            source = shards.at[tab[REL + p] * 4 + at // 2, :, pl.ds(pl.multiple_of(begin + lax.rem(at, 2) * LANES, LANES), LANES)]
            out.append(pltpu.make_async_copy(source, wo.at[pl.ds(p * LANES, LANES), span(tab[COLS + q], LANES)], sems.at[p, q]))
        return out

    @pl.when(pl.program_id(0) == 0)
    def _():
        for p in range(8):
            for copy in copies(p):
                copy.start()

    for p in range(8):
        a = tab[REL + p]
        pair_ref[:, width + p * LANES : width + (p + 1) * LANES] = ret[a // 2, :, span(lax.rem(a, 2), LANES)]

    @pl.when(pl.program_id(0) == 0)
    def _():
        for p in range(8):
            for copy in copies(p):
                copy.wait()

    normed, inv_std = norm_of(mm(pair_ref[:, width:], wo[...]) + vec[5:6, :])
    middle = tok[...].astype(f32) + (normed * vec[1:2, :] + vec[7:8, :])
    norm_ref[...] = normed
    std_ref[...] = inv_std
    mid_ref[...] = middle
    again, _ = norm_of(middle)
    pair_ref[:, :width] = (again * vec[2:3, :] + vec[8:9, :]).astype(bf16)


GELU = 0.7978845608028654
CUBE = 0.044715


def ffn_body(unit, tab, second, upstream, mid, hid, vec, *refs):
    shards, (hown, hsib, pown, psib, sg_ref, lo_ref, sums_ref, upv, dnv, act, slope, back, sems) = refs[0], refs[1:]
    i = pl.program_id(0)
    ff = upv.shape[1]

    def copies(q, which):
        held = (upv, dnv)[which]
        at = tab[HID + q]
        from_cols = pl.ds(pl.multiple_of(which * 2 * unit + lax.rem(at, 2) * unit, unit), unit)
        out = []
        for p in range(8):
            source = shards.at[tab[REL + p] * 4 + at // 2, :, from_cols]
            out.append(pltpu.make_async_copy(source, held.at[pl.ds(p * LANES, LANES), pl.ds(q * unit, unit)], sems.at[which, q, p]))
        return out

    @pl.when(i == 0)
    def _():
        sums_ref[...] = jnp.zeros_like(sums_ref)
        for q in range(8):
            for copy in copies(q, 0):
                copy.start()
        for q in range(8):
            for copy in copies(q, 1):
                copy.start()

    x = second[...]
    total = jnp.zeros((x.shape[0], 1), f32)
    for q in range(8):
        at = slice(q * unit, (q + 1) * unit)

        @pl.when(i == 0)
        def _():
            for copy in copies(q, 0):
                copy.wait()

        pre = mm(x, upv[:, at]) + hid[1:2, at]
        squared = pre * pre
        t = jnp.tanh(pre * (GELU + (GELU * CUBE) * squared))
        one = 0.5 + 0.5 * t
        value = pre * one
        act[:, at] = value
        slope[:, at] = one + 0.5 * pre * (1.0 - t * t) * (GELU + (3 * GELU * CUBE) * squared)
        total = total + jnp.sum(value, axis=1, keepdims=True)
    mean = total / ff
    total = jnp.zeros_like(mean)
    for q in range(8):
        at = slice(q * unit, (q + 1) * unit)
        centred = act[:, at] - mean
        total = total + jnp.sum(centred * centred, axis=1, keepdims=True)
    inv_std = lax.rsqrt(total / ff + EPSILON)
    u = upstream[...]
    m1, m2 = jnp.zeros_like(mean), jnp.zeros_like(mean)
    low = jnp.zeros(mid.shape, f32)
    for q in range(8):
        at = slice(q * unit, (q + 1) * unit)

        @pl.when(i == 0)
        def _():
            for copy in copies(q, 1):
                copy.wait()

        incoming = mm(u, dnv[:, at])
        normed = (act[:, at] - mean) * inv_std
        act[:, at] = normed
        gain = hid[0:1, at]
        held, to = ((hown, at) if q < 4 else (hsib, slice((q - 4) * unit, (q - 3) * unit)))
        hidden = (normed * gain + hid[2:3, at]).astype(bf16)
        held[:, to] = hidden
        low = low + mm_cols(hidden, dnv[:, at])
        along = incoming * normed
        sums_ref[0:1, at] += down_sum(along)
        sums_ref[2:3, at] += down_sum(incoming)
        m1 = m1 + jnp.sum(incoming * gain, axis=1, keepdims=True)
        m2 = m2 + jnp.sum(along * gain, axis=1, keepdims=True)
        back[:, at] = incoming
    m1, m2 = m1 / ff, m2 / ff
    second_grad = jnp.zeros(mid.shape, f32)
    for q in range(8):
        at = slice(q * unit, (q + 1) * unit)
        grad = inv_std * (back[:, at] * hid[0:1, at] - m1 - act[:, at] * m2)
        pre_grad = (grad * slope[:, at]).astype(bf16)
        held, to = ((pown, at) if q < 4 else (psib, slice((q - 4) * unit, (q - 3) * unit)))
        held[:, to] = pre_grad
        sums_ref[1:2, at] += down_sum(pre_grad.astype(f32))
        second_grad = second_grad + mm_cols(pre_grad, upv[:, at])
    sg_ref[...] = second_grad
    out = (mid[...] + low + vec[9:10, :]).astype(bf16)
    for p in range(8):
        lo_ref[:, span(tab[REL + p], LANES)] = out[:, p * LANES : (p + 1) * LANES]


def heads_body(tab, grad, mid, norm, std, up, vec, wo, mg_ref, own_ref, sib_ref, out_ref, sums_ref, scr):
    @pl.when(pl.program_id(0) == 0)
    def _():
        sums_ref[...] = jnp.zeros_like(sums_ref)

    incoming = grad[...]
    again, inv_std = norm_of(mid[...])
    sums_ref[1:2, :] += down_sum(incoming * again)
    sums_ref[4:5, :] += down_sum(incoming)
    middle_grad = up[...].astype(f32) + norm_back(incoming, again, inv_std, vec[2:3, :])
    mg_ref[...] = middle_grad
    normed = norm[...]
    sums_ref[0:1, :] += down_sum(middle_grad * normed)
    sums_ref[3:4, :] += down_sum(middle_grad)
    low = norm_back(middle_grad, normed, std[...], vec[1:2, :]).astype(bf16)
    sums_ref[2:3, :] += down_sum(low.astype(f32))
    scr[...] = low
    for q in range(8):
        held = own_ref if q < 4 else sib_ref
        held[:, (q % 4) * LANES : (q % 4 + 1) * LANES] = scr[:, span(tab[COLS + q], LANES)]
    got = mm_cols(low, wo[...]).astype(bf16)
    for p in range(8):
        a = tab[REL + p]
        out_ref[a // 2, :, span(lax.rem(a, 2), LANES)] = got[:, p * LANES : (p + 1) * LANES]


def turn_body(tab, x0, x1, out):
    tokens = x0.shape[0]
    out[:, :tokens] = x0[...].T
    out[:, tokens:] = x1[...].T


def turn_late_body(tab, x0, both, out):
    tokens = x0.shape[0]
    out[:, :tokens] = x0[...].T
    out[:, tokens:] = both[tokens + 16 :, :].T


def grads_body(counts, widths, tab, *refs):
    ins, (ak, asend, bk, bsend, xt) = refs[:-5], refs[-5:]
    half = bk.shape[0]
    total = sum(widths)
    i = pl.program_id(0)
    at = begin = 0
    for n, (count, wide) in enumerate(zip(counts, widths)):
        xs, (y0, y1) = ins[begin : begin + count], ins[begin + count : begin + count + 2]
        begin += count + 2
        if count == 2:

            @pl.when(i == 4 * n)
            def _():
                turn_body(tab, *xs, xt)

        left = xt if count == 2 else xs[0]
        for q in range(4):

            @pl.when(i == 4 * n + q)
            def _():
                g = mm(left[...], jnp.concatenate([y0[...], y1[...]], axis=0)).astype(bf16)
                if q < 2:
                    (ak, asend)[q][:, at : at + wide] = g
                else:
                    to = slice((q - 2) * total + at, (q - 2) * total + at + wide)
                    bk[:, to] = g[:half]
                    bsend[:, to] = g[half:]

        at += wide


def groups_body(count, tab, *refs):
    pieces, (grad, keep, send, acc) = refs[:count], refs[count:]
    i = pl.program_id(0)
    half = keep.shape[0]
    rows = grad.shape[0]
    for k in range(count):

        @pl.when(i == k)
        def _():
            got = mm(pieces[k][:rows, :].T, grad[...])
            acc[...] = got if k == 0 else acc[...] + got

    @pl.when(i == count - 1)
    def _():
        keep[...] = acc[:half]
        send[...] = acc[half:].astype(bf16)


def fold_body(tab, ak, ra, bk, rb, x0, a2k, a2s, b2k, b2s, y0):
    y0[...] = x0[...]
    rows, cols = b2k.shape
    a = ak[...].astype(f32) + ra[...].astype(f32)
    a2k[...] = a[:rows].astype(bf16)
    a2s[...] = a[rows:].astype(bf16)
    b = bk[...].astype(f32) + rb[...].astype(f32)
    b2k[...] = b[:, :cols].astype(bf16)
    b2s[...] = b[:, cols:].astype(bf16)


def spread_body(tab, ak, ra, bk, rb, g, r, keep, *sends):
    rows, cols = keep.shape[0], ak.shape[1]
    at = 0
    for mine, theirs in ((ak, ra), (bk, rb), (g, r)):
        total = mine[...].astype(f32) + theirs[...].astype(f32)
        to = slice(at, at + total.shape[1])
        at += total.shape[1]
        keep[:, to] = total[:rows]
        for n, send in enumerate(sends, 1):
            send[:, to] = total[n * rows : (n + 1) * rows].astype(bf16)


def gathered_body(widths, tab, keep, r1, r2, r3, low, *refs):
    outs, pieces, (wide_low, total) = refs[: len(widths)], refs[len(widths) : -2], refs[-2:]
    wide_low[...] = low[...].astype(f32)
    total[...] = keep[...] + r1[...].astype(f32) + r2[...].astype(f32) + r3[...].astype(f32)
    half = sum(widths)
    at = 0
    for out, wide in zip(outs, widths):
        out[:, :wide] = total[:, at : at + wide]
        out[:, wide:] = total[:, half + at : half + at + wide]
        at += wide
    for m, piece in enumerate(pieces):
        size = piece.shape[1]
        piece[...] = total[:, pl.ds(pl.multiple_of(2 * half + tab[SLOT + m] * size, size), size)].astype(bf16)


def spill_body(unit, tab, xt, own, sib, out):
    tokens, width = own.shape[0], xt.shape[0]
    for half, y in enumerate((own, sib)):

        @pl.when(pl.program_id(0) // 4 == half)
        def _():
            g = mm(xt[:, :tokens], y[...]).astype(bf16)
            at = tab[HID + pl.program_id(0)]
            for p in range(8):
                out[tab[REL + p] * 4 + at // 2, :, span(lax.rem(at, 2), unit)] = g[p * LANES : (p + 1) * LANES]


def scatter_weights(grid, tab, rows, sets, widths, tag, rider=None):
    total = sum(widths)
    args, specs = [], []
    for n, (xs, y0, y1) in enumerate(sets):
        wide = widths[n]
        tokens = y0[0].shape[0]
        for x, part in xs:
            args.append(x)
            specs.append(whole(x.shape) if part is None else pl.BlockSpec((tokens, rows), lambda *_, part=part: (0, part)))
        for y, begin in (y0, y1):
            args.append(y)
            specs.append(pl.BlockSpec((tokens, wide), lambda i, *_, n=n, begin=begin: (0, begin + jnp.clip(i - 4 * n, 0, 3))))
    outs = [((rows, total), bf16)] * 2 + [((rows // 2, 2 * total), bf16)] * 2
    ak, asend, bk, bsend, *carried = call(
        "grads_" + tag, functools.partial(grads_body, [len(xs) for xs, _, _ in sets], widths), tab, args, outs,
        steps=4 * len(sets), in_specs=specs, scratch=[pltpu.VMEM((rows, 2 * tokens), bf16)], vmem=28, us=6 * len(sets), rider=rider,
    )
    ra, rb = swap(asend, "sp", 2), swap(bsend, "dp", 1)
    rider, ships = yield carried
    quarter = [((rows // 2, total), bf16)] * 4 + [(x.shape, x.dtype) for x in ships]
    a2k, a2s, b2k, b2s, *carried = call("fold_" + tag, fold_body, tab, [ak, ra, bk, rb] + ships, quarter, vmem=34, rider=rider)
    ra, rb = swap(a2s, "dp", 1), swap(b2s, "sp", 2)
    deps = yield carried + [ra, rb]
    (g, r), size = deps
    shard = (rows // 8, 2 * total + g.shape[1])
    keep, *sends = call("spread_" + tag, spread_body, tab, [a2k, ra, b2k, rb, g, r], [(shard, f32)] + [(shard, bf16)] * 3)
    received = [swap(x, "dp", b) for x, b in zip(sends, grid.z_bits)]
    rider, low = yield
    yield call(
        "sum_" + tag, functools.partial(gathered_body, widths), tab, [keep] + received + [low],
        [((rows // 8, 2 * w), f32) for w in widths] + [((rows // 8, size), bf16)] * 3 + [(low.shape, f32)],
        scratch=[pltpu.VMEM(shard, f32)], rider=rider,
    )


def along_z(grid, x):
    lines = [[y + grid.ny * k for k in range(grid.nz)] for y in range(grid.ny)]
    return lax.all_to_all(x, "dp", 0, 0, tiled=True, axis_index_groups=lines)


def rows_body(tab, got, out):
    rows = got.shape[1]
    for k in range(got.shape[0]):
        out[k * rows : (k + 1) * rows, :] = got[tab[ALONG + k]]


def first_grad_body(tab, g, wy0, wy1, mine, cross, far):
    i = pl.program_id(0)
    got = jnp.concatenate([mm_cols(g[...], wy0[...]), mm_cols(g[...], wy1[...])], axis=1)
    rows = g.shape[0]

    @pl.when(i == 0)
    def _():
        mine[...] = got

    @pl.when(i == 1)
    def _():
        cross[:rows] = got.astype(bf16)

    @pl.when(i == 2)
    def _():
        far[...] = got

    @pl.when(i == 3)
    def _():
        cross[rows:] = got.astype(bf16)


def relay_body(tab, far, theirs, send, out, sent):
    sent[...] = send[...]
    out[...] = (far[...] + theirs[...].astype(f32)).astype(bf16)


def final_body(tab, mine, theirs, crossed, tok, mg, vec, s0, out_ref, late_ref, acc, note):
    i = pl.program_id(0)
    width = tok.shape[1]

    @pl.when(i == 0)
    def _():
        acc[...] = jnp.zeros_like(acc)

    incoming = mine[...] + theirs[...].astype(f32) + crossed[...].astype(f32)
    normed, inv_std = norm_of(tok[...].astype(f32))
    acc[0:1, :] += down_sum(incoming * normed)
    acc[1:2, :] += down_sum(incoming)
    total = mg[...] + norm_back(incoming, normed, inv_std, vec[0:1, :])
    for p in range(8):
        out_ref[:, span(tab[REL + p], LANES)] = total[:, p * LANES : (p + 1) * LANES]

    @pl.when(i == pl.num_programs(0) - 1)
    def _():
        note[...] = jnp.zeros_like(note)
        for p in range(8):
            cols = slice(p * LANES, (p + 1) * LANES)
            note[pl.ds(tab[REL + p], 1), :] = acc[0:1, cols]
            note[pl.ds(8 + tab[REL + p], 1), :] = acc[1:2, cols]
        for e in range(2):
            note[16 + e : 17 + e, :] = s0[0:1, e * LANES : (e + 1) * LANES]
            note[18 + e : 19 + e, :] = s0[0:1, (4 + e) * LANES : (5 + e) * LANES]
        note[20:21, :] = s0[1:2, :LANES]
        for n in range(late_ref.shape[0]):
            late_ref[n] = note[...]


def totals_body(sp, tab, got, out):
    out[...] = jnp.zeros_like(out)
    count = got.shape[0]
    total = got[0, :16]
    for n in range(1, count):
        total = total + got[n, :16]
    for p in range(8):
        cols = slice(p * LANES, (p + 1) * LANES)
        out[0:1, cols] = total[p : p + 1]
        out[1:2, cols] = total[8 + p : 9 + p]
    heads = jnp.zeros((1, LANES), f32)
    lane = lax.broadcasted_iota(jnp.int32, (1, LANES), 1)
    for s in range(sp):
        mine = got[s, 16:24]
        for n in range(s + sp, count, sp):
            mine = mine + got[n, 16:24]
        for e in range(2):
            cols = slice((2 * s + e) * LANES, (2 * s + e + 1) * LANES)
            out[2:3, cols] = mine[e : e + 1]
            out[3:4, cols] = mine[2 + e : 3 + e]
        for h in range(4):
            value = jnp.sum(jnp.where(lane == h, mine[4:5], 0.0))
            heads = jnp.where(lane == 4 * s + h, value, heads)
    out[4:5, :LANES] = heads


def pack_body(tab, sums, vec, hid, out_ref):
    width, unit = sums.shape[1], hid.shape[1] // 8
    out_ref[...] = jnp.zeros_like(out_ref)
    for p in range(8):
        to, at = span(tab[REL + p], LANES), slice(p * LANES, (p + 1) * LANES)
        out_ref[0:5, to] = sums[0:5, at]
        out_ref[5:6, to] = vec[10:11, at]
    for v in range(3):
        for q in range(8):
            unit_at = tab[HID + q]
            row, col = 6 + 4 * v + unit_at // 2, lax.rem(unit_at, 2)
            out_ref[pl.ds(row, 1), span(col, unit)] = hid[v : v + 1, q * unit : (q + 1) * unit]


def fast_layer(
    tokens,
    seq_spans,
    valid_mask,
    cotangent,
    w_qkv,
    w_out,
    w_up,
    w_down,
    model_gains,
    model_shifts,
    mid_gain,
    hidden_shifts,
    head_scale,
):
    dp, sp = lax.axis_size("dp"), lax.axis_size("sp")
    grid = Grid(dp, sp)
    rows, width = tokens.shape
    group = rows * sp
    heads = head_scale.shape[0]
    block = width // dp
    ff = mid_gain.shape[0]
    unit = ff // 8
    shard_lanes = 2 * LANES
    step = rows // 2

    rounds = matchings(sp)
    device = lax.axis_index("dp") * sp + lax.axis_index("sp")
    tab = lax.dynamic_slice_in_dim(jnp.asarray(tables(dp, sp, grid.ny, grid.nz, rounds)), device, 1, 0)[0]
    spans = seq_spans[0]
    forth = [[(s, rounds[m][s][2]) for s in range(sp)] for m in range(3)]
    back_to = [[(t, s) for s, t in pairs] for pairs in forth]
    carry = lambda x, pairs: x if all(a == b for a, b in pairs) else lax.ppermute(x, "sp", pairs)

    ORDER.last = ()
    shards = lax.all_gather(jnp.concatenate([w_up, w_down, w_out], axis=1), ("dp", "sp"), axis=0)
    sent = call("part", part_body, tab, [w_qkv], [((block, shard_lanes), bf16)] * 3)
    moved = [carry(x, pairs) for x, pairs in zip(sent, forth)]
    wq_lines = along_z(grid, call("join", join_body, tab, moved, [((grid.nz, block, 3 * shard_lanes), bf16)])[0])
    vcol = valid_mask.astype(f32)[:, None]
    vrow = jnp.pad(valid_mask.astype(bf16), (0, width - rows))[None]
    first, both, upstream, tokr, vec, hid = call(
        "prologue", prologue_body, tab,
        [tokens, cotangent, vcol, vrow, model_gains, model_shifts, mid_gain[None], hidden_shifts],
        [((rows + 16, width), bf16), ((2 * rows + 16, width), bf16), ((rows, width), bf16), ((rows, width), bf16), ((16, width), f32), ((8, ff), f32)],
    )
    beyond = swap(first, "sp", 2)
    theirs = swap(both, "sp", 1)
    upstream_t = call("turn", turn_late_body, tab, [upstream, theirs], [((width, 2 * rows), bf16)], deps=(beyond,))[0]
    wq0 = call("rows_qkv", rows_body, tab, [wq_lines], [((grid.nz * block, 3 * shard_lanes), bf16)])[0]
    wq1 = swap(wq0, "dp", 1)
    firsts = [first, theirs, beyond, swap(beyond, "sp", 1)]
    qkv, keep = call(
        "project", functools.partial(project_body, sp), tab, firsts + [wq0, wq1, model_shifts],
        [((group, 3 * shard_lanes), bf16), ((8, group), f32)], steps=sp,
        out_specs=[by_rows(rows, 3 * shard_lanes), pl.BlockSpec((8, rows), lambda i, *_: (0, i))],
    )
    hd = Heads(4, heads // sp, 0, (0, 1, 2), ORD, WHO, sp, rows)
    scaled, o_t, lse = ORDER.passed(attend_forward(hd, tab, spans, qkv, keep, head_scale, deps=ORDER.last))
    returned = lax.all_to_all(scaled.reshape(sp, rows, shard_lanes), "sp", 0, 0, tiled=True)

    ret_spec = pl.BlockSpec((sp, step, shard_lanes), lambda i, *_: (0, i, 0))
    anywhere = pl.BlockSpec(memory_space=pl.ANY)
    pair, middle, attn_normed, attn_std, wo = call(
        "to_middle", functools.partial(middle_body, 2 * w_up.shape[1]), tab, [returned, tokr, vec, shards],
        [((rows, 2 * width), bf16), ((rows, width), f32), ((rows, width), f32), ((rows, 1), f32), ((width, width), bf16)],
        steps=2,
        in_specs=[ret_spec, by_rows(step, width), whole(vec.shape), anywhere],
        out_specs=[by_rows(step, 2 * width)] + [by_rows(step, width)] * 2 + [by_rows(step, 1), whole((width, width))],
        scratch=[pltpu.SemaphoreType.DMA((8, 8))], vmem=62,
    )
    pair_sib = swap(pair, "sp", 1)
    hid_own, hid_sib, pre_own, pre_sib, second_grad, layer_out, hidden_sums = call(
        "ffn", functools.partial(ffn_body, unit), tab, [pair, upstream, middle, hid, vec, shards],
        [((rows, ff // 2), bf16)] * 4 + [((rows, width), f32), ((rows, width), bf16), ((8, ff), f32)],
        steps=2,
        in_specs=[by_rows(step, width)] * 3 + [whole(hid.shape), whole(vec.shape)] + [anywhere],
        out_specs=[by_rows(step, ff // 2)] * 4 + [by_rows(step, width)] * 2 + [whole((8, ff))],
        scratch=[pltpu.VMEM((width, ff), bf16)] * 2 + [pltpu.VMEM((step, ff), f32)] * 3 + [pltpu.SemaphoreType.DMA((2, 8, 8))],
        vmem=63, us=37,
    )

    pre_across = swap(pre_sib, "sp", 1)
    spilled = call(
        "spill", functools.partial(spill_body, unit), tab, [upstream_t, hid_own, hid_sib], [((dp * sp, block, 2 * unit), bf16)], steps=8,
        in_specs=[pl.BlockSpec((width, rows), lambda *_: (0, 0)),
                  pl.BlockSpec((rows, unit), lambda i, *_: (0, jnp.clip(i, 0, 3))),
                  pl.BlockSpec((rows, unit), lambda i, *_: (0, jnp.clip(i - 4, 0, 3)))],
        vmem=62,
    )[0]
    down_part = lax.psum_scatter(spilled, ("dp", "sp"), scatter_dimension=0, tiled=True)[0]
    middle_grad, attn_own, attn_sib, back, sums = call(
        "to_heads", heads_body, tab, [second_grad, middle, attn_normed, attn_std, upstream, vec, wo],
        [((rows, width), f32)] + [((rows, width // 2), bf16)] * 2 + [((sp, rows, shard_lanes), bf16), ((8, width), f32)],
        steps=2,
        in_specs=[by_rows(step, width)] * 3 + [by_rows(step, 1), by_rows(step, width), whole(vec.shape), whole(wo.shape)],
        out_specs=[by_rows(step, width)] + [by_rows(step, width // 2)] * 2 + [ret_spec, whole((8, width))],
        scratch=[pltpu.VMEM((step, width), bf16)],
        vmem=62,
    )
    attn_across = swap(attn_sib, "sp", 1)
    early = call("pack", pack_body, tab, [sums, vec, hidden_sums], [((24, width), f32)])[0]
    early = (early, swap(early, "sp", 1))

    grads_in = lax.all_to_all(back, "sp", 0, 0, tiled=True).reshape(group, shard_lanes)
    up_sums = scatter_weights(
        grid, tab, width,
        [([(pair, 0), (pair_sib, 0)], (pre_own, 0), (pre_across, 0)), ([(pair, 1), (pair_sib, 1)], (attn_own, 0), (attn_across, 0))],
        (unit, LANES), "up", rider=early,
    )
    (early,) = next(up_sums)
    early = (early, swap(early, "sp", 2))
    wide = 3 * shard_lanes
    qkv_grad, head_sums = ORDER.passed(
        attend_backward(hd, 0, tab, spans, qkv, keep, head_scale, grads_in, o_t, lse, deps=ORDER.last)
    )
    mine, cross, far = call(
        "first_grad", first_grad_body, tab, [qkv_grad, wq0, wq1],
        [((rows, width), f32), ((2 * rows, width), bf16), ((rows, width), f32)], steps=sp,
        in_specs=[by_rows(rows, wide), whole(wq0.shape), whole(wq1.shape)],
        out_specs=[whole((rows, width)), whole((2 * rows, width)), whole((rows, width))],
    )
    cross, early, *second_up = up_sums.send((early, [cross]))
    theirs = swap(cross, "sp", 1)
    keep_rows, send = call(
        "group_grads", functools.partial(groups_body, sp), tab, firsts + [qkv_grad],
        [((width // 2, wide), f32), ((width // 2, wide), bf16)], steps=sp,
        in_specs=[whole(f.shape) for f in firsts] + [by_rows(rows, wide)],
        scratch=[pltpu.VMEM((width, wide), f32)], vmem=30,
    )
    relayed, send = call(
        "relay", relay_body, tab, [far, theirs, send], [((rows, width), bf16), (send.shape, bf16)],
        in_specs=[whole(far.shape), pl.BlockSpec((rows, width), lambda *_: (1, 0)), whole(send.shape)],
    )
    crossed, other_rows = swap(relayed, "sp", 2), swap(send, "dp", 1)
    early = (early, swap(early, "dp", 1))
    grad_tokens, late, early = call(
        "to_tokens", final_body, tab, [mine, theirs, crossed, tokr, middle_grad, vec, head_sums],
        [((rows, width), f32), ((dp * sp, 24, LANES), f32)], steps=2,
        in_specs=[by_rows(step, width)] * 5 + [whole(vec.shape), whole((8, wide))],
        out_specs=[by_rows(step, width), whole((dp * sp, 24, LANES))],
        scratch=[pltpu.VMEM((8, width), f32), pltpu.VMEM((24, LANES), f32)], rider=early, deps=(other_rows, *second_up),
    )
    early = (early, swap(early, "dp", 2))
    late = lax.all_to_all(late, ("dp", "sp"), 0, 0, tiled=True)
    up_sums.send(((keep_rows, other_rows), shard_lanes))
    late = call("totals", functools.partial(totals_body, sp), tab, [late], [((8, width), f32)])[0]
    grad_w_up, grad_w_out, *sent, grad_w_down, early = up_sums.send((early, down_part))
    along = swap(early, "dp", 4)
    got = [carry(x, pairs) for x, pairs in zip(sent, back_to)]
    grad_w_qkv, gain_sums, shift_sums, mid_sums, hid_sums, scale_sums = call(
        "home", home_body, tab, got + [late, early, along],
        [((block, 3 * shard_lanes), f32), ((3, width), f32), ((7, width), f32), ((1, ff), f32), ((2, ff), f32), ((1, heads), f32)],
    )
    return (
        layer_out,
        grad_tokens,
        grad_w_qkv,
        grad_w_out,
        grad_w_up,
        grad_w_down,
        gain_sums,
        shift_sums,
        mid_sums[0],
        hid_sums,
        scale_sums[0],
    )


def per_device(*arrays):
    dp, sp = lax.axis_size("dp"), lax.axis_size("sp")
    (rows, width), heads, ff = arrays[0].shape, arrays[12].shape[0], arrays[10].shape[0]
    if (dp, sp) == (8, 4) and width == 8 * LANES and heads * HEAD == width and ff == 4 * width and rows == 512:
        return fast_layer(*arrays)
    return general_layer(*arrays)


def solution(mesh):
    rows = P(("dp", "sp"), None)
    placed = (rows, P("dp", None), P(("dp", "sp")), rows) + (P("dp", "sp"),) * 4 + (P(),) * 5
    return jax.shard_map(
        per_device,
        mesh=mesh,
        in_specs=placed,
        out_specs=(rows, rows) + (P("dp", "sp"),) * 4 + (P(),) * 5,
        check_vma=False,
    )
```

```python
import functools

import jax
import jax.numpy as jnp
import numpy as np
from jax import lax
from jax.experimental import pallas as pl
from jax.experimental.pallas import tpu as pltpu
from jax.sharding import PartitionSpec as P

EPSILON = 1e-05
MASKED = -1e30
HEAD = 64
bf16 = jnp.bfloat16
f32 = jnp.float32


def mm(a, b):
    return lax.dot_general(a, b, (((1,), (0,)), ((), ())), preferred_element_type=f32)


def mm_rows(a, b):
    return lax.dot_general(a, b, (((0,), (0,)), ((), ())), preferred_element_type=f32)


def mm_cols(a, b):
    return lax.dot_general(a, b, (((1,), (1,)), ((), ())), preferred_element_type=f32)


def skipping(kernel, at, count):
    return lambda *refs: kernel(*refs[:at], *refs[at + count :])


def unread(deps):
    return [pl.BlockSpec(memory_space=pl.ANY)] * len(deps)


def lanes_of(x, h):
    lane = lax.broadcasted_iota(jnp.int32, x.shape, 1) // HEAD
    return jnp.where(lane == h, x, jnp.zeros_like(x))


def segment_of(spans, places):
    count, end = jnp.zeros_like(places), jnp.int32(0)
    for k in range(spans.shape[0]):
        end = end + spans[k]
        count = count + (places >= end).astype(jnp.int32)
    return count


class Heads:
    def __init__(self, nh, local, first, blocks, order_at, who_at, parts, rows):
        self.nh, self.local, self.first, self.blocks = nh, local, first, blocks
        self.order_at, self.who_at, self.parts, self.rows = order_at, who_at, parts, rows
        self.bq, self.bk = min(512, rows), min(256, rows)

    def place(self, tab, row):
        return tab[self.order_at + row // self.rows] * self.rows + row % self.rows


def keys_of(hd, tab, spans, keep_ref, kseg):
    for j in range(hd.parts):
        at = pl.ds(pl.multiple_of(tab[hd.order_at + j] * hd.rows, hd.rows), hd.rows)
        places = j * hd.rows + lax.broadcasted_iota(jnp.int32, (hd.rows, 1), 0)
        kseg[at, :] = jnp.where(keep_ref[:, at].T[:, 0:1] > 0.5, segment_of(spans, places), -1)


def visible(hd, i, j, spans, kseg, at):
    bq, bk = hd.bq, hd.bk
    kpos = j * bk + lax.broadcasted_iota(jnp.int32, (bk, bq), 0)
    qpos = i * bq + lax.broadcasted_iota(jnp.int32, (bk, bq), 1)
    qseg = segment_of(spans, i * bq + lax.broadcasted_iota(jnp.int32, (1, bq), 1))
    return (kseg[at, :] == qseg) & (kpos <= qpos)


def each_block(hd, tab, spans, i, body):
    bq, bk = hd.bq, hd.bk
    first = segment_of(spans, i * bq)

    def step(j, carry):
        at = pl.ds(pl.multiple_of(hd.place(tab, j * bk), bk), bk)
        pl.when(first <= segment_of(spans, (j + 1) * bk - 1))(lambda: body(j, at))
        return carry

    lax.fori_loop(0, ((i + 1) * bq - 1) // bk + 1, step, 0)


def fwd_kernel(hd, tab, spans, q_ref, k_ref, v_ref, keep_ref, hs_ref, scaled_ref, o_ref, lse_ref,
               kseg, vms, sscr, mpart, lpart, acc):
    nh, bq, bk = hd.nh, hd.bq, hd.bk
    i = pl.program_id(0)

    @pl.when(i == 0)
    def _():
        for h in range(nh):
            vms[h] = lanes_of(v_ref[...], h)
        keys_of(hd, tab, spans, keep_ref, kseg)

    qs = q_ref[...] * bf16(0.125)
    qm = [lanes_of(qs, h) for h in range(nh)]
    mpart[...] = jnp.full_like(mpart, MASKED)
    lpart[...] = jnp.zeros_like(lpart)
    acc[...] = jnp.zeros_like(acc)

    def one(j, at):
        kb = k_ref[at, :]
        mask = visible(hd, i, j, spans, kseg, at)
        for h in range(nh):
            s = jnp.where(mask, mm_cols(kb, qm[h]), MASKED)
            sscr[h, at, :] = s
            mpart[h] = jnp.maximum(mpart[h], jnp.max(s.reshape(bk // 8, 8, bq), axis=0))

    each_block(hd, tab, spans, i, one)
    ms = [jnp.max(mpart[h], axis=0, keepdims=True) for h in range(nh)]

    def two(j, at):
        pts = []
        for h in range(nh):
            p = jnp.exp(sscr[h, at, :] - ms[h])
            lpart[h] += jnp.sum(p.reshape(bk // 8, 8, bq), axis=0)
            pts.append(p.astype(bf16).T)
        acc[...] += mm(
            jnp.concatenate(pts, axis=1),
            jnp.concatenate([vms[h, at, :] for h in range(nh)], axis=0),
        )

    each_block(hd, tab, spans, i, two)
    out_t = acc[...].T
    parts = []
    for h in range(nh):
        rows = slice(h * HEAD, (h + 1) * HEAD)
        total = jnp.sum(lpart[h], axis=0, keepdims=True)
        result = out_t[rows, :] * (1.0 / total)
        o_ref[rows, :] = result
        parts.append(result * hs_ref[0, tab[hd.who_at] * hd.local + hd.first + h])
        lse_ref[h : h + 1, :] = ms[h] + jnp.log(total)
    scaled_ref[...] = jnp.concatenate(parts, axis=0).T.astype(bf16)


def head_specs(hd, n, w):
    q, k, v = hd.blocks
    bq = hd.bq
    return [
        pl.BlockSpec((bq, w), lambda i, t, s: (hd.place(t, i * bq) // bq, q)),
        pl.BlockSpec((n, w), lambda i, t, s: (0, k)),
        pl.BlockSpec((n, w), lambda i, t, s: (0, v)),
    ]


def attend_forward(hd, tab, spans, qkv, keep, head_scale, deps=()):
    n, nh, w = qkv.shape[0], hd.nh, hd.nh * HEAD
    bq = hd.bq
    return pl.pallas_call(
        skipping(functools.partial(fwd_kernel, hd), 7, len(deps)),
        grid_spec=pltpu.PrefetchScalarGridSpec(
            num_scalar_prefetch=2,
            grid=(n // bq,),
            in_specs=head_specs(hd, n, w)
            + [pl.BlockSpec((8, n), lambda i, t, s: (0, 0)), pl.BlockSpec(memory_space=pltpu.SMEM)]
            + unread(deps),
            out_specs=[
                pl.BlockSpec((bq, w), lambda i, t, s: (i, 0)),
                pl.BlockSpec((w, bq), lambda i, t, s: (0, i)),
                pl.BlockSpec((8, bq), lambda i, t, s: (0, i)),
            ],
            scratch_shapes=[
                pltpu.VMEM((n, 1), jnp.int32),
                pltpu.VMEM((nh, n, w), bf16),
                pltpu.VMEM((nh, n, bq), f32),
                pltpu.VMEM((nh, 8, bq), f32),
                pltpu.VMEM((nh, 8, bq), f32),
                pltpu.VMEM((bq, w), f32),
            ],
        ),
        out_shape=[
            jax.ShapeDtypeStruct((n, w), bf16),
            jax.ShapeDtypeStruct((w, n), f32),
            jax.ShapeDtypeStruct((8, n), f32),
        ],
        compiler_params=pltpu.CompilerParams(vmem_limit_bytes=60 << 20),
        cost_estimate=pl.CostEstimate(flops=nh * n * n * HEAD * 38, bytes_accessed=1024, transcendentals=0),
        name="attend_forward",
    )(tab, spans, qkv, qkv, qkv, keep, head_scale[None], *deps)


def bwd_kernel(hd, tab, spans, q_ref, k_ref, v_ref, keep_ref, hs_ref, sg_ref, o_ref, lse_ref,
               grad_ref, sums_ref, kseg, dk, dv, dq, gacc, kms):
    nh, bq, bk = hd.nh, hd.bq, hd.bk
    i = pl.program_id(0)
    n, w = k_ref.shape[0], nh * HEAD

    @pl.when(i == 0)
    def _():
        dk[...] = jnp.zeros_like(dk)
        dv[...] = jnp.zeros_like(dv)
        gacc[...] = jnp.zeros_like(gacc)
        for h in range(nh):
            kms[h] = lanes_of(k_ref[...], h)
        keys_of(hd, tab, spans, keep_ref, kseg)

    qs = q_ref[...] * bf16(0.125)
    qm = [lanes_of(qs, h) for h in range(nh)]
    scales = [hs_ref[0, tab[hd.who_at] * hd.local + hd.first + h] for h in range(nh)]
    sg = sg_ref[...].astype(f32)
    lane = lax.broadcasted_iota(jnp.int32, (1, w), 1) // HEAD
    scale_row = jnp.zeros((1, w), f32)
    for h in range(nh):
        scale_row = jnp.where(lane == h, scales[h], scale_row)
    grads = (sg * scale_row).astype(bf16)
    dom = [lanes_of(grads, h) for h in range(nh)]
    o = o_ref[...]
    gacc[...] += sg.T * o
    weighed = grads.astype(f32).T * o
    delta = [jnp.sum(weighed[h * HEAD : (h + 1) * HEAD, :], axis=0, keepdims=True) for h in range(nh)]
    lse = [lse_ref[h : h + 1, :] for h in range(nh)]
    qcat = jnp.concatenate(qm, axis=0)
    docat = jnp.concatenate(dom, axis=0)
    dq[...] = jnp.zeros_like(dq)

    def block(j, at):
        kb = k_ref[at, :]
        vb = v_ref[at, :]
        mask = visible(hd, i, j, spans, kseg, at)
        ps, dss, dsts = [], [], []
        for h in range(nh):
            p = jnp.where(mask, jnp.exp(mm_cols(kb, qm[h]) - lse[h]), 0.0)
            ds = (p * (mm_cols(vb, dom[h]) - delta[h])).astype(bf16)
            ps.append(p.astype(bf16))
            dsts.append(ds.T)
            dss.append(ds)
        dv[at, :] += mm(jnp.concatenate(ps, axis=1), docat)
        dk[at, :] += mm(jnp.concatenate(dss, axis=1), qcat)
        dq[...] += mm(
            jnp.concatenate(dsts, axis=1),
            jnp.concatenate([kms[h, at, :] for h in range(nh)], axis=0),
        )

    each_block(hd, tab, spans, i, block)
    mine = hd.place(tab, i * bq)
    grad_ref[pl.ds(pl.multiple_of(mine, bq), bq), 0:w] = (dq[...] * 0.125).astype(bf16)

    @pl.when(i == n // bq - 1)
    def _():
        grad_ref[:, w : 2 * w] = dk[...].astype(bf16)
        grad_ref[:, 2 * w : 3 * w] = dv[...].astype(bf16)
        place = lax.broadcasted_iota(jnp.int32, (1, 3 * w), 1)
        gains = jnp.zeros((1, 3 * w), f32)
        for h in range(nh):
            gains = jnp.where(place == h, jnp.sum(gacc[h * HEAD : (h + 1) * HEAD, :]), gains)
        sums_ref[...] = jnp.zeros_like(sums_ref)
        sums_ref[0:1, :] = jnp.sum(grad_ref[...].astype(f32), axis=0, keepdims=True)
        sums_ref[1:2, :] = gains


def attend_backward(hd, part, tab, spans, qkv, keep, head_scale, scaled_grad, o_t, lse, deps=()):
    n, nh, w = qkv.shape[0], hd.nh, hd.nh * HEAD
    bq = hd.bq
    return pl.pallas_call(
        skipping(functools.partial(bwd_kernel, hd), 10, len(deps)),
        grid_spec=pltpu.PrefetchScalarGridSpec(
            num_scalar_prefetch=2,
            grid=(n // bq,),
            in_specs=head_specs(hd, n, w)
            + [
                pl.BlockSpec((8, n), lambda i, t, s: (0, 0)),
                pl.BlockSpec(memory_space=pltpu.SMEM),
                pl.BlockSpec((bq, w), lambda i, t, s: (i, part)),
                pl.BlockSpec((w, bq), lambda i, t, s: (0, i)),
                pl.BlockSpec((8, bq), lambda i, t, s: (0, i)),
            ]
            + unread(deps),
            out_specs=[
                pl.BlockSpec((n, 3 * w), lambda i, t, s: (0, 0)),
                pl.BlockSpec((8, 3 * w), lambda i, t, s: (0, 0)),
            ],
            scratch_shapes=[
                pltpu.VMEM((n, 1), jnp.int32),
                pltpu.VMEM((n, w), f32),
                pltpu.VMEM((n, w), f32),
                pltpu.VMEM((bq, w), f32),
                pltpu.VMEM((w, bq), f32),
                pltpu.VMEM((nh, n, w), bf16),
            ],
        ),
        out_shape=[
            jax.ShapeDtypeStruct((n, 3 * w), bf16),
            jax.ShapeDtypeStruct((8, 3 * w), f32),
        ],
        compiler_params=pltpu.CompilerParams(vmem_limit_bytes=60 << 20),
        cost_estimate=pl.CostEstimate(flops=nh * n * n * HEAD * 50, bytes_accessed=1024, transcendentals=0),
        name="attend_backward",
    )(tab, spans, qkv, qkv, qkv, keep, head_scale[None], scaled_grad, o_t, lse, *deps)


def swap(x, axis, bits):
    return lax.ppermute(x, axis, [(i, i ^ bits) for i in range(lax.axis_size(axis))])


def reorder(x, idx, width):
    rows, cols = x.shape
    return jnp.take(x.reshape(rows, cols // width, width), idx, axis=1).reshape(rows, cols)


def reorder_rows(x, idx, height):
    rows, cols = x.shape
    return jnp.take(x.reshape(rows // height, height, cols), idx, axis=0).reshape(rows, cols)


class Grid:
    def __init__(self, dp, sp):
        self.dp, self.sp = dp, sp
        self.nx = max(sp // 2, 1)
        self.ny = self.nx if dp % self.nx == 0 else 1
        self.nz = dp // self.ny
        self.z_bits = [self.ny * k for k in range(1, self.nz)]
        self.y_bits = list(range(1, self.ny))
        self.x_bits = [2 * k for k in range(1, self.nx)]

    def gather_z(self, w):
        return jnp.concatenate([w] + [swap(w, "dp", b) for b in self.z_bits], axis=0)

    def gather_y(self, w):
        return jnp.concatenate([w] + [swap(w, "dp", b) for b in self.y_bits], axis=0)

    def gather(self, w):
        half = w.shape[1] // 2
        rows = self.gather_z(w)
        first, other = rows[:, :half], rows[:, half:]
        first = self.gather_y(first)
        firsts = [first] + [swap(first, "sp", b) for b in self.x_bits]
        other = jnp.concatenate([other] + [swap(other, "sp", b) for b in self.x_bits], axis=1)
        other = self.gather_y(other)
        parts = []
        for k in range(self.nx):
            parts += [firsts[k], other[:, k * half : (k + 1) * half]]
        return jnp.concatenate(parts, axis=1)

    def fold(self, parts, axis, bits):
        total = parts[0].astype(f32)
        for part, b in zip(parts[1:], bits, strict=True):
            total = total + swap(part.astype(bf16), axis, b).astype(f32)
        return total

    def scatter_y(self, g):
        rows = g.shape[0] // self.ny
        return self.fold([g[k * rows : (k + 1) * rows] for k in range(self.ny)], "dp", self.y_bits)

    def scatter_z(self, g):
        rows = g.shape[0] // self.nz
        return self.fold([g[k * rows : (k + 1) * rows] for k in range(self.nz)], "dp", self.z_bits)

    def scatter_x(self, g):
        cols = g.shape[1] // self.nx
        return self.fold([g[:, k * cols : (k + 1) * cols] for k in range(self.nx)], "sp", self.x_bits)

    def scatter(self, g):
        cols = g.shape[1] // self.nx
        half = cols // 2
        first = jnp.concatenate([g[:, k * cols : k * cols + half] for k in range(self.nx)], axis=1)
        other = jnp.concatenate([g[:, k * cols + half : (k + 1) * cols] for k in range(self.nx)], axis=1)
        first = self.scatter_y(self.scatter_x(first))
        other = self.scatter_x(self.scatter_y(other))
        return self.scatter_z(jnp.concatenate([first, other], axis=1))

    def all_sum(self, v):
        for axis in ("sp", "dp"):
            bit = 1
            while bit < lax.axis_size(axis):
                v = v + swap(v, axis, bit)
                bit *= 2
        return v


def norm_forward(halves, gains, shifts):
    width = sum(h.shape[1] for h in halves)
    mean = sum(jnp.sum(h, axis=1, keepdims=True) for h in halves) / width
    centred = [h - mean for h in halves]
    inv_std = lax.rsqrt(sum(jnp.sum(c * c, axis=1, keepdims=True) for c in centred) / width + EPSILON)
    normed = [c * inv_std for c in centred]
    return [n * a + b for n, a, b in zip(normed, gains, shifts)], normed, inv_std


def norm_backward(incoming, normed, inv_std, gains):
    width = sum(h.shape[1] for h in incoming)
    scaled = [e * a for e, a in zip(incoming, gains)]
    mean = sum(jnp.sum(s, axis=1, keepdims=True) for s in scaled) / width
    along = sum(jnp.sum(s * n, axis=1, keepdims=True) for s, n in zip(scaled, normed)) / width
    grads = [inv_std * (s - mean - n * along) for s, n in zip(scaled, normed)]
    gain_sums = [jnp.sum(e * n, axis=0) for e, n in zip(incoming, normed)]
    return grads, gain_sums, [jnp.sum(e, axis=0) for e in incoming]


def general_layer(
    tokens,
    seq_spans,
    valid_mask,
    cotangent,
    w_qkv,
    w_out,
    w_up,
    w_down,
    model_gains,
    model_shifts,
    mid_gain,
    hidden_shifts,
    head_scale,
):
    dp, sp = lax.axis_size("dp"), lax.axis_size("sp")
    grid = Grid(dp, sp)
    nx, ny, nz = grid.nx, grid.ny, grid.nz
    me_d, me_s = lax.axis_index("dp"), lax.axis_index("sp")
    rows, width = tokens.shape
    group = rows * sp
    heads = head_scale.shape[0]
    nh = heads // sp
    lw = nh * HEAD
    block = width // dp
    ff = mid_gain.shape[0]

    place = jnp.arange(dp, dtype=jnp.int32)
    to_rel = ((place % nz) * ny + place // nz) ^ me_d
    away = place ^ me_d
    to_abs = (away % ny) * nz + away // ny
    sp_place = jnp.arange(sp, dtype=jnp.int32)
    sp_rel = ((sp_place % nx) * 2 + sp_place // nx) ^ me_s
    sp_away = sp_place ^ me_s
    sp_abs = (sp_away % 2) * nx + sp_away // 2

    pad_rows = 16
    valid_rows = rows // lw
    blocks = w_qkv.reshape(block, 3, lw).transpose(1, 0, 2)
    blocks = jnp.concatenate([blocks, jnp.zeros((sp - 3, block, lw), bf16)], axis=0)
    turned = jnp.concatenate(
        [lax.dynamic_slice_in_dim(blocks, (t - 3 * me_s) % sp, 1, 0) for t in range(sp)], axis=0
    )
    flag_rows = jnp.concatenate(
        [valid_mask.astype(bf16).reshape(valid_rows, lw), jnp.zeros((pad_rows - valid_rows, lw), bf16)], axis=0
    )
    sent = jnp.concatenate([turned, jnp.broadcast_to(flag_rows[None], (sp, pad_rows, lw))], axis=1)
    got = lax.all_to_all(sent, "sp", 0, 0, tiled=True)
    keep = got[:, block : block + valid_rows].reshape(group) > 0.5
    wq_shard = jnp.concatenate(
        [lax.dynamic_slice_in_dim(got, (t * sp + me_s) // 3, 1, 0)[0, :block] for t in range(3)], axis=1
    )
    wq = grid.gather_y(grid.gather_z(wq_shard))

    gains = reorder(model_gains, to_rel, block)
    shifts = reorder(model_shifts, to_rel, block)
    stream = reorder(tokens, to_rel, block).astype(f32)
    upstream = reorder(cotangent, to_rel, block) * valid_mask.astype(bf16)[:, None]
    (first_out,), (first_normed,), first_std = norm_forward([stream], gains[0:1], shifts[3:4])
    first = first_out.astype(bf16)

    crossed = [first] + [swap(first, "sp", b) for b in grid.x_bits]
    firsts = []
    for piece in crossed:
        firsts += [piece, swap(piece, "sp", 1)]
    piece_bits = [b for k in [0] + grid.x_bits for b in (k, k + 1)]
    qkv_shift = jnp.concatenate(
        [
            lax.dynamic_slice_in_dim(model_shifts[0], me_s * lw, lw, 0),
            jnp.zeros((lw,), f32),
            lax.dynamic_slice_in_dim(model_shifts[1], me_s * lw, lw, 0),
        ]
    )
    firsts_cat = jnp.concatenate(firsts, axis=0)
    qkv_rel = (mm(firsts_cat, wq) + qkv_shift).astype(bf16)
    group_order = sp_place ^ me_s
    qkv = reorder_rows(qkv_rel, group_order, rows)

    low_down = jnp.concatenate([w_out, w_down], axis=1)
    od_own = grid.gather(low_down)
    up_own = grid.gather(w_up)
    oc, dc = w_out.shape[1], w_down.shape[1]
    out_own = jnp.concatenate([od_own[:, k * (oc + dc) : k * (oc + dc) + oc] for k in range(nx)], axis=1)
    down_own = jnp.concatenate([od_own[:, k * (oc + dc) + oc : (k + 1) * (oc + dc)] for k in range(nx)], axis=1)
    wos = jnp.concatenate([out_own, swap(out_own, "sp", 1)], axis=1)
    downs = [down_own, swap(down_own, "sp", 1)]
    ups = [up_own, swap(up_own, "sp", 1)]
    wo = reorder(reorder_rows(wos, to_abs, block), sp_abs, oc)

    tab = jnp.concatenate([sp_place, me_s[None].astype(jnp.int32)])
    hd = Heads(nh, nh, 0, (0, 1, 2), 0, sp, sp, rows)
    keep_col = jnp.broadcast_to(keep.astype(f32)[None, :], (8, group))
    scaled, o_t, lse = attend_forward(hd, tab, seq_spans[0], qkv, keep_col, head_scale)
    returned = lax.all_to_all(scaled.reshape(sp, rows, lw), "sp", 0, 0, tiled=True)
    merged = jnp.concatenate([returned[t] for t in range(sp)], axis=1)

    attn_pre = reorder(mm(merged, wo) + model_shifts[2], to_rel, block)
    (attn_out,), (attn_normed,), attn_std = norm_forward([attn_pre], gains[1:2], shifts[4:5])
    middle = stream + attn_out
    (second_out,), (second_normed,), second_std = norm_forward([middle], gains[2:3], shifts[5:6])
    second = second_out.astype(bf16)

    ff_half = ff // 2
    hidden_vectors = reorder(
        jnp.concatenate([mid_gain[None], hidden_shifts], axis=0), sp_rel, ff // sp
    )
    split = lambda v: [v[:, :ff_half], v[:, ff_half:]]
    hg, hb, hs = split(hidden_vectors[0:1]), split(hidden_vectors[1:2]), split(hidden_vectors[2:3])
    pre = [mm(second, w) + b for w, b in zip(ups, hb)]
    activated, pulls = zip(*[jax.vjp(jax.nn.gelu, p) for p in pre])
    hidden_out, hidden_normed, hidden_std = norm_forward(activated, hg, hs)
    hidden = [h.astype(bf16) for h in hidden_out]
    out_rel = middle + mm_cols(hidden[0], downs[0]) + mm_cols(hidden[1], downs[1]) + shifts[6:7]
    layer_out = reorder(out_rel.astype(bf16), to_abs, block)

    pair = lambda x: jnp.concatenate([x, swap(x, "sp", 1)], axis=0)
    across = lambda halves: jnp.concatenate([halves[0], swap(halves[1], "sp", 1)], axis=0)
    upstream_pair = pair(upstream)
    g_down = mm_rows(upstream_pair, across(hidden)).astype(bf16)
    grad_w_down = grid.scatter(g_down)

    hidden_grad = [mm(upstream, w) for w in downs]
    act_grad, grad_mid, grad_mid_shift = norm_backward(hidden_grad, hidden_normed, hidden_std, hg)
    pre_grad = [pull(a)[0].astype(bf16) for pull, a in zip(pulls, act_grad)]
    second_grad = mm_cols(pre_grad[0], ups[0]) + mm_cols(pre_grad[1], ups[1])
    (middle_part,), (gain_ffn,), (shift_ffn,) = norm_backward([second_grad], [second_normed], second_std, gains[2:3])
    middle_grad = upstream.astype(f32) + middle_part
    (attn_grad_full,), (gain_attn,), (shift_attn,) = norm_backward([middle_grad], [attn_normed], attn_std, gains[1:2])
    attn_grad_rel = attn_grad_full.astype(bf16)
    attn_grad = reorder(attn_grad_rel, to_abs, block)
    merged_grad = mm_cols(attn_grad, wo).astype(bf16)
    scattered = jnp.stack([merged_grad[:, t * lw : (t + 1) * lw] for t in range(sp)], axis=0)
    scaled_grad = lax.all_to_all(scattered, "sp", 0, 0, tiled=True).reshape(group, lw)

    g_up = mm_rows(pair(second), across(pre_grad)).astype(bf16)
    grad_w_up = grid.scatter(g_up)
    merged_rel = reorder(merged, to_rel, block)
    attn_grad_cols = reorder(attn_grad, sp_rel, oc)
    g_out = mm_rows(pair(merged_rel), across([attn_grad_cols[:, : width // 2], attn_grad_cols[:, width // 2 :]]))
    grad_w_out = grid.scatter_z(grid.scatter_y(grid.scatter_x(g_out)))

    qkv_grad, head_sums = attend_backward(
        hd, 0, tab, seq_spans[0], qkv, keep_col, head_scale, scaled_grad, o_t, lse
    )
    qkv_grad_rel = reorder_rows(qkv_grad, group_order, rows)
    first_part = mm_cols(qkv_grad_rel, wq)
    pieces = [first_part[t * rows : (t + 1) * rows] for t in range(sp)]
    folded = [
        pieces[t].astype(f32) + swap(pieces[t + 1].astype(bf16), "sp", 1).astype(f32) for t in range(0, sp, 2)
    ]
    first_grad = grid.fold(folded, "sp", grid.x_bits)
    (input_part,), (gain_in,), (shift_in,) = norm_backward([first_grad], [first_normed], first_std, gains[0:1])
    grad_tokens = reorder(middle_grad + input_part, to_abs, block)

    g_qkv = mm_rows(firsts_cat, qkv_grad_rel)
    g_mine = grid.scatter_z(grid.scatter_y(g_qkv)).astype(bf16)
    g_blocks = jnp.concatenate(
        [g_mine.reshape(block, 3, lw).transpose(1, 0, 2), jnp.zeros((1, block, lw), bf16)], axis=0
    )
    back = []
    for t in range(sp):
        which = jnp.int32(3)
        for u in range(3):
            which = jnp.where((u * sp + me_s) // 3 == t, u, which)
        back.append(lax.dynamic_slice_in_dim(g_blocks, which, 1, 0))
    home = lax.all_to_all(jnp.concatenate(back, axis=0), "sp", 0, 0, tiled=True)
    grad_w_qkv = jnp.concatenate(
        [lax.dynamic_slice_in_dim(home, (3 * me_s + u) % sp, 1, 0)[0] for u in range(3)], axis=1
    ).astype(f32)

    qkv_sums = jnp.sum(qkv_grad.astype(f32), axis=0)
    zeros = jnp.zeros((2, width), f32)
    bias_sums = lax.dynamic_update_slice(
        zeros, jnp.stack([qkv_sums[:lw], qkv_sums[2 * lw :]]), (0, me_s * lw)
    )
    sum_early = jnp.concatenate(
        [
            reorder(
                jnp.stack(
                    [
                        gain_attn,
                        gain_ffn,
                        jnp.sum(attn_grad_rel.astype(f32), axis=0),
                        shift_attn,
                        shift_ffn,
                        jnp.sum(upstream.astype(f32), axis=0),
                    ]
                ),
                to_abs,
                block,
            ),
            reorder(
                jnp.stack(
                    [
                        jnp.concatenate(grad_mid),
                        jnp.concatenate([jnp.sum(p.astype(f32), axis=0) for p in pre_grad]),
                        jnp.concatenate(grad_mid_shift),
                    ]
                ),
                sp_abs,
                ff // sp,
            ).reshape(3 * ff // width, width),
        ],
        axis=0,
    )
    early = grid.all_sum(sum_early)
    scale_row = lax.dynamic_update_slice(
        jnp.zeros((1, width), f32), head_sums[1:2, :nh], (0, me_s * nh)
    )
    late = grid.all_sum(
        jnp.concatenate(
            [reorder(jnp.stack([gain_in, shift_in]), to_abs, block), bias_sums, scale_row], axis=0
        )
    )
    grad_model_gains = jnp.stack([late[0], early[0], early[1]])
    grad_model_shifts = jnp.stack([late[2], late[3], early[2], late[1], early[3], early[4], early[5]])
    hidden_sums = early[6:].reshape(3, ff)
    return (
        layer_out,
        grad_tokens,
        grad_w_qkv,
        grad_w_out,
        grad_w_up,
        grad_w_down,
        grad_model_gains,
        grad_model_shifts,
        hidden_sums[0],
        hidden_sums[1:3],
        late[4, :heads],
    )


REL, HID, ORD, COLS, WHO, SEND, SLOT, ALONG = 0, 8, 16, 24, 32, 33, 36, 40
LANES = 128


def matchings(sp):
    left = {s: {3 * s + k: (3 * s + k) % sp for k in range(3)} for s in range(sp)}
    rounds = []
    for _ in range(3):
        taken = {}

        def seat(s, seen):
            for b, to in sorted(left[s].items(), key=lambda e: e[1] != s):
                if to not in seen:
                    seen.add(to)
                    if to not in taken or seat(taken[to][0], seen):
                        taken[to] = (s, b)
                        return True
            return False

        for s in range(sp):
            seat(s, set())
        one = [None] * sp
        for to, (s, b) in taken.items():
            one[s] = (b - 3 * s, b // sp, to)
            del left[s][b]
        rounds.append(one)
    return rounds


def tables(dp, sp, ny, nz, rounds):
    out = np.zeros((dp * sp, 128), np.int32)
    for d in range(dp):
        for s in range(sp):
            row = out[d * sp + s]
            where = {}
            for p in range(dp):
                row[REL + p] = ((p % nz) * ny + p // nz) ^ d
                where[row[REL + p]] = p
            for q in range(2 * sp):
                dc, half, dx = q // 4, q // 2 % 2, q % 2
                row[HID + q] = ((dx * 2 + dc) ^ s) * 2 + half
                row[COLS + q] = where[row[HID + q]]
            for t in range(sp):
                row[ORD + t] = s ^ t
            row[WHO] = s
            for k in range(nz):
                row[ALONG + k] = d // ny ^ k
            for m in range(3):
                row[SEND + m] = rounds[m][s][0]
                row[SLOT + m] = next(rounds[m][a][1] for a in range(sp) if rounds[m][a][2] == s)
    return out


def span(index, size):
    return pl.ds(pl.multiple_of(index * size, size), size)


def norm_of(x):
    mean = jnp.mean(x, axis=1, keepdims=True)
    centred = x - mean
    inv_std = lax.rsqrt(jnp.mean(centred * centred, axis=1, keepdims=True) + EPSILON)
    return centred * inv_std, inv_std


def norm_back(incoming, normed, inv_std, gain):
    scaled = incoming * gain
    mean = jnp.mean(scaled, axis=1, keepdims=True)
    along = jnp.mean(scaled * normed, axis=1, keepdims=True)
    return inv_std * (scaled - mean - normed * along)


def down_sum(x):
    return jnp.sum(x, axis=0, keepdims=True)


def whole(shape):
    return pl.BlockSpec(shape, lambda *_: (0,) * len(shape))


def by_rows(rows, cols):
    return pl.BlockSpec((rows, cols), lambda i, *_: (i, 0))


class Order:
    last = ()

    def after(self, deps):
        return tuple(deps) + self.last

    def passed(self, outs):
        self.last = (outs[-1],)
        return outs


ORDER = Order()


def with_rider(body, at, count):
    def both(*refs):
        first, second, total = refs[at], refs[at + 1], refs[at + 2 + count]

        @pl.when(pl.program_id(0) == 0)
        def _():
            total[...] = first[...] + second[...]

        body(*refs[:at], *refs[at + 2 : at + 2 + count], *refs[at + 3 + count :])

    return both


def call(name, body, tab, args, outs, steps=1, in_specs=None, out_specs=None, scratch=(), deps=(), vmem=20, us=0, rider=None):
    in_specs = [whole(a.shape) for a in args] if in_specs is None else in_specs
    out_specs = [whole(s) for s, _ in outs] if out_specs is None else out_specs
    if rider is not None:
        body = with_rider(body, 1 + len(args), len(outs))
        args, outs = list(args) + list(rider), list(outs) + [(rider[0].shape, rider[0].dtype)]
        in_specs = list(in_specs) + [whole(rider[0].shape)] * 2
        out_specs = list(out_specs) + [whole(rider[0].shape)]
    deps = ORDER.after(deps)
    made = pl.pallas_call(
        skipping(body, 1 + len(args), len(deps)),
        grid_spec=pltpu.PrefetchScalarGridSpec(
            num_scalar_prefetch=1,
            grid=(steps,),
            in_specs=list(in_specs) + unread(deps),
            out_specs=list(out_specs),
            scratch_shapes=list(scratch),
        ),
        out_shape=[jax.ShapeDtypeStruct(s, t) for s, t in outs],
        compiler_params=pltpu.CompilerParams(vmem_limit_bytes=vmem << 20),
        cost_estimate=pl.CostEstimate(flops=int(us * 1.1e9) + 1024, bytes_accessed=1024, transcendentals=0),
        name=name,
    )(tab, *args, *deps)
    return ORDER.passed(made)


def part_body(tab, w, *outs):
    width = outs[0].shape[1]
    for m, out in enumerate(outs):
        out[...] = w[:, span(tab[SEND + m], width)]


def join_body(tab, *refs):
    pieces, out = refs[:-1], refs[-1]
    for m, piece in enumerate(pieces):
        for k in range(out.shape[0]):
            out[k, :, span(tab[SLOT + m], piece.shape[1])] = piece[...]


def home_body(tab, p0, p1, p2, late, e0, e1, out, gains, shifts, mid, hid, scale):
    size, width = p0.shape[1], late.shape[1]
    early = e0[...] + e1[...]
    for m, piece in enumerate((p0, p1, p2)):
        out[:, span(tab[SEND + m], size)] = piece[...].astype(f32)
    for row, source in enumerate((late[0:1], early[0:1], early[1:2])):
        gains[row : row + 1, :] = source
    for row, source in enumerate((late[2:3], late[3:4], early[2:3], late[1:2], early[3:4], early[4:5], early[5:6])):
        shifts[row : row + 1, :] = source
    for k in range(mid.shape[1] // width):
        to = slice(k * width, (k + 1) * width)
        mid[:, to] = early[6 + k : 7 + k, :]
        hid[0:1, to] = early[10 + k : 11 + k, :]
        hid[1:2, to] = early[14 + k : 15 + k, :]
    scale[...] = late[4:5, : scale.shape[1]]


def prologue_body(tab, tok, cot, vcol, vrow, gains, shifts, mid, hsh, first_ref, both_ref, up_ref, tokr_ref, vec_ref, hid_ref):
    rows, width = tok.shape
    unit = mid.shape[1] // 8
    valid = vcol[...]
    vec_ref[...] = jnp.zeros_like(vec_ref)
    hid_ref[...] = jnp.zeros_like(hid_ref)
    for p in range(8):
        at, to = span(tab[REL + p], LANES), slice(p * LANES, (p + 1) * LANES)
        tokr_ref[:, to] = tok[:, at]
        vec_ref[0:3, to] = gains[:, at]
        vec_ref[3:10, to] = shifts[:, at]
        at, to = span(tab[HID + p], unit), slice(p * unit, (p + 1) * unit)
        hid_ref[0:1, to] = mid[:, at]
        hid_ref[1:3, to] = hsh[:, at]
    gain, shift = vec_ref[0:1, :], vec_ref[6:7, :]

    def chunk(i, carry):
        at = span(i, 64)
        normed, _ = norm_of(tokr_ref[at, :].astype(f32))
        first_ref[at, :] = (normed * gain + shift).astype(bf16)
        return carry

    lax.fori_loop(0, rows // 64, chunk, 0)
    first_ref[rows:, :] = jnp.broadcast_to(vrow[...], (16, width))
    both_ref[: rows + 16, :] = first_ref[...]
    for p in range(8):
        at, to = span(tab[REL + p], LANES), slice(p * LANES, (p + 1) * LANES)
        masked = cot[:, at].astype(f32) * valid
        up_ref[:, to] = masked.astype(bf16)
        vec_ref[10:11, to] = down_sum(masked)
    both_ref[rows + 16 :, :] = up_ref[...]


def project_body(count, tab, *refs):
    pieces, (w0, w1, shifts, out_ref, keep_ref) = refs[:count], refs[count:]
    rows, depth = out_ref.shape[0], w0.shape[0]
    at = span(tab[WHO], 2 * LANES)
    bias = jnp.concatenate([shifts[0:1, at], jnp.zeros((1, 2 * LANES), f32), shifts[1:2, at]], axis=1)
    for k in range(count):

        @pl.when(pl.program_id(0) == k)
        def _():
            x = pieces[k]
            out_ref[...] = (mm(x[:rows, :depth], w0[...]) + mm(x[:rows, depth:], w1[...]) + bias).astype(bf16)
            keep_ref[...] = x[rows : rows + 16, :rows].astype(f32)[:8]


def middle_body(begin, tab, ret, tok, vec, shards, pair_ref, mid_ref, norm_ref, std_ref, wo, sems):
    width = tok.shape[1]

    def copies(p):
        out = []
        for q in range(8):
            at = tab[HID + q]
            source = shards.at[tab[REL + p] * 4 + at // 2, :, pl.ds(pl.multiple_of(begin + lax.rem(at, 2) * LANES, LANES), LANES)]
            out.append(pltpu.make_async_copy(source, wo.at[pl.ds(p * LANES, LANES), span(tab[COLS + q], LANES)], sems.at[p, q]))
        return out

    @pl.when(pl.program_id(0) == 0)
    def _():
        for p in range(8):
            for copy in copies(p):
                copy.start()

    for p in range(8):
        a = tab[REL + p]
        pair_ref[:, width + p * LANES : width + (p + 1) * LANES] = ret[a // 2, :, span(lax.rem(a, 2), LANES)]

    @pl.when(pl.program_id(0) == 0)
    def _():
        for p in range(8):
            for copy in copies(p):
                copy.wait()

    normed, inv_std = norm_of(mm(pair_ref[:, width:], wo[...]) + vec[5:6, :])
    middle = tok[...].astype(f32) + (normed * vec[1:2, :] + vec[7:8, :])
    norm_ref[...] = normed
    std_ref[...] = inv_std
    mid_ref[...] = middle
    again, _ = norm_of(middle)
    pair_ref[:, :width] = (again * vec[2:3, :] + vec[8:9, :]).astype(bf16)


GELU = 0.7978845608028654
CUBE = 0.044715


def ffn_body(unit, tab, second, upstream, mid, hid, vec, *refs):
    shards, (hown, hsib, pown, psib, sg_ref, lo_ref, sums_ref, upv, dnv, act, slope, back, sems) = refs[0], refs[1:]
    i = pl.program_id(0)
    ff = upv.shape[1]

    def copies(q, which):
        held = (upv, dnv)[which]
        at = tab[HID + q]
        from_cols = pl.ds(pl.multiple_of(which * 2 * unit + lax.rem(at, 2) * unit, unit), unit)
        out = []
        for p in range(8):
            source = shards.at[tab[REL + p] * 4 + at // 2, :, from_cols]
            out.append(pltpu.make_async_copy(source, held.at[pl.ds(p * LANES, LANES), pl.ds(q * unit, unit)], sems.at[which, q, p]))
        return out

    @pl.when(i == 0)
    def _():
        sums_ref[...] = jnp.zeros_like(sums_ref)
        for q in range(8):
            for copy in copies(q, 0):
                copy.start()
        for q in range(8):
            for copy in copies(q, 1):
                copy.start()

    x = second[...]
    total = jnp.zeros((x.shape[0], 1), f32)
    for q in range(8):
        at = slice(q * unit, (q + 1) * unit)

        @pl.when(i == 0)
        def _():
            for copy in copies(q, 0):
                copy.wait()

        pre = mm(x, upv[:, at]) + hid[1:2, at]
        squared = pre * pre
        t = jnp.tanh(pre * (GELU + (GELU * CUBE) * squared))
        one = 0.5 + 0.5 * t
        value = pre * one
        act[:, at] = value
        slope[:, at] = one + 0.5 * pre * (1.0 - t * t) * (GELU + (3 * GELU * CUBE) * squared)
        total = total + jnp.sum(value, axis=1, keepdims=True)
    mean = total / ff
    total = jnp.zeros_like(mean)
    for q in range(8):
        at = slice(q * unit, (q + 1) * unit)
        centred = act[:, at] - mean
        total = total + jnp.sum(centred * centred, axis=1, keepdims=True)
    inv_std = lax.rsqrt(total / ff + EPSILON)
    u = upstream[...]
    m1, m2 = jnp.zeros_like(mean), jnp.zeros_like(mean)
    low = jnp.zeros(mid.shape, f32)
    for q in range(8):
        at = slice(q * unit, (q + 1) * unit)

        @pl.when(i == 0)
        def _():
            for copy in copies(q, 1):
                copy.wait()

        incoming = mm(u, dnv[:, at])
        normed = (act[:, at] - mean) * inv_std
        act[:, at] = normed
        gain = hid[0:1, at]
        held, to = ((hown, at) if q < 4 else (hsib, slice((q - 4) * unit, (q - 3) * unit)))
        hidden = (normed * gain + hid[2:3, at]).astype(bf16)
        held[:, to] = hidden
        low = low + mm_cols(hidden, dnv[:, at])
        along = incoming * normed
        sums_ref[0:1, at] += down_sum(along)
        sums_ref[2:3, at] += down_sum(incoming)
        m1 = m1 + jnp.sum(incoming * gain, axis=1, keepdims=True)
        m2 = m2 + jnp.sum(along * gain, axis=1, keepdims=True)
        back[:, at] = incoming
    m1, m2 = m1 / ff, m2 / ff
    second_grad = jnp.zeros(mid.shape, f32)
    for q in range(8):
        at = slice(q * unit, (q + 1) * unit)
        grad = inv_std * (back[:, at] * hid[0:1, at] - m1 - act[:, at] * m2)
        pre_grad = (grad * slope[:, at]).astype(bf16)
        held, to = ((pown, at) if q < 4 else (psib, slice((q - 4) * unit, (q - 3) * unit)))
        held[:, to] = pre_grad
        sums_ref[1:2, at] += down_sum(pre_grad.astype(f32))
        second_grad = second_grad + mm_cols(pre_grad, upv[:, at])
    sg_ref[...] = second_grad
    out = (mid[...] + low + vec[9:10, :]).astype(bf16)
    for p in range(8):
        lo_ref[:, span(tab[REL + p], LANES)] = out[:, p * LANES : (p + 1) * LANES]


def heads_body(tab, grad, mid, norm, std, up, vec, wo, mg_ref, own_ref, sib_ref, out_ref, sums_ref, scr):
    @pl.when(pl.program_id(0) == 0)
    def _():
        sums_ref[...] = jnp.zeros_like(sums_ref)

    incoming = grad[...]
    again, inv_std = norm_of(mid[...])
    sums_ref[1:2, :] += down_sum(incoming * again)
    sums_ref[4:5, :] += down_sum(incoming)
    middle_grad = up[...].astype(f32) + norm_back(incoming, again, inv_std, vec[2:3, :])
    mg_ref[...] = middle_grad
    normed = norm[...]
    sums_ref[0:1, :] += down_sum(middle_grad * normed)
    sums_ref[3:4, :] += down_sum(middle_grad)
    low = norm_back(middle_grad, normed, std[...], vec[1:2, :]).astype(bf16)
    sums_ref[2:3, :] += down_sum(low.astype(f32))
    scr[...] = low
    for q in range(8):
        held = own_ref if q < 4 else sib_ref
        held[:, (q % 4) * LANES : (q % 4 + 1) * LANES] = scr[:, span(tab[COLS + q], LANES)]
    got = mm_cols(low, wo[...]).astype(bf16)
    for p in range(8):
        a = tab[REL + p]
        out_ref[a // 2, :, span(lax.rem(a, 2), LANES)] = got[:, p * LANES : (p + 1) * LANES]


def turn_body(tab, x0, x1, out):
    tokens = x0.shape[0]
    out[:, :tokens] = x0[...].T
    out[:, tokens:] = x1[...].T


def turn_late_body(tab, x0, both, out):
    tokens = x0.shape[0]
    out[:, :tokens] = x0[...].T
    out[:, tokens:] = both[tokens + 16 :, :].T


def grads_body(counts, widths, tab, *refs):
    ins, (ak, asend, bk, bsend, xt) = refs[:-5], refs[-5:]
    half = bk.shape[0]
    total = sum(widths)
    i = pl.program_id(0)
    at = begin = 0
    for n, (count, wide) in enumerate(zip(counts, widths)):
        xs, (y0, y1) = ins[begin : begin + count], ins[begin + count : begin + count + 2]
        begin += count + 2
        if count == 2:

            @pl.when(i == 4 * n)
            def _():
                turn_body(tab, *xs, xt)

        left = xt if count == 2 else xs[0]
        for q in range(4):

            @pl.when(i == 4 * n + q)
            def _():
                g = mm(left[...], jnp.concatenate([y0[...], y1[...]], axis=0)).astype(bf16)
                if q < 2:
                    (ak, asend)[q][:, at : at + wide] = g
                else:
                    to = slice((q - 2) * total + at, (q - 2) * total + at + wide)
                    bk[:, to] = g[:half]
                    bsend[:, to] = g[half:]

        at += wide


def groups_body(count, tab, *refs):
    pieces, (grad, keep, send, acc) = refs[:count], refs[count:]
    i = pl.program_id(0)
    half = keep.shape[0]
    rows = grad.shape[0]
    for k in range(count):

        @pl.when(i == k)
        def _():
            got = mm(pieces[k][:rows, :].T, grad[...])
            acc[...] = got if k == 0 else acc[...] + got

    @pl.when(i == count - 1)
    def _():
        keep[...] = acc[:half]
        send[...] = acc[half:].astype(bf16)


def fold_body(tab, ak, ra, bk, rb, x0, a2k, a2s, b2k, b2s, y0):
    y0[...] = x0[...]
    rows, cols = b2k.shape
    a = ak[...].astype(f32) + ra[...].astype(f32)
    a2k[...] = a[:rows].astype(bf16)
    a2s[...] = a[rows:].astype(bf16)
    b = bk[...].astype(f32) + rb[...].astype(f32)
    b2k[...] = b[:, :cols].astype(bf16)
    b2s[...] = b[:, cols:].astype(bf16)


def spread_body(tab, ak, ra, bk, rb, g, r, keep, *sends):
    rows, cols = keep.shape[0], ak.shape[1]
    at = 0
    for mine, theirs in ((ak, ra), (bk, rb), (g, r)):
        total = mine[...].astype(f32) + theirs[...].astype(f32)
        to = slice(at, at + total.shape[1])
        at += total.shape[1]
        keep[:, to] = total[:rows]
        for n, send in enumerate(sends, 1):
            send[:, to] = total[n * rows : (n + 1) * rows].astype(bf16)


def gathered_body(widths, tab, keep, r1, r2, r3, low, *refs):
    outs, pieces, (wide_low, total) = refs[: len(widths)], refs[len(widths) : -2], refs[-2:]
    wide_low[...] = low[...].astype(f32)
    total[...] = keep[...] + r1[...].astype(f32) + r2[...].astype(f32) + r3[...].astype(f32)
    half = sum(widths)
    at = 0
    for out, wide in zip(outs, widths):
        out[:, :wide] = total[:, at : at + wide]
        out[:, wide:] = total[:, half + at : half + at + wide]
        at += wide
    for m, piece in enumerate(pieces):
        size = piece.shape[1]
        piece[...] = total[:, pl.ds(pl.multiple_of(2 * half + tab[SLOT + m] * size, size), size)].astype(bf16)


def spill_body(unit, tab, xt, own, sib, out):
    tokens, width = own.shape[0], xt.shape[0]
    for half, y in enumerate((own, sib)):

        @pl.when(pl.program_id(0) // 4 == half)
        def _():
            g = mm(xt[:, :tokens], y[...]).astype(bf16)
            at = tab[HID + pl.program_id(0)]
            for p in range(8):
                out[tab[REL + p] * 4 + at // 2, :, span(lax.rem(at, 2), unit)] = g[p * LANES : (p + 1) * LANES]


def scatter_weights(grid, tab, rows, sets, widths, tag, rider=None):
    total = sum(widths)
    args, specs = [], []
    for n, (xs, y0, y1) in enumerate(sets):
        wide = widths[n]
        tokens = y0[0].shape[0]
        for x, part in xs:
            args.append(x)
            specs.append(whole(x.shape) if part is None else pl.BlockSpec((tokens, rows), lambda *_, part=part: (0, part)))
        for y, begin in (y0, y1):
            args.append(y)
            specs.append(pl.BlockSpec((tokens, wide), lambda i, *_, n=n, begin=begin: (0, begin + jnp.clip(i - 4 * n, 0, 3))))
    outs = [((rows, total), bf16)] * 2 + [((rows // 2, 2 * total), bf16)] * 2
    ak, asend, bk, bsend, *carried = call(
        "grads_" + tag, functools.partial(grads_body, [len(xs) for xs, _, _ in sets], widths), tab, args, outs,
        steps=4 * len(sets), in_specs=specs, scratch=[pltpu.VMEM((rows, 2 * tokens), bf16)], vmem=28, us=6 * len(sets), rider=rider,
    )
    ra, rb = swap(asend, "sp", 2), swap(bsend, "dp", 1)
    rider, ships = yield carried
    quarter = [((rows // 2, total), bf16)] * 4 + [(x.shape, x.dtype) for x in ships]
    a2k, a2s, b2k, b2s, *carried = call("fold_" + tag, fold_body, tab, [ak, ra, bk, rb] + ships, quarter, vmem=34, rider=rider)
    ra, rb = swap(a2s, "dp", 1), swap(b2s, "sp", 2)
    deps = yield carried + [ra, rb]
    (g, r), size = deps
    shard = (rows // 8, 2 * total + g.shape[1])
    keep, *sends = call("spread_" + tag, spread_body, tab, [a2k, ra, b2k, rb, g, r], [(shard, f32)] + [(shard, bf16)] * 3)
    received = [swap(x, "dp", b) for x, b in zip(sends, grid.z_bits)]
    rider, low = yield
    yield call(
        "sum_" + tag, functools.partial(gathered_body, widths), tab, [keep] + received + [low],
        [((rows // 8, 2 * w), f32) for w in widths] + [((rows // 8, size), bf16)] * 3 + [(low.shape, f32)],
        scratch=[pltpu.VMEM(shard, f32)], rider=rider,
    )


def along_z(grid, x):
    lines = [[y + grid.ny * k for k in range(grid.nz)] for y in range(grid.ny)]
    return lax.all_to_all(x, "dp", 0, 0, tiled=True, axis_index_groups=lines)


def rows_body(tab, got, out):
    rows = got.shape[1]
    for k in range(got.shape[0]):
        out[k * rows : (k + 1) * rows, :] = got[tab[ALONG + k]]


def first_grad_body(tab, g, wy0, wy1, mine, cross, far):
    i = pl.program_id(0)
    got = jnp.concatenate([mm_cols(g[...], wy0[...]), mm_cols(g[...], wy1[...])], axis=1)
    rows = g.shape[0]

    @pl.when(i == 0)
    def _():
        mine[...] = got

    @pl.when(i == 1)
    def _():
        cross[:rows] = got.astype(bf16)

    @pl.when(i == 2)
    def _():
        far[...] = got

    @pl.when(i == 3)
    def _():
        cross[rows:] = got.astype(bf16)


def relay_body(tab, far, theirs, send, out, sent):
    sent[...] = send[...]
    out[...] = (far[...] + theirs[...].astype(f32)).astype(bf16)


def final_body(tab, mine, theirs, crossed, tok, mg, vec, s0, out_ref, late_ref, acc, note):
    i = pl.program_id(0)
    width = tok.shape[1]

    @pl.when(i == 0)
    def _():
        acc[...] = jnp.zeros_like(acc)

    incoming = mine[...] + theirs[...].astype(f32) + crossed[...].astype(f32)
    normed, inv_std = norm_of(tok[...].astype(f32))
    acc[0:1, :] += down_sum(incoming * normed)
    acc[1:2, :] += down_sum(incoming)
    total = mg[...] + norm_back(incoming, normed, inv_std, vec[0:1, :])
    for p in range(8):
        out_ref[:, span(tab[REL + p], LANES)] = total[:, p * LANES : (p + 1) * LANES]

    @pl.when(i == pl.num_programs(0) - 1)
    def _():
        note[...] = jnp.zeros_like(note)
        for p in range(8):
            cols = slice(p * LANES, (p + 1) * LANES)
            note[pl.ds(tab[REL + p], 1), :] = acc[0:1, cols]
            note[pl.ds(8 + tab[REL + p], 1), :] = acc[1:2, cols]
        for e in range(2):
            note[16 + e : 17 + e, :] = s0[0:1, e * LANES : (e + 1) * LANES]
            note[18 + e : 19 + e, :] = s0[0:1, (4 + e) * LANES : (5 + e) * LANES]
        note[20:21, :] = s0[1:2, :LANES]
        for n in range(late_ref.shape[0]):
            late_ref[n] = note[...]


def totals_body(sp, tab, got, out):
    out[...] = jnp.zeros_like(out)
    count = got.shape[0]
    total = got[0, :16]
    for n in range(1, count):
        total = total + got[n, :16]
    for p in range(8):
        cols = slice(p * LANES, (p + 1) * LANES)
        out[0:1, cols] = total[p : p + 1]
        out[1:2, cols] = total[8 + p : 9 + p]
    heads = jnp.zeros((1, LANES), f32)
    lane = lax.broadcasted_iota(jnp.int32, (1, LANES), 1)
    for s in range(sp):
        mine = got[s, 16:24]
        for n in range(s + sp, count, sp):
            mine = mine + got[n, 16:24]
        for e in range(2):
            cols = slice((2 * s + e) * LANES, (2 * s + e + 1) * LANES)
            out[2:3, cols] = mine[e : e + 1]
            out[3:4, cols] = mine[2 + e : 3 + e]
        for h in range(4):
            value = jnp.sum(jnp.where(lane == h, mine[4:5], 0.0))
            heads = jnp.where(lane == 4 * s + h, value, heads)
    out[4:5, :LANES] = heads


def pack_body(tab, sums, vec, hid, out_ref):
    width, unit = sums.shape[1], hid.shape[1] // 8
    out_ref[...] = jnp.zeros_like(out_ref)
    for p in range(8):
        to, at = span(tab[REL + p], LANES), slice(p * LANES, (p + 1) * LANES)
        out_ref[0:5, to] = sums[0:5, at]
        out_ref[5:6, to] = vec[10:11, at]
    for v in range(3):
        for q in range(8):
            unit_at = tab[HID + q]
            row, col = 6 + 4 * v + unit_at // 2, lax.rem(unit_at, 2)
            out_ref[pl.ds(row, 1), span(col, unit)] = hid[v : v + 1, q * unit : (q + 1) * unit]


def fast_layer(
    tokens,
    seq_spans,
    valid_mask,
    cotangent,
    w_qkv,
    w_out,
    w_up,
    w_down,
    model_gains,
    model_shifts,
    mid_gain,
    hidden_shifts,
    head_scale,
):
    dp, sp = lax.axis_size("dp"), lax.axis_size("sp")
    grid = Grid(dp, sp)
    rows, width = tokens.shape
    group = rows * sp
    heads = head_scale.shape[0]
    block = width // dp
    ff = mid_gain.shape[0]
    unit = ff // 8
    shard_lanes = 2 * LANES
    step = rows // 2

    rounds = matchings(sp)
    device = lax.axis_index("dp") * sp + lax.axis_index("sp")
    tab = lax.dynamic_slice_in_dim(jnp.asarray(tables(dp, sp, grid.ny, grid.nz, rounds)), device, 1, 0)[0]
    spans = seq_spans[0]
    forth = [[(s, rounds[m][s][2]) for s in range(sp)] for m in range(3)]
    back_to = [[(t, s) for s, t in pairs] for pairs in forth]
    carry = lambda x, pairs: x if all(a == b for a, b in pairs) else lax.ppermute(x, "sp", pairs)

    ORDER.last = ()
    shards = lax.all_gather(jnp.concatenate([w_up, w_down, w_out], axis=1), ("dp", "sp"), axis=0)
    sent = call("part", part_body, tab, [w_qkv], [((block, shard_lanes), bf16)] * 3)
    moved = [carry(x, pairs) for x, pairs in zip(sent, forth)]
    wq_lines = along_z(grid, call("join", join_body, tab, moved, [((grid.nz, block, 3 * shard_lanes), bf16)])[0])
    vcol = valid_mask.astype(f32)[:, None]
    vrow = jnp.pad(valid_mask.astype(bf16), (0, width - rows))[None]
    first, both, upstream, tokr, vec, hid = call(
        "prologue", prologue_body, tab,
        [tokens, cotangent, vcol, vrow, model_gains, model_shifts, mid_gain[None], hidden_shifts],
        [((rows + 16, width), bf16), ((2 * rows + 16, width), bf16), ((rows, width), bf16), ((rows, width), bf16), ((16, width), f32), ((8, ff), f32)],
    )
    beyond = swap(first, "sp", 2)
    theirs = swap(both, "sp", 1)
    upstream_t = call("turn", turn_late_body, tab, [upstream, theirs], [((width, 2 * rows), bf16)], deps=(beyond,))[0]
    wq0 = call("rows_qkv", rows_body, tab, [wq_lines], [((grid.nz * block, 3 * shard_lanes), bf16)])[0]
    wq1 = swap(wq0, "dp", 1)
    firsts = [first, theirs, beyond, swap(beyond, "sp", 1)]
    qkv, keep = call(
        "project", functools.partial(project_body, sp), tab, firsts + [wq0, wq1, model_shifts],
        [((group, 3 * shard_lanes), bf16), ((8, group), f32)], steps=sp,
        out_specs=[by_rows(rows, 3 * shard_lanes), pl.BlockSpec((8, rows), lambda i, *_: (0, i))],
    )
    hd = Heads(4, heads // sp, 0, (0, 1, 2), ORD, WHO, sp, rows)
    scaled, o_t, lse = ORDER.passed(attend_forward(hd, tab, spans, qkv, keep, head_scale, deps=ORDER.last))
    returned = lax.all_to_all(scaled.reshape(sp, rows, shard_lanes), "sp", 0, 0, tiled=True)

    ret_spec = pl.BlockSpec((sp, step, shard_lanes), lambda i, *_: (0, i, 0))
    anywhere = pl.BlockSpec(memory_space=pl.ANY)
    pair, middle, attn_normed, attn_std, wo = call(
        "to_middle", functools.partial(middle_body, 2 * w_up.shape[1]), tab, [returned, tokr, vec, shards],
        [((rows, 2 * width), bf16), ((rows, width), f32), ((rows, width), f32), ((rows, 1), f32), ((width, width), bf16)],
        steps=2,
        in_specs=[ret_spec, by_rows(step, width), whole(vec.shape), anywhere],
        out_specs=[by_rows(step, 2 * width)] + [by_rows(step, width)] * 2 + [by_rows(step, 1), whole((width, width))],
        scratch=[pltpu.SemaphoreType.DMA((8, 8))], vmem=62,
    )
    pair_sib = swap(pair, "sp", 1)
    hid_own, hid_sib, pre_own, pre_sib, second_grad, layer_out, hidden_sums = call(
        "ffn", functools.partial(ffn_body, unit), tab, [pair, upstream, middle, hid, vec, shards],
        [((rows, ff // 2), bf16)] * 4 + [((rows, width), f32), ((rows, width), bf16), ((8, ff), f32)],
        steps=2,
        in_specs=[by_rows(step, width)] * 3 + [whole(hid.shape), whole(vec.shape)] + [anywhere],
        out_specs=[by_rows(step, ff // 2)] * 4 + [by_rows(step, width)] * 2 + [whole((8, ff))],
        scratch=[pltpu.VMEM((width, ff), bf16)] * 2 + [pltpu.VMEM((step, ff), f32)] * 3 + [pltpu.SemaphoreType.DMA((2, 8, 8))],
        vmem=63, us=37,
    )

    pre_across = swap(pre_sib, "sp", 1)
    spilled = call(
        "spill", functools.partial(spill_body, unit), tab, [upstream_t, hid_own, hid_sib], [((dp * sp, block, 2 * unit), bf16)], steps=8,
        in_specs=[pl.BlockSpec((width, rows), lambda *_: (0, 0)),
                  pl.BlockSpec((rows, unit), lambda i, *_: (0, jnp.clip(i, 0, 3))),
                  pl.BlockSpec((rows, unit), lambda i, *_: (0, jnp.clip(i - 4, 0, 3)))],
        vmem=62,
    )[0]
    down_part = lax.psum_scatter(spilled, ("dp", "sp"), scatter_dimension=0, tiled=True)[0]
    middle_grad, attn_own, attn_sib, back, sums = call(
        "to_heads", heads_body, tab, [second_grad, middle, attn_normed, attn_std, upstream, vec, wo],
        [((rows, width), f32)] + [((rows, width // 2), bf16)] * 2 + [((sp, rows, shard_lanes), bf16), ((8, width), f32)],
        steps=2,
        in_specs=[by_rows(step, width)] * 3 + [by_rows(step, 1), by_rows(step, width), whole(vec.shape), whole(wo.shape)],
        out_specs=[by_rows(step, width)] + [by_rows(step, width // 2)] * 2 + [ret_spec, whole((8, width))],
        scratch=[pltpu.VMEM((step, width), bf16)],
        vmem=62,
    )
    attn_across = swap(attn_sib, "sp", 1)
    early = call("pack", pack_body, tab, [sums, vec, hidden_sums], [((24, width), f32)])[0]
    early = (early, swap(early, "sp", 1))

    grads_in = lax.all_to_all(back, "sp", 0, 0, tiled=True).reshape(group, shard_lanes)
    up_sums = scatter_weights(
        grid, tab, width,
        [([(pair, 0), (pair_sib, 0)], (pre_own, 0), (pre_across, 0)), ([(pair, 1), (pair_sib, 1)], (attn_own, 0), (attn_across, 0))],
        (unit, LANES), "up", rider=early,
    )
    (early,) = next(up_sums)
    early = (early, swap(early, "sp", 2))
    wide = 3 * shard_lanes
    qkv_grad, head_sums = ORDER.passed(
        attend_backward(hd, 0, tab, spans, qkv, keep, head_scale, grads_in, o_t, lse, deps=ORDER.last)
    )
    mine, cross, far = call(
        "first_grad", first_grad_body, tab, [qkv_grad, wq0, wq1],
        [((rows, width), f32), ((2 * rows, width), bf16), ((rows, width), f32)], steps=sp,
        in_specs=[by_rows(rows, wide), whole(wq0.shape), whole(wq1.shape)],
        out_specs=[whole((rows, width)), whole((2 * rows, width)), whole((rows, width))],
    )
    keep_rows, send = call(
        "group_grads", functools.partial(groups_body, sp), tab, firsts + [qkv_grad],
        [((width // 2, wide), f32), ((width // 2, wide), bf16)], steps=sp,
        in_specs=[whole(f.shape) for f in firsts] + [by_rows(rows, wide)],
        scratch=[pltpu.VMEM((width, wide), f32)], vmem=30,
    )
    cross, early, *second_up = up_sums.send((early, [cross]))
    theirs = swap(cross, "sp", 1)
    relayed, send = call(
        "relay", relay_body, tab, [far, theirs, send], [((rows, width), bf16), (send.shape, bf16)],
        in_specs=[whole(far.shape), pl.BlockSpec((rows, width), lambda *_: (1, 0)), whole(send.shape)],
    )
    crossed, other_rows = swap(relayed, "sp", 2), swap(send, "dp", 1)
    early = (early, swap(early, "dp", 1))
    grad_tokens, late, early = call(
        "to_tokens", final_body, tab, [mine, theirs, crossed, tokr, middle_grad, vec, head_sums],
        [((rows, width), f32), ((dp * sp, 24, LANES), f32)], steps=2,
        in_specs=[by_rows(step, width)] * 5 + [whole(vec.shape), whole((8, wide))],
        out_specs=[by_rows(step, width), whole((dp * sp, 24, LANES))],
        scratch=[pltpu.VMEM((8, width), f32), pltpu.VMEM((24, LANES), f32)], rider=early, deps=(other_rows, *second_up),
    )
    early = (early, swap(early, "dp", 2))
    late = lax.all_to_all(late, ("dp", "sp"), 0, 0, tiled=True)
    up_sums.send(((keep_rows, other_rows), shard_lanes))
    late = call("totals", functools.partial(totals_body, sp), tab, [late], [((8, width), f32)])[0]
    grad_w_up, grad_w_out, *sent, grad_w_down, early = up_sums.send((early, down_part))
    along = swap(early, "dp", 4)
    got = [carry(x, pairs) for x, pairs in zip(sent, back_to)]
    grad_w_qkv, gain_sums, shift_sums, mid_sums, hid_sums, scale_sums = call(
        "home", home_body, tab, got + [late, early, along],
        [((block, 3 * shard_lanes), f32), ((3, width), f32), ((7, width), f32), ((1, ff), f32), ((2, ff), f32), ((1, heads), f32)],
    )
    return (
        layer_out,
        grad_tokens,
        grad_w_qkv,
        grad_w_out,
        grad_w_up,
        grad_w_down,
        gain_sums,
        shift_sums,
        mid_sums[0],
        hid_sums,
        scale_sums[0],
    )


def per_device(*arrays):
    dp, sp = lax.axis_size("dp"), lax.axis_size("sp")
    (rows, width), heads, ff = arrays[0].shape, arrays[12].shape[0], arrays[10].shape[0]
    if (dp, sp) == (8, 4) and width == 8 * LANES and heads * HEAD == width and ff == 4 * width and rows == 512:
        return fast_layer(*arrays)
    return general_layer(*arrays)


def solution(mesh):
    rows = P(("dp", "sp"), None)
    placed = (rows, P("dp", None), P(("dp", "sp")), rows) + (P("dp", "sp"),) * 4 + (P(),) * 5
    return jax.shard_map(
        per_device,
        mesh=mesh,
        in_specs=placed,
        out_specs=(rows, rows) + (P("dp", "sp"),) * 4 + (P(),) * 5,
        check_vma=False,
    )
```
